32 devices in a mesh: dp: 8 (over z, y), tensor: 4 (over x, core).
Axes of the slice: x: 2, y: 2, z: 4, core: 2. Of those that a mesh axis runs over, the one named last changes fastest.
Arguments:
- block_input: bfloat16 [32, 512, 1024], P('dp'), may hold values from -6 to 6
- segment_ids: int32 [32, 512], P('dp'), may hold values from 0 to 3, never falling along the last dimension, each value on 1 to 256 neighbouring positions
- query_weight: bfloat16 [1024, 1024], P(None, 'tensor')
- key_weight: bfloat16 [1024, 1024], P(None, 'tensor'), may hold values from -0.1875 to 0.1875
- value_weight: bfloat16 [1024, 1024], P(None, 'tensor'), may hold values from -0.1875 to 0.1875
- output_weight: bfloat16 [1024, 1024], P('tensor'), may hold values from -0.375 to 0.375
- first_gain: float32 [1024], replicated, may hold values from 0.1 to 1.9
- first_shift: float32 [1024], replicated, may hold values from -3 to 3
- up_weight: bfloat16 [1024, 4096], P(None, 'tensor'), may hold values from -0.1875 to 0.1875
- down_weight: bfloat16 [4096, 1024], P('tensor'), may hold values from -0.125 to 0.125
- second_gain: float32 [1024], replicated, may hold values from 0.1 to 1.9
- second_shift: float32 [1024], replicated, may hold values from -3 to 3
- out_grad: bfloat16 [32, 512, 1024], P('dp'), may hold values from -6 to 6
Outputs:
- layer_out: bfloat16 [32, 512, 1024], P('dp')
- input_grad: bfloat16 [32, 512, 1024], P('dp')
- query_grad: float32 [1024, 1024], P('dp', 'tensor')
- key_grad: float32 [1024, 1024], P('dp', 'tensor')
- value_grad: float32 [1024, 1024], P('dp', 'tensor')
- output_grad: float32 [1024, 1024], P('tensor', 'dp')
- first_gain_grad: float32 [1024], P('dp')
- first_shift_grad: float32 [1024], P('dp')
- up_grad: float32 [1024, 4096], P('dp', 'tensor')
- down_grad: float32 [4096, 1024], P('tensor', 'dp')
- second_gain_grad: float32 [1024], P('dp')
- second_shift_grad: float32 [1024], P('dp')
- query_clipped: float32 [1024, 1024], P(None, 'tensor')
- key_clipped: float32 [1024, 1024], P(None, 'tensor')
The draws below stay inside these ranges and needn't reach their ends.
Inputs may be any that keep to these rules, and one draw needn't show every extreme that they name: `segment_ids`: ids within a sequence never fall; each document has 1 to 256 tokens.
All inputs are finite; a program needn't handle non-finite values.
Results may differ from the reference program's by a relative error of at most 0.014.
The reference program's roundings to bfloat16 on the way count: a program that leaves them out, or rounds other values in their place, can miss the bound.
Values sent between devices are 32-bit elements; how exact they have to be, the bound alone decides.
No kernel may reach another device: no remote copies, remote signals or barrier semaphores. Data moves between devices by JAX's collectives and lax.ppermute only.
A program may use at most 192 MiB of HBM per device.

```python
import math
import jax
import jax.numpy as jnp
import numpy as np
from jax import lax

D = 1024
HEADS = 16
HEAD_DIM = 64
FF = 4096
SEQ_LEN = 512
WINDOW = 256
DOCS = 4
DOC_MOST = 256
SEQS = 32


def draw_query_weight(key, part):
    key = jax.random.fold_in(key, 7)
    head_key, entry_key = jax.random.split(key)
    head_scale = jnp.exp(jax.random.uniform(head_key, (HEADS,), jnp.float32, 0.0, math.log(3.0)))
    entries = jnp.clip(jax.random.normal(entry_key, (D, D), jnp.float32), -6.0, 6.0)
    column_scale = jnp.repeat(head_scale, HEAD_DIM)
    return (entries * column_scale[None, :] * D ** (-0.5)).astype(jnp.bfloat16)


def with_spikes(values, rng, source, target, shards_of, factor):
    owner, partner = [(jnp.arange(values.shape[position]) // (values.shape[position] // shards_of)).reshape([-1 if axis == position else 1 for axis in range(values.ndim)]) for position in (source, target)]
    chosen = jax.random.permutation(rng, shards_of)[partner]
    strong = (owner == chosen) | (owner == (partner + shards_of // 2) % shards_of)
    return jnp.where(strong, factor * values, values)


def level_of(key, extent, cuts, smallest, top_value):
    factor_of = 1.0
    for axis_at, parts in cuts:
        heights = jax.random.uniform(jax.random.fold_in(jax.random.fold_in(key, 6), axis_at), (parts,), jnp.float32, smallest / len(cuts), top_value / len(cuts))
        factor_of = factor_of * jnp.repeat(jnp.exp(heights), extent[axis_at] // parts).reshape((-1,) + (1,) * (len(extent) - 1 - axis_at))
    return factor_of


def split_up(count, total, limit, lean):
    portions = [(1 << 20) // math.isqrt(grade ** lean) + 1 for grade in range(2, count + 1)]
    spare, given = total - limit - (count - 1), [1] * (count - 1)
    while spare > 0:
        free = [i for i in range(count - 1) if given[i] < limit]
        whole, remaining = sum([portions[i] for i in free]), spare
        for i in free:
            addition = min(limit - given[i], max(1, remaining * portions[i] // whole), spare)
            given[i] = given[i] + addition
            spare = spare - addition
    return np.array([limit] + given)


def ragged_sizes(rng, count, total, limit, slope):
    if count == 2:
        one = jax.random.randint(rng, (), max(1, total - limit), min(limit, total - 1) + 1)
        return jnp.stack([one, total - one])
    tallies = jnp.asarray(split_up(count, total, limit, slope), jnp.int32)
    pairs = (count - 1) // 2
    source_of, receiver = tallies[1:1 + 2 * pairs:2], tallies[2:2 + 2 * pairs:2]
    margin = jnp.minimum(source_of - 1, limit - receiver)
    moved = jax.random.randint(jax.random.fold_in(rng, 1), (pairs,), 0, 1 << 20) % (margin + 1)
    tallies = tallies.at[1:1 + 2 * pairs:2].set(source_of - moved).at[2:2 + 2 * pairs:2].set(receiver + moved)
    return tallies[jax.random.permutation(jax.random.fold_in(rng, 2), count)]


def gaussian(own_key, extent, spread, bound, cuts=(), kind=jnp.bfloat16):
    values = jax.random.normal(own_key, extent, jnp.float32) * spread
    if len(cuts) > 0:
        values = level_of(own_key, extent, cuts, -0.22, 0.18) * values
    return jnp.clip(values, min=-bound, max=bound).astype(kind)


def bell_draw_with(own_key, dims, scale, limit, cuts, heavy, held_as=jnp.bfloat16):
    values = scale * jax.random.normal(own_key, dims, jnp.float32)
    if cuts:
        values = values * level_of(own_key, dims, cuts, -0.22, 0.18)
    return jnp.clip(with_spikes(values, jax.random.fold_in(own_key, 3), *heavy), -limit, limit).astype(held_as)


def setup_inputs(seed: int = 0) -> dict:
    key_of = jax.random.split(jax.random.key(seed), 14)
    return {
        "block_input": bell_draw_with(key_of[0], (SEQS, SEQ_LEN, D), 1.0, 6.0, ((0, 8),), (0, 2, 8, 2.0)),
        "segment_ids": jax.vmap(lambda own: jnp.searchsorted(jnp.cumsum(ragged_sizes(own, DOCS, SEQ_LEN, DOC_MOST, 2)), jnp.arange(SEQ_LEN), side="right"))(jax.random.split(key_of[1], SEQS)).reshape((SEQS, SEQ_LEN)).astype(jnp.int32),
        "query_weight": draw_query_weight(jax.random.fold_in(key_of[13], 71), 0),
        "key_weight": gaussian(key_of[3], (D, D), D ** -0.5, 0.1875, ((1, 4),)),
        "value_weight": gaussian(key_of[4], (D, D), D ** -0.5, 0.1875, ((1, 4),)),
        "output_weight": gaussian(key_of[5], (D, D), (D // 4) ** -0.5, 0.375, ((0, 4),)),
        "first_gain": jnp.clip(1.0 + 0.18 * jax.random.normal(key_of[6], (D,), jnp.float32), 0.1, 1.9),
        "first_shift": gaussian(key_of[7], (D,), 0.5, 3.0, (), jnp.float32),
        "up_weight": gaussian(key_of[8], (D, FF), D ** -0.5, 0.1875, ((1, 4),)),
        "down_weight": gaussian(key_of[9], (FF, D), (FF // 2) ** -0.5, 0.125, ((0, 4),)),
        "second_gain": jnp.clip(1.0 + 0.18 * jax.random.normal(key_of[10], (D,), jnp.float32), 0.1, 1.9),
        "second_shift": gaussian(key_of[11], (D,), 0.5, 3.0, (), jnp.float32),
        "out_grad": bell_draw_with(key_of[12], (SEQS, SEQ_LEN, D), 1.0, 6.0, ((0, 8),), (0, 2, 8, 2.0)),
    }


far_score = -1e+30
eps_norm = 1e-06
clip_limit = 10.0

@jax.custom_vjp
def low(v):
    return lax.optimization_barrier(v.astype(jnp.bfloat16)).astype(jnp.float32)

@jax.custom_vjp
def low_back(v):
    return v

def low_keep(v):
    return (low(v), None)

def low_pass(kept, grad):
    return (grad,)

def back_keep(v):
    return (v, None)

def back_low(kept, grad):
    return (low(grad),)
low.defvjp(low_keep, low_pass)
low_back.defvjp(back_keep, back_low)

def multiply(left, right):
    return jnp.einsum('...i,ij->...j', left, right, precision=lax.Precision.HIGHEST)

def layer_norm(total, gain, offset):
    average = lax.optimization_barrier(jnp.mean(total, axis=-1, keepdims=True))
    centred = total - average
    variance = lax.optimization_barrier(jnp.mean(centred * centred, axis=-1, keepdims=True))
    return centred * lax.rsqrt(variance + eps_norm) * gain + offset

def window_mask(segments):
    places = jnp.arange(segments.shape[0])
    nearby = jnp.abs(places[:, None] - places[None, :]) < WINDOW
    return nearby & (segments[:, None] == segments[None, :])

def attend(pieces):
    queries, keys, values, segments = pieces
    scores = jnp.einsum('qhd,khd->hqk', queries, keys, precision=lax.Precision.HIGHEST) * HEAD_DIM ** (-0.5)
    scores = low_back(scores)
    masked = jnp.where(window_mask(segments)[None], scores, far_score)
    row_top = lax.optimization_barrier(jnp.max(masked, axis=-1, keepdims=True))
    raised = jnp.exp(masked - row_top)
    chances = raised / lax.optimization_barrier(jnp.sum(raised, axis=-1, keepdims=True))
    mixed = jnp.einsum('hqk,khd->qhd', low(chances), values, precision=lax.Precision.HIGHEST)
    return (mixed, lax.optimization_barrier(jnp.max(row_top, axis=(1, 2))))

def forward(segment_ids, inputs, w_query, w_key, w_value, w_output, gain_one, offset_one, w_up, w_down, gain_two, offset_two):
    seq_count, seq_len, model_width = inputs.shape

    def heads_of(weight):
        return low_back(low(multiply(inputs, weight))).reshape(seq_count, seq_len, HEADS, HEAD_DIM)
    queries = heads_of(w_query)
    keys = heads_of(w_key)
    values = heads_of(w_value)
    mixed, tops = lax.map(jax.checkpoint(attend), (queries, keys, values, segment_ids))
    mixed = low_back(low(mixed.reshape(seq_count, seq_len, model_width)))
    branch = low_back(multiply(mixed, w_output))
    hidden = layer_norm(inputs + branch, gain_one, offset_one)
    before = low_back(multiply(low(hidden), w_up))
    active = low(jax.nn.gelu(before, approximate=False))
    branch_two = low_back(multiply(active, w_down))
    result = layer_norm(hidden + branch_two, gain_two, offset_two)
    return (result, lax.optimization_barrier(jnp.max(tops, axis=0)))

def reference(block_input, segment_ids, query_weight, key_weight, value_weight, output_weight, first_gain, first_shift, up_weight, down_weight, second_gain, second_shift, out_grad):
    floats = tuple((member.astype(jnp.float32) for member in (block_input, query_weight, key_weight, value_weight, output_weight, first_gain, first_shift, up_weight, down_weight, second_gain, second_shift)))

    def run(*members):
        return forward(segment_ids, *members)
    layer, pull, tops = jax.vjp(run, *floats, has_aux=True)
    grads = pull(out_grad.astype(jnp.float32))
    factor = jnp.sqrt(clip_limit / jnp.maximum(tops, clip_limit))
    column_factor = jnp.repeat(factor, HEAD_DIM)
    return (layer.astype(jnp.bfloat16), grads[0].astype(jnp.bfloat16), grads[1], grads[2], grads[3], grads[4], grads[5], grads[6], grads[7], grads[8], grads[9], grads[10], floats[1] * column_factor[None, :], floats[2] * column_factor[None, :])
```

```python
import jax
import jax.numpy as jnp
from jax import lax
from jax.experimental import pallas as pl
from jax.experimental.pallas import tpu as pltpu
from jax.sharding import PartitionSpec as P

F32 = jnp.float32
BF16 = jnp.bfloat16
HEAD_DIM = 64
FAR = -1e30
EPS = 1e-06
CLIP = 10.0
SCALE = HEAD_DIM**-0.5
ROOT_HALF = 0.5**0.5
BELL = 0.3989422804014327
MIB = 1 << 20


def dot(left, right, left_dim=1, right_dim=0):
    return lax.dot_general(
        left, right, (((left_dim,), (right_dim,)), ((), ())), preferred_element_type=F32
    )


def normalize(total):
    average = jnp.mean(total, axis=-1, keepdims=True)
    centred = total - average
    variance = jnp.mean(centred * centred, axis=-1, keepdims=True)
    scaled = lax.rsqrt(variance + EPS)
    return centred * scaled, scaled


def norm_back(upstream, normed, scaled, gain):
    weighted = upstream * gain
    first = jnp.mean(weighted, axis=-1, keepdims=True)
    second = jnp.mean(weighted * normed, axis=-1, keepdims=True)
    return scaled * (weighted - first - normed * second)


def head_of(width):
    return lax.broadcasted_iota(jnp.int32, (1, width), 1) // HEAD_DIM


def params(vmem_mib, dims=1):
    return pltpu.CompilerParams(
        vmem_limit_bytes=vmem_mib * MIB,
        dimension_semantics=("arbitrary",) * dims if dims else None,
    )


def cost(flops, bytes_accessed, transcendentals=0):
    return pl.CostEstimate(
        flops=int(flops), bytes_accessed=int(bytes_accessed), transcendentals=int(transcendentals)
    )


def attend_kernel(x_ref, wq_ref, wk_ref, wv_ref, row_ref, col_ref, o_ref, top_ref):
    x = x_ref[0]
    queries = (dot(x, wq_ref[...]).astype(BF16) * SCALE).astype(BF16)
    keys = dot(x, wk_ref[...]).astype(BF16)
    values = dot(x, wv_ref[...]).astype(BF16)
    width = queries.shape[1]
    owner = head_of(width)
    same = col_ref[0][:, 0:1] == row_ref[0][0:1, :]
    total = jnp.zeros(queries.shape, F32)
    zero = jnp.zeros((), BF16)
    for head in range(width // HEAD_DIM):
        mine = owner == head
        scores = dot(jnp.where(mine, queries, zero), keys, 1, 1)
        scores = jnp.where(same, scores, FAR)
        top = jnp.max(scores, axis=-1, keepdims=True)
        raised = jnp.exp(scores - top)
        chances = raised * (1.0 / jnp.sum(raised, axis=-1, keepdims=True))
        total = total + dot(chances.astype(BF16), jnp.where(mine, values, zero))
        top_ref[head : head + 1, :] = jnp.broadcast_to(
            jnp.max(top, axis=0, keepdims=True), (1, top_ref.shape[1])
        )
    o_ref[...] = total.astype(BF16).astype(F32)


def attend(s, block_input, wq, wk, wv, seg_row, seg_col):
    _, length, depth = block_input.shape
    width = wq.shape[1]
    heads = width // HEAD_DIM
    return pl.pallas_call(
        attend_kernel,
        grid=(1,),
        in_specs=[
            pl.BlockSpec((1, length, depth), lambda i: (s, 0, 0)),
            pl.BlockSpec((depth, width), lambda i: (0, 0)),
            pl.BlockSpec((depth, width), lambda i: (0, 0)),
            pl.BlockSpec((depth, width), lambda i: (0, 0)),
            pl.BlockSpec((1, 8, length), lambda i: (s, 0, 0)),
            pl.BlockSpec((1, length, 128), lambda i: (s, 0, 0)),
        ],
        out_specs=[
            pl.BlockSpec((length, width), lambda i: (0, 0)),
            pl.BlockSpec((heads, 128), lambda i: (0, 0)),
        ],
        out_shape=[
            jax.ShapeDtypeStruct((length, width), F32),
            jax.ShapeDtypeStruct((heads, 128), F32),
        ],
        compiler_params=params(32),
        cost_estimate=cost(
            2 * length * depth * 3 * width + 4 * length * length * width,
            2 * length * depth + 6 * depth * width,
            heads * length * length,
        ),
        name="attend",
    )(block_input, wq, wk, wv, seg_row, seg_col)


def widen_kernel(where_ref, wq_ref, wk_ref, wv_ref, wo_ref, slice_ref, out_ref):
    width = wq_ref.shape[1]
    for index, ref in enumerate((wq_ref, wk_ref, wv_ref)):
        slice_ref[:, index * width : (index + 1) * width] = ref[...].astype(F32)
    out_ref[...] = wo_ref[...].astype(F32)


def widen(where, wq, wk, wv, wo, part):
    width = wq.shape[1]
    rows = pl.BlockSpec((part, width), lambda i, w: (w[3], 0))
    whole = lambda i, w: (0, 0)
    return pl.pallas_call(
        widen_kernel,
        grid_spec=pltpu.PrefetchScalarGridSpec(
            num_scalar_prefetch=1,
            grid=(1,),
            in_specs=[rows, rows, rows, pl.BlockSpec(wo.shape, whole)],
            out_specs=[pl.BlockSpec((part, 3 * width), whole), pl.BlockSpec(wo.shape, whole)],
        ),
        out_shape=[
            jax.ShapeDtypeStruct((part, 3 * width), F32),
            jax.ShapeDtypeStruct(wo.shape, F32),
        ],
        compiler_params=params(16),
        cost_estimate=cost(0, 6 * wo.size + 18 * part * width),
        name="widen",
    )(where, wq, wk, wv, wo)


def pair_kernel(where_ref, wq_ref, wk_ref, wv_ref, wo_ref, others_ref, far_ref, *out_refs):
    index = pl.program_id(0)
    width = wq_ref.shape[1]
    mine = index == where_ref[2]
    for place, (own, out) in enumerate(zip((wq_ref, wk_ref, wv_ref), out_refs)):
        other = others_ref[:, place * width : (place + 1) * width].astype(BF16)
        out[...] = jnp.where(mine, own[...], other)
    out_refs[3][...] = jnp.where(mine, wo_ref[...], far_ref[...].astype(BF16))


def pair(where, wq, wk, wv, wo, others, far):
    depth, width = wq.shape
    whole = lambda i, w: (0, 0)
    column = pl.BlockSpec((depth, width), lambda i, w: (0, i))
    return pl.pallas_call(
        pair_kernel,
        grid_spec=pltpu.PrefetchScalarGridSpec(
            num_scalar_prefetch=1,
            grid=(2,),
            in_specs=[pl.BlockSpec(a.shape, whole) for a in (wq, wk, wv, wo, others, far)],
            out_specs=[column, column, column, pl.BlockSpec(wo.shape, lambda i, w: (i, 0))],
        ),
        out_shape=[jax.ShapeDtypeStruct((depth, 2 * width), BF16)] * 3
        + [jax.ShapeDtypeStruct((2 * wo.shape[0], wo.shape[1]), BF16)],
        compiler_params=params(32),
        cost_estimate=cost(0, 32 * depth * width),
        name="pair",
    )(where, wq, wk, wv, wo, others, far)


def finish_kernel(where_ref, own_ref, near_ref, *rest):
    out_ref = rest[-1]
    mine = pl.program_id(0) == where_ref[1]
    out_ref[0] = jnp.where(mine, own_ref[...], near_ref[...]).astype(BF16)


def finish(s, count, where, own, near, input_grad):
    half, depth = own.shape
    whole = pl.BlockSpec((half, depth), lambda i, w: (0, 0))
    carried = [] if input_grad is None else [input_grad]
    return pl.pallas_call(
        finish_kernel,
        grid_spec=pltpu.PrefetchScalarGridSpec(
            num_scalar_prefetch=1,
            grid=(2,),
            in_specs=[whole, whole, *[pl.BlockSpec(memory_space=pl.ANY)] * len(carried)],
            out_specs=pl.BlockSpec((1, half, depth), lambda i, w: (s, i, 0)),
        ),
        out_shape=jax.ShapeDtypeStruct((count, 2 * half, depth), BF16),
        input_output_aliases={3: 0} if carried else {},
        compiler_params=params(16),
        cost_estimate=cost(0, 12 * half * depth),
        name="finish",
    )(where, own, near, *carried)


def assemble_kernel(where_ref, own_ref, far_ref, near_ref, both_ref, out_ref):
    place = pl.program_id(0) ^ where_ref[0]

    @pl.when(place == 0)
    def _():
        out_ref[...] = own_ref[...].astype(BF16)

    @pl.when(place == 2)
    def _():
        out_ref[...] = far_ref[...].astype(BF16)

    @pl.when(place == 1)
    def _():
        out_ref[...] = near_ref[...].astype(BF16)

    @pl.when(place == 3)
    def _():
        out_ref[...] = both_ref[...].astype(BF16)


def assemble(where, own, far, near, both):
    rows, columns = own.shape
    whole = lambda i, w: (0, 0)
    return pl.pallas_call(
        assemble_kernel,
        grid_spec=pltpu.PrefetchScalarGridSpec(
            num_scalar_prefetch=1,
            grid=(4,),
            in_specs=[pl.BlockSpec((rows, columns), whole)] * 4,
            out_specs=pl.BlockSpec((rows, columns), lambda i, w: (i, 0)),
        ),
        out_shape=jax.ShapeDtypeStruct((4 * rows, columns), BF16),
        compiler_params=params(24),
        cost_estimate=cost(0, 20 * rows * columns),
        name="assemble",
    )(where, own, far, near, both)


def forward_kernel(
    where_ref, x_ref, own_ref, near_ref, far_ref, both_ref, wo_ref, gain_ref, shift_ref,
    up_ref, down_ref,
    normed_ref, scaled_ref, low_ref, active_ref, pull_ref, send_ref, keep_ref,
    mixed_ref,
):
    step = pl.program_id(0)
    me = where_ref[0]
    width = own_ref.shape[1]
    for flip, piece in enumerate((own_ref, near_ref, far_ref, both_ref)):
        start = pl.multiple_of((me ^ flip) * width, width)
        mixed_ref[:, pl.ds(start, width)] = piece[...].astype(BF16)
    branch = dot(mixed_ref[...], wo_ref[...])
    normed, scaled = normalize(x_ref[0].astype(F32) + branch)
    normed_ref[...] = normed
    scaled_ref[...] = jnp.broadcast_to(scaled, scaled_ref.shape)
    low = (normed * gain_ref[...] + shift_ref[...]).astype(BF16)
    low_ref[...] = low
    before = dot(low, up_ref[...])
    chance = 0.5 * (1.0 + lax.erf(before * ROOT_HALF))
    active = (before * chance).astype(BF16)
    active_ref[...] = active
    pull_ref[...] = chance + before * (jnp.exp(-0.5 * before * before) * BELL)
    part = dot(active, down_ref[...])

    @pl.when(step == 0)
    def _():
        send_ref[...] = part

    @pl.when(step == 1)
    def _():
        keep_ref[...] = part


def half_of(step, where):
    return (1 - where[1] + step) % 2


def forward(s, where, block_input, pieces, wo, gain, shift, up, down):
    _, length, depth = block_input.shape
    width = pieces[0].shape[1]
    hidden = up.shape[1]
    half = length // 2
    rows = lambda i, w: (half_of(i, w), 0)
    whole = lambda i, w: (0, 0)
    return pl.pallas_call(
        forward_kernel,
        grid_spec=pltpu.PrefetchScalarGridSpec(
            num_scalar_prefetch=1,
            grid=(2,),
            in_specs=[
                pl.BlockSpec((1, half, depth), lambda i, w: (s, half_of(i, w), 0)),
                *[pl.BlockSpec((half, width), rows)] * 4,
                pl.BlockSpec((4 * width, depth), whole),
                pl.BlockSpec((1, depth), whole),
                pl.BlockSpec((1, depth), whole),
                pl.BlockSpec((depth, hidden), whole),
                pl.BlockSpec((hidden, depth), whole),
            ],
            out_specs=[
                pl.BlockSpec((half, depth), rows),
                pl.BlockSpec((half, 128), rows),
                pl.BlockSpec((half, depth), rows),
                pl.BlockSpec((half, hidden), rows),
                pl.BlockSpec((half, hidden), rows),
                pl.BlockSpec((half, depth), whole),
                pl.BlockSpec((half, depth), whole),
            ],
            scratch_shapes=[pltpu.VMEM((half, 4 * width), BF16)],
        ),
        out_shape=[
            jax.ShapeDtypeStruct((length, depth), F32),
            jax.ShapeDtypeStruct((length, 128), F32),
            jax.ShapeDtypeStruct((length, depth), BF16),
            jax.ShapeDtypeStruct((length, hidden), BF16),
            jax.ShapeDtypeStruct((length, hidden), F32),
            jax.ShapeDtypeStruct((half, depth), F32),
            jax.ShapeDtypeStruct((half, depth), F32),
        ],
        compiler_params=params(40),
        cost_estimate=cost(
            2 * length * depth * (4 * width + 2 * hidden),
            2 * depth * (4 * width + 2 * hidden) + 20 * length * depth,
            2 * length * hidden,
        ),
        name="forward",
    )(where, block_input, *pieces, wo, gain, shift, up, down)


def backward_kernel(
    where_ref, normed_ref, gain_ref, shift_ref, own_ref, near_ref, grad_ref, second_gain_ref,
    second_shift_ref, pull_ref, up_ref, down_ref, *rest,
):
    out_ref, slope_ref, slope_low_ref, before_ref, send_ref, keep_ref, sums_ref = rest[-7:]
    step = pl.program_id(0)
    total = jnp.where(step == 0, near_ref[...], own_ref[...])
    hidden = normed_ref[...] * gain_ref[...] + shift_ref[...]
    normed, scaled = normalize(hidden + total)
    out_ref[0] = (normed * second_gain_ref[...] + second_shift_ref[...]).astype(BF16)
    upstream = grad_ref[0].astype(F32)
    gain_part = jnp.sum(upstream * normed, axis=0, keepdims=True)
    shift_part = jnp.sum(upstream, axis=0, keepdims=True)

    @pl.when(step == 0)
    def _():
        sums_ref[...] = jnp.zeros_like(sums_ref)

    sums_ref[0:1, :] += gain_part
    sums_ref[1:2, :] += shift_part
    slope = norm_back(upstream, normed, scaled, second_gain_ref[...])
    slope_ref[...] = slope
    low = slope.astype(BF16)
    slope_low_ref[...] = low
    before = (dot(low, down_ref[...], 1, 1) * pull_ref[...]).astype(BF16)
    before_ref[...] = before
    part = dot(before, up_ref[...], 1, 1)

    @pl.when(step == 0)
    def _():
        send_ref[...] = part

    @pl.when(step == 1)
    def _():
        keep_ref[...] = part


def backward(
    s, where, normed, gain, shift, own, near, out_grad, second_gain, second_shift, pull, up, down,
    layer_out,
):
    count, length, depth = out_grad.shape
    hidden = up.shape[1]
    half = length // 2
    rows = lambda i, w: (half_of(i, w), 0)
    whole = lambda i, w: (0, 0)
    block = lambda i, w: (s, half_of(i, w), 0)
    vector = pl.BlockSpec((1, depth), whole)
    carried = [] if layer_out is None else [layer_out]
    return pl.pallas_call(
        backward_kernel,
        grid_spec=pltpu.PrefetchScalarGridSpec(
            num_scalar_prefetch=1,
            grid=(2,),
            in_specs=[
                pl.BlockSpec((half, depth), rows),
                vector,
                vector,
                pl.BlockSpec((half, depth), whole),
                pl.BlockSpec((half, depth), whole),
                pl.BlockSpec((1, half, depth), block),
                vector,
                vector,
                pl.BlockSpec((half, hidden), rows),
                pl.BlockSpec((depth, hidden), whole),
                pl.BlockSpec((hidden, depth), whole),
                *[pl.BlockSpec(memory_space=pl.ANY)] * len(carried),
            ],
            out_specs=[
                pl.BlockSpec((1, half, depth), block),
                pl.BlockSpec((half, depth), rows),
                pl.BlockSpec((half, depth), rows),
                pl.BlockSpec((half, hidden), rows),
                pl.BlockSpec((half, depth), whole),
                pl.BlockSpec((half, depth), whole),
                pl.BlockSpec((8, depth), whole),
            ],
        ),
        out_shape=[
            jax.ShapeDtypeStruct((count, length, depth), BF16),
            jax.ShapeDtypeStruct((length, depth), F32),
            jax.ShapeDtypeStruct((length, depth), BF16),
            jax.ShapeDtypeStruct((length, hidden), BF16),
            jax.ShapeDtypeStruct((half, depth), F32),
            jax.ShapeDtypeStruct((half, depth), F32),
            jax.ShapeDtypeStruct((8, depth), F32),
        ],
        input_output_aliases={12: 0} if carried else {},
        compiler_params=params(40),
        cost_estimate=cost(4 * length * depth * hidden, 4 * depth * hidden + 22 * length * depth),
        name="backward",
    )(
        where, normed, gain, shift, own, near, out_grad, second_gain, second_shift, pull, up, down,
        *carried,
    )


def products_kernel(*refs):
    *terms, out_ref = refs
    count = len(terms) // 2
    total = dot(terms[0][...], terms[count][...], 0, 0)
    for left, right in zip(terms[1:count], terms[count + 1 :]):
        total = total + dot(left[...], right[...], 0, 0)
    out_ref[...] = total


def products(lefts, rights, tile=256):
    length, depth = lefts[0].shape
    width = rights[0].shape[1]
    count = len(lefts)
    return pl.pallas_call(
        products_kernel,
        grid=(depth // tile,),
        in_specs=[pl.BlockSpec((length, tile), lambda i: (0, i))] * count
        + [pl.BlockSpec((length, width), lambda i: (0, 0))] * count,
        out_specs=pl.BlockSpec((tile, width), lambda i: (i, 0)),
        out_shape=jax.ShapeDtypeStruct((depth, width), F32),
        compiler_params=params(32),
        cost_estimate=cost(
            2 * count * length * depth * width,
            2 * count * length * (depth + width) + 4 * depth * width,
        ),
        name="products",
    )(*lefts, *rights)


def project_kernel(x_ref, wq_ref, wk_ref, wv_ref, q_ref, k_ref, v_ref):
    x = x_ref[0]
    q_ref[0] = (dot(x, wq_ref[...]).astype(BF16) * SCALE).astype(BF16)
    k_ref[0] = dot(x, wk_ref[...]).astype(BF16)
    v_ref[0] = dot(x, wv_ref[...]).astype(BF16)


def project(block_input, wq, wk, wv):
    count, length, depth = block_input.shape
    width = wq.shape[1]
    weight = pl.BlockSpec((depth, width), lambda s: (0, 0))
    out = pl.BlockSpec((1, length, width), lambda s: (s, 0, 0))
    return pl.pallas_call(
        project_kernel,
        grid=(count,),
        in_specs=[pl.BlockSpec((1, length, depth), lambda s: (s, 0, 0)), weight, weight, weight],
        out_specs=[out] * 3,
        out_shape=[jax.ShapeDtypeStruct((count, length, width), BF16)] * 3,
        compiler_params=params(32),
        cost_estimate=cost(
            6 * count * length * depth * width, 2 * count * length * (depth + 3 * width)
        ),
        name="project",
    )(block_input, wq, wk, wv)


def first_kernel(
    where_ref, own_ref, near_ref, slope_ref, normed_ref, scaled_ref, gain_ref, wo_ref,
    one_ref, low_ref, mixed_ref, sums_ref,
):
    step = pl.program_id(0)
    total = jnp.where(step == 0, near_ref[...], own_ref[...])
    upstream = slope_ref[...] + total
    normed = normed_ref[...]

    @pl.when(step == 0)
    def _():
        sums_ref[...] = jnp.zeros_like(sums_ref)

    sums_ref[0:1, :] += jnp.sum(upstream * normed, axis=0, keepdims=True)
    sums_ref[1:2, :] += jnp.sum(upstream, axis=0, keepdims=True)
    slope = norm_back(upstream, normed, scaled_ref[:, 0:1], gain_ref[...])
    low = slope.astype(BF16)
    low_ref[...] = low
    mixed_ref[...] = dot(low, wo_ref[...], 1, 1).astype(BF16)

    @pl.when(step == 1)
    def _():
        one_ref[...] = slope


def first(where, own, near, slope, normed, scaled, gain, wo):
    length, depth = slope.shape
    width = wo.shape[0]
    half = length // 2
    rows = lambda i, w: (half_of(i, w), 0)
    whole = lambda i, w: (0, 0)
    return pl.pallas_call(
        first_kernel,
        grid_spec=pltpu.PrefetchScalarGridSpec(
            num_scalar_prefetch=1,
            grid=(2,),
            in_specs=[
                pl.BlockSpec((half, depth), whole),
                pl.BlockSpec((half, depth), whole),
                pl.BlockSpec((half, depth), rows),
                pl.BlockSpec((half, depth), rows),
                pl.BlockSpec((half, 128), rows),
                pl.BlockSpec((1, depth), whole),
                pl.BlockSpec((width, depth), whole),
            ],
            out_specs=[
                pl.BlockSpec((half, depth), whole),
                pl.BlockSpec((half, depth), rows),
                pl.BlockSpec((half, width), rows),
                pl.BlockSpec((8, depth), whole),
            ],
        ),
        out_shape=[
            jax.ShapeDtypeStruct((half, depth), F32),
            jax.ShapeDtypeStruct((length, depth), BF16),
            jax.ShapeDtypeStruct((length, width), BF16),
            jax.ShapeDtypeStruct((8, depth), F32),
        ],
        compiler_params=params(32),
        cost_estimate=cost(2 * length * depth * width, 18 * length * depth),
        name="first",
    )(where, own, near, slope, normed, scaled, gain, wo)


def attend_back_kernel(
    where_ref, q_ref, k_ref, v_ref, go_ref, row_ref, col_ref, wq_ref, wk_ref, wv_ref, one_ref,
    gq_ref, gk_ref, gv_ref, send_ref, keep_ref,
    key_slope, value_slope, part_ref,
):
    group = pl.program_id(0)
    queries, keys, values, upstream = q_ref[0], k_ref[0], v_ref[0], go_ref[...]
    width = queries.shape[1]
    half = queries.shape[0] // 2
    owner = head_of(width)
    same = col_ref[0][:, 0:1] == row_ref[0][0:1, :]
    zero = jnp.zeros((), BF16)
    queries_t = queries.T
    upstream_t = upstream.T
    query_slope = jnp.zeros(queries.shape, F32)
    for head in range(width // HEAD_DIM):
        mine = owner == head
        place = slice(head * HEAD_DIM, (head + 1) * HEAD_DIM)
        scores = dot(jnp.where(mine, queries, zero), keys, 1, 1)
        scores = jnp.where(same, scores, FAR)
        top = jnp.max(scores, axis=-1, keepdims=True)
        raised = jnp.exp(scores - top)
        chances = raised * (1.0 / jnp.sum(raised, axis=-1, keepdims=True))
        drift = dot(jnp.where(mine, upstream, zero), values, 1, 1)
        slopes = chances * (drift - jnp.sum(drift * chances, axis=-1, keepdims=True))
        slopes = slopes.astype(BF16)
        query_slope = query_slope + dot(slopes, jnp.where(mine, keys, zero))
        key_slope[place, :] = dot(queries_t[place, :], slopes)
        value_slope[place, :] = dot(upstream_t[place, :], chances.astype(BF16))
    gq = (query_slope * SCALE).astype(BF16)
    gk = key_slope[...].T.astype(BF16)
    gv = value_slope[...].T.astype(BF16)
    gq_ref[...] = gq
    gk_ref[...] = gk
    gv_ref[...] = gv
    part = dot(gq, wq_ref[...], 1, 1) + dot(gk, wk_ref[...], 1, 1) + dot(gv, wv_ref[...], 1, 1)

    @pl.when(group == 0)
    def _():
        part_ref[...] = part

    @pl.when(group == 1)
    def _():
        part_ref[...] += part
        core = where_ref[1]
        kept = pl.multiple_of(core * half, half)
        sent = pl.multiple_of((1 - core) * half, half)
        keep_ref[...] = part_ref[pl.ds(kept, half), :] + one_ref[...]
        send_ref[...] = part_ref[pl.ds(sent, half), :]


def attend_back(s, where, q, k, v, mixed_slope, seg_row, seg_col, wq, wk, wv, one):
    _, length, both = q.shape
    depth = wq.shape[0]
    width = both // 2
    half = length // 2
    piece = pl.BlockSpec((1, length, width), lambda g, w: (s, 0, g))
    flat = pl.BlockSpec((length, width), lambda g, w: (0, g))
    weight = pl.BlockSpec((depth, width), lambda g, w: (0, g))
    whole = lambda g, w: (0, 0)
    return pl.pallas_call(
        attend_back_kernel,
        grid_spec=pltpu.PrefetchScalarGridSpec(
            num_scalar_prefetch=1,
            grid=(2,),
            in_specs=[
                piece,
                piece,
                piece,
                flat,
                pl.BlockSpec((1, 8, length), lambda g, w: (s, 0, 0)),
                pl.BlockSpec((1, length, 128), lambda g, w: (s, 0, 0)),
                weight,
                weight,
                weight,
                pl.BlockSpec((half, depth), whole),
            ],
            out_specs=[
                flat,
                flat,
                flat,
                pl.BlockSpec((half, depth), whole),
                pl.BlockSpec((half, depth), whole),
            ],
            scratch_shapes=[
                pltpu.VMEM((width, length), F32),
                pltpu.VMEM((width, length), F32),
                pltpu.VMEM((length, depth), F32),
            ],
        ),
        out_shape=[
            jax.ShapeDtypeStruct((length, both), BF16),
            jax.ShapeDtypeStruct((length, both), BF16),
            jax.ShapeDtypeStruct((length, both), BF16),
            jax.ShapeDtypeStruct((half, depth), F32),
            jax.ShapeDtypeStruct((half, depth), F32),
        ],
        compiler_params=params(40),
        cost_estimate=cost(
            10 * length * length * both + 6 * length * depth * both,
            6 * depth * both + 12 * length * depth,
            length * length * both // HEAD_DIM,
        ),
        name="attend_back",
    )(where, q, k, v, mixed_slope, seg_row, seg_col, wq, wk, wv, one)


def head_products_kernel(where_ref, *refs):
    *terms, out_ref = refs
    count = len(terms) // 2
    total = dot(terms[0][0], terms[count][...], 0, 0)
    for left, right in zip(terms[1:count], terms[count + 1 :]):
        total = total + dot(left[0], right[...], 0, 0)
    out_ref[...] = total


def head_products(where, block_input, rights, tile=256):
    count, length, depth = block_input.shape
    width = rights[0].shape[1] // 2
    return pl.pallas_call(
        head_products_kernel,
        grid_spec=pltpu.PrefetchScalarGridSpec(
            num_scalar_prefetch=1,
            grid=(depth // tile,),
            in_specs=[
                pl.BlockSpec((1, length, tile), lambda i, w, s=s: (s, 0, i)) for s in range(count)
            ]
            + [pl.BlockSpec((length, width), lambda i, w: (0, w[2]))] * count,
            out_specs=pl.BlockSpec((tile, width), lambda i, w: (i, 0)),
        ),
        out_shape=jax.ShapeDtypeStruct((depth, width), F32),
        compiler_params=params(32),
        cost_estimate=cost(
            2 * count * length * depth * width,
            2 * count * length * (depth + width) + 4 * depth * width,
        ),
        name="head_products",
    )(where, *[block_input] * count, *rights)


def solution(mesh):
    ranks = mesh.shape["dp"]
    group = mesh.shape["tensor"]
    assert group == 4
    near_pairs = [(t, t ^ 1) for t in range(group)]
    far_pairs = [(t, t ^ 2) for t in range(group)]

    def near(value):
        return lax.ppermute(value, "tensor", near_pairs)

    def far(value):
        return lax.ppermute(value, "tensor", far_pairs)

    def gather_pieces(own):
        beside = near(own)
        across = far(own)
        return own, beside, across, near(across)

    def sum_halves(send, keep):
        chip = keep + near(send)
        total = chip + far(chip)
        return total, near(total)

    def scatter(value):
        return lax.psum_scatter(value, "dp", scatter_dimension=0, tiled=True)

    def body(
        block_input, segment_ids, query_weight, key_weight, value_weight, output_weight,
        first_gain, first_shift, up_weight, down_weight, second_gain, second_shift, out_grad,
    ):
        count, length, depth = block_input.shape
        width = query_weight.shape[1]
        me = lax.axis_index("tensor")
        rank = lax.axis_index("dp")
        core = me % 2
        chip = me // 2
        where = jnp.stack([me, core, chip, rank]).astype(jnp.int32)
        seg_row = jnp.broadcast_to(segment_ids[:, None, :], (count, 8, length))
        seg_col = jnp.broadcast_to(segment_ids[:, :, None], (count, length, 128))
        gain_one, shift_one = first_gain[None], first_shift[None]
        gain_two, shift_two = second_gain[None], second_shift[None]

        part = depth // ranks
        slices, wo_wide = widen(
            where, query_weight, key_weight, value_weight, output_weight, part
        )
        wo_own, wo_near, wo_far, wo_both = gather_pieces(wo_wide)
        wo = assemble(where, wo_own, wo_far, wo_near, wo_both)

        others = lax.all_gather(far(slices), "dp", axis=0, tiled=True)
        wq, wk, wv, wo_pair = pair(
            where, query_weight, key_weight, value_weight, output_weight, others, wo_far
        )

        tops, mixed, kept, sums = [], [], [], []
        for s in range(count):
            own, top = attend(
                s, block_input, query_weight, key_weight, value_weight, seg_row, seg_col
            )
            tops.append(top)
            mixed.append(own)
            pieces = gather_pieces(own)
            normed, scaled, low, active, pull, send, keep = forward(
                s, where, block_input, pieces, wo, gain_one, shift_one, up_weight, down_weight
            )
            kept.append((normed, scaled, low, active, pull))
            sums.append(sum_halves(send, keep))

        layer_out = None
        slopes, slope_lows, befores, hidden_sums, second_sums = [], [], [], [], []
        for s in range(count):
            normed, scaled, low, active, pull = kept[s]
            layer_out, slope, slope_low, before, send, keep, second = backward(
                s, where, normed, gain_one, shift_one, *sums[s], out_grad, gain_two, shift_two,
                pull, up_weight, down_weight, layer_out,
            )
            slopes.append(slope)
            slope_lows.append(slope_low)
            befores.append(before)
            second_sums.append(second)
            hidden_sums.append(sum_halves(send, keep))

        up_part = products([k[2] for k in kept], befores)
        down_part = products(slope_lows, [k[3] for k in kept])
        up_grad = scatter(up_part)
        down_grad = scatter(down_part).T

        q, k, v = project(block_input, wq, wk, wv)
        input_grad = None
        ones, gqs, gks, gvs, first_sums = [], [], [], [], []
        for s in range(count):
            normed, scaled = kept[s][:2]
            one, one_low, mixed_slope, first_sum = first(
                where, *hidden_sums[s], slopes[s], normed, scaled, gain_one, wo_pair
            )
            ones.append(one_low)
            first_sums.append(first_sum)
            gq, gk, gv, send, keep = attend_back(
                s, where, q, k, v, mixed_slope, seg_row, seg_col, wq, wk, wv, one
            )
            gqs.append(gq)
            gks.append(gk)
            gvs.append(gv)
            mine = keep + near(send)
            input_grad = finish(s, count, where, mine, near(mine), input_grad)

        output_part = products(ones, [m.astype(BF16) for m in mixed])
        query_part = head_products(where, block_input, gqs)
        key_part = head_products(where, block_input, gks)
        value_part = head_products(where, block_input, gvs)
        output_grad = scatter(output_part).T
        query_grad = scatter(query_part)
        key_grad = scatter(key_part)
        value_grad = scatter(value_part)

        gains = jnp.concatenate(
            [sum(x[0:2] for x in first_sums), sum(x[0:2] for x in second_sums)], axis=0
        )
        gains = lax.all_gather(gains, "dp", axis=0, tiled=False)
        gains = jnp.sum(
            lax.dynamic_slice_in_dim(gains, rank * part, part, 2), axis=0
        )
        peak = jnp.max(jnp.stack([t[:, 0] for t in tops]), axis=0)
        peak = jnp.max(lax.all_gather(peak, "dp", axis=0, tiled=False), axis=0)
        factor = jnp.sqrt(CLIP / jnp.maximum(peak, CLIP))
        column_factor = jnp.repeat(factor, HEAD_DIM)
        query_clipped = query_weight.astype(F32) * column_factor[None, :]
        key_clipped = key_weight.astype(F32) * column_factor[None, :]
        return (
            layer_out, input_grad, query_grad, key_grad, value_grad, output_grad,
            gains[0], gains[1], up_grad, down_grad, gains[2], gains[3],
            query_clipped, key_clipped,
        )

    batch = P("dp", None, None)
    in_specs = (
        batch, P("dp", None), P(None, "tensor"), P(None, "tensor"), P(None, "tensor"),
        P("tensor", None), P(), P(), P(None, "tensor"), P("tensor", None), P(), P(), batch,
    )
    out_specs = (
        batch, batch, P("dp", "tensor"), P("dp", "tensor"), P("dp", "tensor"), P("tensor", "dp"),
        P("dp"), P("dp"), P("dp", "tensor"), P("tensor", "dp"), P("dp"), P("dp"),
        P(None, "tensor"), P(None, "tensor"),
    )
    return jax.shard_map(body, mesh=mesh, in_specs=in_specs, out_specs=out_specs, check_vma=False)
```

```python
import functools

import jax
import jax.numpy as jnp
from jax import lax
from jax.experimental import pallas as pl
from jax.experimental.pallas import tpu as pltpu
from jax.sharding import PartitionSpec as P

F32 = jnp.float32
BF16 = jnp.bfloat16
HEAD_DIM = 64
FAR = -1e30
EPS = 1e-06
CLIP = 10.0
SCALE = HEAD_DIM**-0.5
ROOT_HALF = 0.5**0.5
BELL = 0.3989422804014327
GROUP = 4
DOCS = 4
MIB = 1 << 20
RING = (0, 2, 4, 6, 7, 5, 3, 1)
OWNERS = tuple(
    tuple(RING[(RING.index(r) + way * (1 + n)) % 8] for n in range(8) for way in (-1, 1))
    for r in range(8)
)
ANY = pl.BlockSpec(memory_space=pl.ANY)
RESIDENT = pl.BlockSpec(memory_space=pltpu.VMEM)


def dot(left, right, left_dim=1, right_dim=0):
    return lax.dot_general(
        left, right, (((left_dim,), (right_dim,)), ((), ())), preferred_element_type=F32
    )


def normalize(total):
    average = jnp.mean(total, axis=-1, keepdims=True)
    centred = total - average
    variance = jnp.mean(centred * centred, axis=-1, keepdims=True)
    scaled = lax.rsqrt(variance + EPS)
    return centred * scaled, scaled


def norm_back(upstream, normed, scaled, gain):
    weighted = upstream * gain
    first = jnp.mean(weighted, axis=-1, keepdims=True)
    second = jnp.mean(weighted * normed, axis=-1, keepdims=True)
    return scaled * (weighted - first - normed * second)


def lanes(width):
    lane = lax.broadcasted_iota(jnp.int32, (1, width), 1)
    return lane // HEAD_DIM, lane % HEAD_DIM


def mask_terms(ids, width):
    _, lane = lanes(width)
    equal = ids == lane
    document = lane < DOCS
    queries = jnp.where(document & equal, FAR, 0.0).astype(BF16)
    keys = jnp.where(document & equal, 0.0, jnp.where(lane < DOCS + 3, 1.0, 0.0)).astype(BF16)
    return queries, keys


def split(value):
    high = value.astype(BF16)
    rest = value - high.astype(F32)
    middle = rest.astype(BF16)
    return high, middle, (rest - middle.astype(F32)).astype(BF16)


def pick(head, owner, own, spare, zero):
    return jnp.where(owner == head, own, jnp.where(owner == (head + 1) % GROUP, spare, zero))


def shape(dims, dtype):
    return jax.ShapeDtypeStruct(tuple(dims), dtype)


def whole_block(array):
    zeros = (0,) * len(array.shape)
    return pl.BlockSpec(tuple(array.shape), lambda i, w: zeros)


def rows_block(rows, columns):
    return pl.BlockSpec((rows, columns), lambda i, w: (i, 0))


class Order:
    def __init__(self):
        self.token, self.stored = None, False

    def taken(self):
        if self.token is None:
            return []
        if self.stored:
            return [pltpu.with_memory_space_constraint(self.token, pltpu.HBM)]
        return [self.token]

    def give(self, results, stored):
        sizes = [r.size * r.dtype.itemsize for r in results]
        index = sizes.index(min(sizes))
        self.token, self.stored = results[index], index in stored


def launch(
    kernel, name, where, inputs, in_specs, outs, out_specs, grid, vmem, after,
    scratch=(), aliases=None, streamed=(), stored=(),
):
    count = len(inputs)
    tokens = after.taken()
    inputs = [
        pltpu.with_memory_space_constraint(value, pltpu.HBM) if i in streamed else value
        for i, value in enumerate(inputs)
    ]
    outs = [
        pltpu.HBM(value.shape, value.dtype) if i in stored else value
        for i, value in enumerate(outs)
    ]

    def run(where_ref, *refs):
        kernel(where_ref, *refs[:count], *refs[count + len(tokens) :])

    results = pl.pallas_call(
        run,
        grid_spec=pltpu.PrefetchScalarGridSpec(
            num_scalar_prefetch=1,
            grid=grid,
            in_specs=list(in_specs) + [ANY] * len(tokens),
            out_specs=list(out_specs),
            scratch_shapes=list(scratch),
        ),
        out_shape=outs,
        input_output_aliases=aliases or {},
        compiler_params=pltpu.CompilerParams(
            vmem_limit_bytes=vmem * MIB, dimension_semantics=("arbitrary",) * len(grid)
        ),
        cost_estimate=pl.CostEstimate(flops=1, bytes_accessed=1, transcendentals=0),
        name=name,
    )(where, *inputs, *tokens)
    after.give(results, stored)
    return results


def gate_kernel(*refs):
    del refs


def gate(where, *values, after):
    outs = [shape(v.shape, v.dtype) for v in values]
    return launch(
        gate_kernel, "gate", where, values, [ANY] * len(values), outs, [ANY] * len(values), (1,),
        2, after, aliases={i + 1: i for i in range(len(values))},
    )


def parts_kernel(where_ref, value_ref, left_ref, right_ref, slices_ref):
    rows, half = left_ref.shape
    left_ref[...] = value_ref[0:rows, 0:half]
    right_ref[...] = value_ref[0:rows, half:]
    slices_ref[...] = value_ref[rows:, 0 : slices_ref.shape[1]]


def parts(where, value, rows, columns, after):
    depth = value.shape[1]
    outs = [shape((rows, depth // 2), F32)] * 2 + [shape((value.shape[0] - rows, columns), F32)]
    return launch(
        parts_kernel, "parts", where, (value,), [whole_block(value)], outs,
        [whole_block(o) for o in outs], (1,), 8, after,
    )


def widen_heads_kernel(where_ref, wq_ref, wk_ref, wv_ref, wo_ref, sq, sk, sv, own, wide, wo):
    width = wq_ref.shape[1]
    for index, ref in enumerate((wq_ref, wk_ref, wv_ref)):
        columns = slice(index * width, (index + 1) * width)
        value = ref[...]
        own[:, columns] = value
        wide[:, columns] = value.astype(F32)
    rows, depth = wo_ref.shape
    for index, ref in enumerate((sq, sk, sv)):
        wo[rows:, index * width : (index + 1) * width] = ref[...].astype(F32)
    wo[rows:, 3 * width :] = jnp.zeros((wo.shape[0] - rows, depth - 3 * width), F32)
    for index in range(depth // width):
        wide[index * rows : (index + 1) * rows, 3 * width :] = wo_ref[
            :, index * width : (index + 1) * width
        ].astype(F32)
    wo[0:rows, :] = wo_ref[...].astype(F32)


def widen_heads(where, wq, wk, wv, wo, part, after):
    depth, width = wq.shape
    rows = pl.BlockSpec((part, width), lambda i, w: (w[3], 0))
    outs = [
        shape((depth, 3 * width), BF16),
        shape((depth, 4 * width), F32),
        shape((wo.shape[0] + part, depth), F32),
    ]
    inputs = (wq, wk, wv, wo)
    return launch(
        widen_heads_kernel, "widen_heads", where, (*inputs, wq, wk, wv),
        [whole_block(a) for a in inputs] + [rows] * 3, outs, [whole_block(o) for o in outs], (1,),
        12, after, streamed=range(7),
    )


def assemble_kernel(where_ref, own_ref, near_ref, *refs):
    *halves, out_ref = refs
    rows, depth = own_ref.shape
    half = depth // 2
    mine = where_ref[2] * 2 * rows
    other = (1 - where_ref[2]) * 2 * rows
    out_ref[pl.ds(pl.multiple_of(mine, rows), rows), :] = own_ref[...]
    out_ref[pl.ds(pl.multiple_of(mine + rows, rows), rows), :] = near_ref[...]
    for start, left, right in ((other, *halves[0:2]), (other + rows, *halves[2:4])):
        place = pl.ds(pl.multiple_of(start, rows), rows)
        out_ref[place, 0:half] = left[...].astype(BF16)
        out_ref[place, half:] = right[...].astype(BF16)


def assemble(where, own, near, far, both, after):
    rows, columns = own.shape
    out = shape((4 * rows, columns), BF16)
    inputs = (own, near, *far, *both)
    return launch(
        assemble_kernel, "assemble", where, inputs, [whole_block(a) for a in inputs], [out],
        [whole_block(out)], (1,), 14, after,
    )[0]


def narrow_near_kernel(where_ref, wide_ref, heads_ref, wo_ref):
    width = heads_ref.shape[1] // 3
    heads_ref[...] = wide_ref[:, 0 : 3 * width].astype(BF16)
    rows, depth = wo_ref.shape
    for index in range(depth // width):
        wo_ref[:, index * width : (index + 1) * width] = wide_ref[
            index * rows : (index + 1) * rows, 3 * width :
        ].astype(BF16)


def narrow_near(where, wide, wo, after):
    depth, columns = wide.shape
    outs = [shape((depth, 3 * columns // 4), BF16), shape(wo.shape, BF16)]
    return launch(
        narrow_near_kernel, "narrow_near", where, (wide,), [whole_block(wide)], outs,
        [whole_block(o) for o in outs], (1,), 14, after,
    )


def convert_kernel(where_ref, *refs):
    half = len(refs) // 2
    for source, target in zip(refs[:half], refs[half:]):
        target[...] = source[...].astype(target.dtype)


def convert(where, *values, dtype, after):
    specs = [rows_block(v.shape[0] // 4, v.shape[1]) for v in values]
    held = range(len(values))
    return launch(
        convert_kernel, "convert", where, values, specs, [shape(v.shape, dtype) for v in values],
        specs, (4,), 10, after, streamed=held if dtype == F32 else (), stored=held,
    )


def narrow_kernel(where_ref, wide_ref, left_ref, right_ref):
    width = left_ref.shape[1]
    left_ref[...] = wide_ref[:, 0:width].astype(BF16)
    right_ref[...] = wide_ref[:, width:].astype(BF16)


def narrow(where, wide, after):
    rows, width = wide.shape[0] // 4, wide.shape[1] // 2
    return launch(
        narrow_kernel, "narrow", where, (wide,), [rows_block(rows, 2 * width)],
        [shape((4 * rows, width), BF16)] * 2, [rows_block(rows, width)] * 2, (4,), 8, after,
        streamed=(0,),
    )


def project_group(x, weights):
    width = weights.shape[1] // 3
    q = (dot(x, weights[:, 0:width]).astype(BF16) * SCALE).astype(BF16)
    k = dot(x, weights[:, width : 2 * width]).astype(BF16)
    v = dot(x, weights[:, 2 * width : 3 * width]).astype(BF16)
    return q, k, v


def attend_kernel(
    where_ref, x_ref, own_ref, near_ref, col_ref, low_ref, qkv_ref, top_ref, *rest
):
    *o_refs, sums_ref = rest
    x = x_ref[0]
    length = x.shape[0]
    width = own_ref.shape[1] // 3
    owner, _ = lanes(width)
    mask_q, mask_k = mask_terms(col_ref[0][:, 0:1], width)
    zero = jnp.zeros((), BF16)
    sums_ref[...] = jnp.zeros_like(sums_ref)
    for group, weights in enumerate((own_ref, near_ref)):
        queries, keys, values = project_group(x, weights)
        for index, value in enumerate((queries, keys, values)):
            start = (3 * group + index) * width
            qkv_ref[0, :, start : start + width] = value
        total = jnp.zeros(queries.shape, F32)
        for head in range(GROUP):
            mine = owner == head
            scores = dot(
                pick(head, owner, queries, mask_q, zero), jnp.where(mine, keys, mask_k), 1, 1
            )
            top = jnp.max(scores, axis=-1, keepdims=True)
            raised = jnp.exp(scores - top)
            summed = jnp.sum(raised, axis=-1, keepdims=True)
            chances = raised * (1.0 / summed)
            total = total + dot(chances.astype(BF16), jnp.where(mine, values, zero))
            row = group * GROUP + head
            sums_ref[:, row : row + 1] = top + jnp.log(summed)
            top_ref[0, row : row + 1, :] = jnp.broadcast_to(
                jnp.max(top, axis=0, keepdims=True), (1, top_ref.shape[2])
            )
        low = total.astype(BF16)
        low_ref[0, :, group * width : (group + 1) * width] = low
        for index, o_ref in enumerate(o_refs):

            @pl.when(pl.program_id(0) == index)
            def _(o_ref=o_ref):
                o_ref[0:length, group * width : (group + 1) * width] = low.astype(F32)

    for index, o_ref in enumerate(o_refs):

        @pl.when(pl.program_id(0) == index)
        def _(o_ref=o_ref):
            o_ref[length:, :] = sums_ref[...].T[0:8, :]


def sequence(i, dims):
    return pl.BlockSpec((1, *dims), lambda g, w: (2 * w[1] + i, 0, 0))


def attend(where, x, own, near, seg_col, after):
    count, length, depth = x.shape
    both = 2 * own.shape[1] // 3
    outs = [
        shape((count // 2, length, both), BF16),
        shape((count // 2, length, 3 * both), BF16),
        shape((count // 2, both // HEAD_DIM, 128), F32),
    ]
    out_specs = [pl.BlockSpec((1, *o.shape[1:]), lambda i, w: (i, 0, 0)) for o in outs]
    outs += [shape((length + 8, both), F32)] * (count // 2)
    out_specs += [whole_block(o) for o in outs[3:]]
    return launch(
        attend_kernel, "attend", where, (x, own, near, seg_col),
        [
            pl.BlockSpec((1, length, depth), lambda i, w: (2 * w[1] + i, 0, 0)),
            RESIDENT,
            RESIDENT,
            pl.BlockSpec((1, length, 128), lambda i, w: (2 * w[1] + i, 0, 0)),
        ],
        outs, out_specs, (count // 2,), 20, after, streamed=(0, 3), stored=(0, 1),
        scratch=[pltpu.VMEM((length, 128), F32)],
    )


def project_kernel(where_ref, x_ref, far_ref, both_ref, out_ref):
    width = far_ref.shape[1] // 3
    for group, weights in enumerate((far_ref, both_ref)):
        for index, value in enumerate(project_group(x_ref[0], weights)):
            start = (3 * group + index) * width
            out_ref[0, :, start : start + width] = value


def project(where, x, far, both, after):
    count, length, depth = x.shape
    width = far.shape[1]
    return launch(
        project_kernel, "project", where, (x, far, both),
        [
            pl.BlockSpec((1, length, depth), lambda i, w: (2 * w[1] + i, 0, 0)),
            RESIDENT,
            RESIDENT,
        ],
        [shape((count // 2, length, 2 * width), BF16)],
        [pl.BlockSpec((1, length, 2 * width), lambda i, w: (i, 0, 0))],
        (count // 2,), 12, after, streamed=(0,), stored=(0,),
    )[0]


def fetch(sources, held_ref, arrived):
    first = pl.program_id(0) == 0
    copies = [
        pltpu.make_async_copy(source, held_ref.at[n], arrived.at[n])
        for n, source in enumerate(sources)
    ]

    @pl.when(first)
    def _():
        for copy in copies:
            copy.start()

    def get(n):
        @pl.when(first)
        def _():
            copies[n].wait()

        return held_ref[n]

    return get


def forward_kernel(
    where_ref, x_ref, mixed_ref, mixed_far_ref, wo_ref, gain_ref,
    shift_ref, up_own, up_near, down_own, down_near,
    normed_ref, scaled_ref, low_ref, active_ref, pull_ref, *rest,
):
    *part_refs, both_ref, held_ref, arrived = rest
    weight = fetch((up_own, down_own, up_near, down_near), held_ref, arrived)
    width = mixed_ref.shape[1]
    chip = where_ref[2]
    both_ref[:, pl.ds(pl.multiple_of(chip * width, width), width)] = mixed_ref[...].astype(BF16)
    both_ref[:, pl.ds(pl.multiple_of((1 - chip) * width, width), width)] = mixed_far_ref[
        ...
    ].astype(BF16)
    normed, scaled = normalize(x_ref[0].astype(F32) + dot(both_ref[...], wo_ref[...]))
    normed_ref[...] = normed
    scaled_ref[...] = jnp.broadcast_to(scaled, scaled_ref.shape)
    low = (normed * gain_ref[...] + shift_ref[...]).astype(BF16)
    low_ref[...] = low
    hidden = up_own.shape[1]
    parts = []
    for group in range(2):
        columns = slice(group * hidden, (group + 1) * hidden)
        before = dot(low, weight(2 * group))
        chance = 0.5 * (1.0 + lax.erf(before * ROOT_HALF))
        active = (before * chance).astype(BF16)
        active_ref[:, columns] = active
        pull_ref[:, columns] = chance + before * (jnp.exp(-0.5 * before * before) * BELL)
        parts.append(dot(active, weight(2 * group + 1)))
    total = parts[0] + parts[1]
    if len(part_refs) == 1:
        part_refs[0][...] = total
        return
    for index, ref in enumerate(part_refs):

        @pl.when(pl.program_id(0) == index)
        def _(ref=ref):
            ref[...] = total


def fetched(array):
    return [pltpu.VMEM((4, *array.shape), array.dtype), pltpu.SemaphoreType.DMA((4,))]


def forward(i, where, x, mixed, mixed_far, wo, gain, shift, ups, downs, after, halves):
    _, length, depth = x.shape
    width = mixed.shape[1]
    hidden = 2 * ups[0].shape[1]
    half = length // 2
    pieces = rows_block(half, width)
    outs = [
        shape((length, depth), F32),
        shape((length, 128), F32),
        shape((length, depth), BF16),
        shape((length, hidden), BF16),
        shape((length, hidden), F32),
    ]
    out_specs = [rows_block(half, o.shape[1]) for o in outs]
    if halves:
        outs += [shape((half, depth), F32)] * 2
        out_specs += [whole_block(o) for o in outs[5:]]
    else:
        outs.append(shape((length, depth), F32))
        out_specs.append(rows_block(half, depth))
    return launch(
        forward_kernel, "forward", where, (x, mixed, mixed_far, wo, gain, shift, *ups, *downs),
        [
            pl.BlockSpec((1, half, depth), lambda g, w: (2 * w[1] + i, g, 0)),
            pieces,
            pieces,
            RESIDENT,
            whole_block(gain),
            whole_block(shift),
            *[ANY] * 4,
        ],
        outs, out_specs, (2,), 30, after,
        streamed=(0, 6, 7, 8, 9), stored=(0, 1, 2, 3, 4),
        scratch=[pltpu.VMEM((half, 2 * width), BF16), *fetched(ups[0])],
    )


def backward_kernel(
    where_ref, normed_ref, gain_ref, shift_ref, grad_ref, second_gain_ref, second_shift_ref,
    pull_ref, up_own, up_near, down_own, down_near, *rest, halves,
):
    (
        final_ref, out_ref, slope_ref, slope_low_ref, before_ref, sums_ref, part_out_ref, held_ref,
        arrived,
    ) = rest[-9:]
    weight = fetch((down_own, up_own, down_near, up_near), held_ref, arrived)
    step = pl.program_id(0)
    hidden = normed_ref[...] * gain_ref[...] + shift_ref[...]
    if halves:
        first, second, far_first, far_second = rest[:4]
        total = jnp.where(step == 0, first[...] + far_first[...], second[...] + far_second[...])
    else:
        total = rest[0][...] + rest[1][...]
    normed, scaled = normalize(hidden + total)
    out = (normed * second_gain_ref[...] + second_shift_ref[...]).astype(BF16)
    final_ref[0] = out
    out_ref[...] = out.astype(F32)
    upstream = grad_ref[0].astype(F32)

    @pl.when(step == 0)
    def _():
        sums_ref[...] = jnp.zeros_like(sums_ref)

    sums_ref[0:1, :] += jnp.sum(upstream * normed, axis=0, keepdims=True)
    sums_ref[1:2, :] += jnp.sum(upstream, axis=0, keepdims=True)
    slope = norm_back(upstream, normed, scaled, second_gain_ref[...])
    slope_ref[...] = slope
    low = slope.astype(BF16)
    slope_low_ref[...] = low
    units = up_own.shape[1]
    parts = []
    for group in range(2):
        columns = slice(group * units, (group + 1) * units)
        before = (dot(low, weight(2 * group), 1, 1) * pull_ref[:, columns]).astype(BF16)
        before_ref[:, columns] = before
        parts.append(dot(before, weight(2 * group + 1), 1, 1))
    part_out_ref[...] = parts[0] + parts[1]


def backward(
    i, where, normed, gain, shift, part, part_far, out_grad, second_gain, second_shift, pull,
    ups, downs, final, after,
):
    count, length, depth = out_grad.shape
    hidden = 2 * ups[0].shape[1]
    half = length // 2
    outs = [
        shape((length, depth), F32),
        shape((length, depth), F32),
        shape((length, depth), BF16),
        shape((length, hidden), BF16),
        shape((8, depth), F32),
        shape((length, depth), F32),
    ]
    out_specs = [rows_block(half, o.shape[1]) for o in outs]
    out_specs[4] = whole_block(outs[4])
    block = pl.BlockSpec((1, half, depth), lambda g, w: (2 * w[1] + i, g, 0))
    vector = whole_block(gain)
    rows = rows_block(half, depth)
    carried = [] if final is None else [final]
    halves = len(part) == 2
    last = 11 + 2 * len(part)
    return launch(
        functools.partial(backward_kernel, halves=halves), "backward", where,
        (
            normed, gain, shift, out_grad, second_gain, second_shift, pull, *ups, *downs, *part,
            *part_far, *carried,
        ),
        [
            rows,
            vector,
            vector,
            block,
            vector,
            vector,
            rows_block(half, hidden),
            *[ANY] * 4,
            *[whole_block(a) if halves else rows for a in (*part, *part_far)],
            *[ANY] * len(carried),
        ],
        [shape((count, length, depth), BF16), *outs], [block, *out_specs], (2,), 34, after,
        streamed=(0, 3, *range(6, 11), *[last] * len(carried)), stored=(0, 1, 2, 3, 4),
        scratch=fetched(ups[0]), aliases={last + 1: 0} if carried else {},
    )


def products_kernel(where_ref, *refs):
    *terms, kept_ref, sent_ref = refs
    count = len(terms) // 2
    width = kept_ref.shape[1]
    for group, out_ref in enumerate((kept_ref, sent_ref)):
        columns = slice(group * width, (group + 1) * width)
        total = dot(terms[0][...], terms[count][:, columns], 0, 0)
        for left, right in zip(terms[1:count], terms[count + 1 :]):
            total = total + dot(left[...], right[:, columns], 0, 0)
        out_ref[...] = total


def products(where, lefts, rights, after):
    length, depth = lefts[0].shape
    width = rights[0].shape[1] // 2
    count = len(lefts)
    tile = depth // 4
    return launch(
        products_kernel, "products", where, (*lefts, *rights),
        [pl.BlockSpec((length, tile), lambda i, w: (0, i))] * count
        + [whole_block(r) for r in rights],
        [shape((depth, width), F32)] * 2, [rows_block(tile, width)] * 2, (4,), 18, after,
        streamed=range(2 * count), stored=(0, 1),
    )


def first_kernel(
    where_ref, part_ref, part_far_ref, slope_ref, normed_ref, scaled_ref, gain_ref,
    wo_ref, one_ref, low_ref, mixed_ref, mixed_far_ref, sums_ref,
):
    step = pl.program_id(0)
    upstream = slope_ref[...] + (part_ref[...] + part_far_ref[...])
    normed = normed_ref[...]

    @pl.when(step == 0)
    def _():
        sums_ref[...] = jnp.zeros_like(sums_ref)

    sums_ref[0:1, :] += jnp.sum(upstream * normed, axis=0, keepdims=True)
    sums_ref[1:2, :] += jnp.sum(upstream, axis=0, keepdims=True)
    slope = norm_back(upstream, normed, scaled_ref[:, 0:1], gain_ref[...])
    one_ref[...] = slope
    low = slope.astype(BF16)
    low_ref[...] = low
    width = mixed_ref.shape[1]
    for ref, chip in ((mixed_ref, where_ref[2]), (mixed_far_ref, 1 - where_ref[2])):
        weights = wo_ref[pl.ds(pl.multiple_of(chip * width, width), width), :]
        ref[...] = dot(low, weights, 1, 1).astype(BF16)


def first(where, part, part_far, slope, normed, scaled, gain, wo, after):
    length, depth = slope.shape
    both = wo.shape[0] // 2
    half = length // 2
    outs = [
        shape((length, depth), F32),
        shape((length, depth), BF16),
        shape((length, both), BF16),
        shape((length, both), BF16),
        shape((8, depth), F32),
    ]
    out_specs = [rows_block(half, o.shape[1]) for o in outs]
    out_specs[4] = whole_block(outs[4])
    rows = rows_block(half, depth)
    return launch(
        first_kernel, "first", where, (part, part_far, slope, normed, scaled, gain, wo),
        [rows, rows, rows, rows, rows_block(half, 128), whole_block(gain), RESIDENT],
        outs, out_specs, (2,), 18, after, streamed=(2, 3, 4), stored=(0, 1),
    )


def attend_back_kernel(where_ref, qkv_ref, go_ref, sums_ref, col_ref, own_ref, near_ref, *rest):
    *extra, out_ref, grads_ref, key_slope, value_slope = rest
    if extra:
        part_ref, one_ref, *_, final_ref = extra
    length = out_ref.shape[0]
    width = own_ref.shape[1] // 3
    owner, lane = lanes(width)
    mask_q, mask_k = mask_terms(col_ref[0][:, 0:1], width)
    zero = jnp.zeros((), BF16)
    term = lane - DOCS
    sums = split(sums_ref[...])
    for group, weights in enumerate((own_ref, near_ref)):
        start = 3 * group * width
        queries, keys, values = (
            qkv_ref[0, :, start + n * width : start + (n + 1) * width] for n in range(3)
        )
        upstream = go_ref[:, group * width : (group + 1) * width]
        row = lax.broadcasted_iota(jnp.int32, (8, 1), 0)
        spare_q = jnp.zeros(queries.shape, F32)
        for n, value in enumerate(sums):
            target = (row // GROUP == group) & ((row % GROUP + 1) % GROUP == owner) & (term == n)
            spare_q = spare_q + dot(value, jnp.where(target, -1.0, 0.0).astype(BF16), 0, 0)
        spare_q = spare_q.astype(BF16) + mask_q
        queries_t = queries.T
        upstream_t = upstream.T
        query_slope = jnp.zeros(queries.shape, F32)
        for head in range(GROUP):
            mine = owner == head
            place = slice(head * HEAD_DIM, (head + 1) * HEAD_DIM)
            chances = jnp.exp(
                dot(pick(head, owner, queries, spare_q, zero), jnp.where(mine, keys, mask_k), 1, 1)
            )
            drift = dot(jnp.where(mine, upstream, zero), values, 1, 1)
            slopes = chances * (drift - jnp.sum(drift * chances, axis=-1, keepdims=True))
            slopes = slopes.astype(BF16)
            query_slope = query_slope + dot(slopes, jnp.where(mine, keys, zero))
            key_slope[place, :] = dot(queries_t[place, :], slopes)
            value_slope[place, :] = dot(upstream_t[place, :], chances.astype(BF16))
        grads_ref[:, start : start + width] = (query_slope * SCALE).astype(BF16)
        grads_ref[:, start + width : start + 2 * width] = key_slope[...].T.astype(BF16)
        grads_ref[:, start + 2 * width : start + 3 * width] = value_slope[...].T.astype(BF16)
        part = dot(grads_ref[:, start : start + 3 * width], weights[...], 1, 1)
        if group == 0:
            out_ref[...] = part
        else:
            out_ref[...] += part
    if extra:
        final = (one_ref[...] + (part_ref[...] + out_ref[...])).astype(BF16)
        final_ref[0] = final
        out_ref[...] = final.astype(F32)


def attend_back(
    i, where, qkv, index, go, mixed, seg_col, own, near, after, extra=(), final=None, count=0
):
    _, length, columns = qkv.shape
    depth, width = own.shape
    out = shape((length, depth), F32)
    grads = shape((length, columns), BF16)
    outs = [out, grads]
    out_specs = [whole_block(o) for o in outs]
    carried = [] if final is None else [final]
    if extra:
        outs = [shape((count, length, depth), BF16), out]
        out_specs = [sequence(i, (length, depth)), whole_block(out)]
    scratch = [pltpu.VMEM((width // 3, length), F32)] * 2
    if extra:
        scratch = [pltpu.VMEM((length, columns), BF16), *scratch]
    return launch(
        attend_back_kernel, "attend_back", where,
        (qkv, go, mixed, seg_col, own, near, *extra, *carried),
        [
            pl.BlockSpec((1, length, columns), lambda g, w: (index, 0, 0)),
            whole_block(go),
            pl.BlockSpec((8, columns // 3), lambda g, w: (length // 8, 0)),
            sequence(i, (length, 128)),
            RESIDENT,
            RESIDENT,
            *[whole_block(e) for e in extra],
            *[ANY] * len(carried),
        ],
        outs, out_specs, (1,), 22, after, scratch=scratch,
        streamed=(0, 3, *range(8, 8 + len(carried))), stored=(0, 1) if extra else (1,),
        aliases={9: 0} if carried else {},
    )


def head_products_kernel(where_ref, *refs, count):
    def take():
        nonlocal refs
        taken, refs = refs[:count], refs[count:]
        return taken

    x_refs, one_refs, grad_refs, mixed_refs, first_refs, second_refs = (take() for _ in range(6))
    tile = x_refs[0].shape[2]
    width = mixed_refs[0].shape[2] // 2
    heads = dot(x_refs[0][0], grad_refs[0][...], 0, 0)
    mixed = dot(one_refs[0][...], mixed_refs[0][0], 0, 0)
    for n in range(1, count):
        heads = heads + dot(x_refs[n][0], grad_refs[n][...], 0, 0)
        mixed = mixed + dot(one_refs[n][...], mixed_refs[n][0], 0, 0)
    for group, (left, right) in enumerate((refs[0:2], refs[2:4])):
        start = 3 * group * width
        left[0, 0:tile, :] = heads[:, start : start + width]
        left[0, tile:, :] = heads[:, start + width : start + 2 * width]
        right[0, 0:tile, :] = heads[:, start + 2 * width : start + 3 * width]
        right[0, tile : 2 * tile, :] = mixed[:, group * width : (group + 1) * width]
        right[0, 2 * tile :, :] = jnp.zeros((8, width), F32)
        for row, sums in ((0, first_refs), (2, second_refs)):
            total = sums[0][0:2, :]
            for ref in sums[1:]:
                total = total + ref[0:2, :]
            right[0, 2 * tile + row : 2 * tile + row + 2, 0:tile] = total


def head_products(where, x, ones, grads, mixed, firsts, seconds, after):
    _, length, depth = x.shape
    count = len(ones)
    width = mixed.shape[2] // 2
    tile = 128
    outs = [shape((depth // tile, 2 * tile + rows, width), F32) for rows in (0, 8)] * 2
    return launch(
        functools.partial(head_products_kernel, count=count), "head_products", where,
        (*[x] * count, *ones, *grads, *[mixed] * count, *firsts, *seconds),
        [
            pl.BlockSpec((1, length, tile), lambda b, w, i=i: (2 * w[1] + i, 0, b))
            for i in range(count)
        ]
        + [pl.BlockSpec((length, tile), lambda b, w: (0, b))] * count
        + [whole_block(a) for a in grads]
        + [pl.BlockSpec((1, *mixed.shape[1:]), lambda b, w, i=i: (i, 0, 0)) for i in range(count)]
        + [pl.BlockSpec((8, tile), lambda b, w: (0, b))] * (2 * count),
        outs, [pl.BlockSpec((1, *o.shape[1:]), lambda b, w: (b, 0, 0)) for o in outs],
        (depth // tile,), 14, after, streamed=range(4 * count), stored=range(4),
    )


def ring_kernel(where_ref, *refs, arrivals, blocks, passed):
    outs = refs[len(refs) - 2 - passed :]
    for way in range(2):
        total = None
        for ref in refs[way : arrivals + blocks : 2]:
            value = ref[0] if len(ref.shape) == 3 else ref[...]
            total = value if total is None else total + value
        if total is not None:
            outs[way][...] = total
    for way in range(passed):
        outs[len(outs) - passed + way][...] = refs[arrivals + blocks + way][0]


def ring_step(owners, n, arrived, blocks, following, after):
    def block(array, way, step):
        return pl.BlockSpec((1, *array.shape[1:]), lambda i, w: (w[2 * step + way], 0, 0))

    specs = [whole_block(a) for a in arrived]
    specs += [block(array, i % 2, n) for i, array in enumerate(blocks)]
    specs += [block(array, i % 2, n + 1) for i, array in enumerate(following)]
    inputs = (*arrived, *blocks, *following)
    outs = [shape(array.shape[1:], F32) for array in (*blocks, *following)[0:2]]
    outs += [shape(array.shape[1:], F32) for array in following]
    return launch(
        functools.partial(
            ring_kernel, arrivals=len(arrived), blocks=len(blocks), passed=len(following)
        ),
        "ring_step", owners, inputs, specs, outs, [whole_block(o) for o in outs],
        (1,), 8, after, streamed=range(len(arrived), len(inputs)),
    )


def finish_kernel(where_ref, value_ref, final_ref, out_ref):
    del final_ref
    out_ref[0] = value_ref[0].astype(BF16)


def finish(i, where, values, final, after):
    _, length, depth = values.shape
    half = length // 2
    return launch(
        finish_kernel, "finish", where, (values, final),
        [pl.BlockSpec((1, half, depth), lambda g, w: (1 - w[1], g, 0)), ANY],
        [shape(final.shape, BF16)],
        [pl.BlockSpec((1, half, depth), lambda g, w: (2 * (1 - w[1]) + i, g, 0))],
        (2,), 8, after, aliases={2: 0}, stored=(0,), streamed=(0, 1),
    )[0]


def solution(mesh):
    ranks = mesh.shape["dp"]
    group = mesh.shape["tensor"]
    assert group == 4 and ranks % 8 == 0
    near_pairs = [(t, t ^ 1) for t in range(group)]
    far_pairs = [(t, t ^ 2) for t in range(group)]
    turns = (
        [(RING[p], RING[(p + 1) % 8]) for p in range(8)],
        [(RING[p], RING[(p - 1) % 8]) for p in range(8)],
    )

    def near(value):
        return lax.ppermute(value, "tensor", near_pairs)

    cores = [[0, 1], [2, 3]]

    def both_cores(value):
        return lax.all_gather(value, "tensor", axis=0, axis_index_groups=cores)

    def scatter(value):
        return lax.psum_scatter(value, "dp", scatter_dimension=0, tiled=True)

    def far(value):
        return lax.ppermute(value, "tensor", far_pairs)

    def body(
        block_input, segment_ids, query_weight, key_weight, value_weight, output_weight,
        first_gain, first_shift, up_weight, down_weight, second_gain, second_shift, out_grad,
    ):
        count, length, depth = block_input.shape
        width = query_weight.shape[1]
        part = depth // ranks
        mine = range(count // 2)
        me = lax.axis_index("tensor")
        rank = lax.axis_index("dp")
        where = jnp.stack([me, me % 2, me // 2, rank]).astype(jnp.int32)
        seg_col = jnp.broadcast_to(segment_ids[:, :, None], (count, length, 128))
        gain_one, shift_one = first_gain[None], first_shift[None]
        gain_two, shift_two = second_gain[None], second_shift[None]
        order = Order()

        def then(call, *args, **kwargs):
            return call(*args, after=order, **kwargs)

        own_low, own_wide, wo_wide = then(
            widen_heads, where, query_weight, key_weight, value_weight, output_weight, part
        )
        near_wide, wo_far = near(own_wide), far(wo_wide)
        near_low, wo_near = then(narrow_near, where, near_wide, output_weight)
        wide = then(convert, where, up_weight, down_weight, dtype=F32)
        wide_near = [near(w) for w in wide]
        mixed_low, qkv, tops, *mixed = then(
            attend, where, block_input, own_low, near_low, seg_col
        )
        mixed_far = [far(m) for m in mixed]
        *wo_far, slices = then(parts, where, wo_far, output_weight.shape[0], 3 * width)
        wo_both = [near(w) for w in wo_far]
        others = lax.all_gather(
            jnp.concatenate([slices, near(slices)], axis=1), "dp", axis=0, tiled=True
        )
        up_near, down_near = then(convert, where, *wide_near, dtype=BF16)
        ups, downs = (up_weight, up_near), (down_weight, down_near)
        wo = then(assemble, where, output_weight, wo_near, wo_far, wo_both)

        forwards, part_far = [], []
        for i in mine:
            forwards.append(
                then(
                    forward, i, where, block_input, mixed[i], mixed_far[i], wo, gain_one,
                    shift_one, ups, downs, halves=i == 0,
                )
            )
            part_far.append([far(p) for p in forwards[i][5:]])

        heads_own = width // HEAD_DIM
        peak = jnp.max(tops, axis=0)
        peak = jnp.maximum(peak[:heads_own], near(peak)[heads_own:])
        step = 1
        while step < ranks:
            peak = jnp.maximum(peak, lax.ppermute(peak, "dp", [(i, i ^ step) for i in range(ranks)]))
            step *= 2
        (peak,) = then(gate, where, peak)

        written = {"layer_out": None, "input_grad": None}
        backs, slope_far = [], []
        for i in mine:
            normed, scaled, low, active, pull, *part_sum = forwards[i]
            backs.append(
                then(
                    backward, i, where, normed, gain_one, shift_one, part_sum, part_far[i],
                    out_grad, gain_two, shift_two, pull, ups, downs, written["layer_out"],
                )
            )
            written["layer_out"], *backs[i] = backs[i]
            slope_far.append(far(backs[i][5]))
            if i == 0:
                far_low, both_low = then(narrow, where, others)
                qkv_far = then(project, where, block_input, far_low, both_low)

        lows, actives = [f[2] for f in forwards], [f[3] for f in forwards]
        slope_lows, befores = [b[2] for b in backs], [b[3] for b in backs]
        up_kept, up_sent = then(products, where, lows, befores)
        down_kept, down_sent = then(products, where, slope_lows, actives)

        def ring_of(blocks, following=(), nears=()):
            held = then(ring_step, owners, 0, nears, blocks, following)
            for n in range(1, 8):
                arrived = [lax.ppermute(h, "dp", t) for h, t in zip(held, turns)]
                arrived += [near(h) for h in held[2:]]
                yield None
                held = then(
                    ring_step, owners, n, arrived, blocks, following if n < 7 else ()
                )
            yield held

        if ranks == 8:
            owners = lax.dynamic_index_in_dim(jnp.asarray(OWNERS, jnp.int32), rank, 0, False)
            following, blocks = [
                [a.reshape(8, part, a.shape[1]) for a in pair]
                for pair in ((up_sent, down_sent), (up_kept, down_kept))
            ]
            passed = then(ring_step, owners, -1, (), (), following)
            ring = ring_of(blocks, following, [near(p) for p in passed[2:]])
            next(ring)
        else:
            ring = iter(())
            up_grad = scatter(up_kept + near(up_sent))
            down_grad = scatter(down_kept + near(down_sent))

        def write(which, i, value):
            written[which] = then(finish, i, where, value, written[which])

        def first_back(i):
            return then(
                first, where, backs[i][5], slope_far[i], backs[i][1], *forwards[i][:2], gain_one,
                wo,
            )

        def own_back(i, go):
            return then(
                attend_back, i, where, qkv, i, go, mixed[i], seg_col, own_low, near_low,
            )

        def far_back(i, go_far, own_part, one):
            written["input_grad"], result = then(
                attend_back, i, where, qkv_far, i, go_far, mixed_far[i], seg_col, far_low,
                both_low, extra=(own_part, one), final=written["input_grad"], count=count,
            )
            return both_cores(result)

        firsts, owns = [], []
        firsts.append(first_back(0))
        next(ring, None)
        owns.append(own_back(0, firsts[0][2]))
        next(ring, None)
        inputs = [far_back(0, firsts[0][3], owns[0][0], firsts[0][0])]
        next(ring, None)
        firsts.append(first_back(1))
        layers = [both_cores(v) for v in then(gate, where, *[b[0] for b in backs])]
        owns.append(own_back(1, firsts[1][2]))
        next(ring, None)
        left, right, *sent = then(
            head_products, where, block_input, [f[1] for f in firsts], [o[1] for o in owns],
            mixed_low, [f[4] for f in firsts], [b[4] for b in backs],
        )
        sent = [near(a) for a in sent]
        if ranks == 8:
            *_, (up_grad, down_grad) = ring
            ring = ring_of((left, right, *sent))
            next(ring)
        write("layer_out", 0, layers[0])
        next(ring, None)
        write("layer_out", 1, layers[1])
        next(ring, None)
        inputs.append(far_back(1, firsts[1][3], owns[1][0], firsts[1][0]))
        next(ring, None)
        write("input_grad", 0, inputs[0])
        next(ring, None)
        next(ring, None)
        write("input_grad", 1, inputs[1])

        tile = 128
        if ranks == 8:
            *_, (left, right) = ring
            query_grad, key_grad = left[:tile], left[tile:]
            value_grad, output_grad = right[:tile], right[tile : 2 * tile].T
            gains = right[2 * tile : 2 * tile + 4, :tile]
        else:
            left, right = left + sent[0], right + sent[1]

            def rows_of(value, n):
                return scatter(value[:, n * tile : (n + 1) * tile].reshape(depth, width))

            query_grad, key_grad, value_grad = rows_of(left, 0), rows_of(left, 1), rows_of(right, 0)
            output_grad = rows_of(right, 1).T
            gains = right[:, 2 * tile : 2 * tile + 4, :tile].transpose(0, 2, 1)
            gains = scatter(gains.reshape(depth, 4)).T

        factor = jnp.sqrt(CLIP / jnp.maximum(peak[:, 0], CLIP))
        column_factor = jnp.repeat(factor, HEAD_DIM)
        query_clipped = query_weight.astype(F32) * column_factor[None, :]
        key_clipped = key_weight.astype(F32) * column_factor[None, :]
        return (
            written["layer_out"], written["input_grad"], query_grad, key_grad, value_grad, output_grad,
            gains[0], gains[1], up_grad, down_grad.T, gains[2], gains[3],
            query_clipped, key_clipped,
        )

    batch = P("dp", None, None)
    in_specs = (
        batch, P("dp", None), P(None, "tensor"), P(None, "tensor"), P(None, "tensor"),
        P("tensor", None), P(), P(), P(None, "tensor"), P("tensor", None), P(), P(), batch,
    )
    out_specs = (
        batch, batch, P("dp", "tensor"), P("dp", "tensor"), P("dp", "tensor"), P("tensor", "dp"),
        P("dp"), P("dp"), P("dp", "tensor"), P("tensor", "dp"), P("dp"), P("dp"),
        P(None, "tensor"), P(None, "tensor"),
    )
    return jax.shard_map(body, mesh=mesh, in_specs=in_specs, out_specs=out_specs, check_vma=False)
```

```python
import functools

import jax
import jax.numpy as jnp
from jax import lax
from jax.experimental import pallas as pl
from jax.experimental.pallas import tpu as pltpu
from jax.sharding import PartitionSpec as P

F32 = jnp.float32
BF16 = jnp.bfloat16
HEAD_DIM = 64
FAR = -1e30
EPS = 1e-06
CLIP = 10.0
SCALE = HEAD_DIM**-0.5
ROOT_HALF = 0.5**0.5
BELL = 0.3989422804014327
GROUP = 4
BLOCK = 128
DOCS = 4
MIB = 1 << 20
RING = (0, 2, 4, 6, 7, 5, 3, 1)
OWNERS = tuple(
    tuple(RING[(RING.index(r) + way * (1 + n)) % 8] for n in range(8) for way in (-1, 1))
    for r in range(8)
)
ANY = pl.BlockSpec(memory_space=pl.ANY)
RESIDENT = pl.BlockSpec(memory_space=pltpu.VMEM)


def dot(left, right, left_dim=1, right_dim=0):
    return lax.dot_general(
        left, right, (((left_dim,), (right_dim,)), ((), ())), preferred_element_type=F32
    )


def normalize(total):
    average = jnp.mean(total, axis=-1, keepdims=True)
    centred = total - average
    variance = jnp.mean(centred * centred, axis=-1, keepdims=True)
    scaled = lax.rsqrt(variance + EPS)
    return centred * scaled, scaled


def norm_back(upstream, normed, scaled, gain):
    weighted = upstream * gain
    first = jnp.mean(weighted, axis=-1, keepdims=True)
    second = jnp.mean(weighted * normed, axis=-1, keepdims=True)
    return scaled * (weighted - first - normed * second)


def lanes(width):
    lane = lax.broadcasted_iota(jnp.int32, (1, width), 1)
    return lane // HEAD_DIM, lane % HEAD_DIM


def split(value):
    high = value.astype(BF16)
    rest = value - high.astype(F32)
    middle = rest.astype(BF16)
    return high, middle, (rest - middle.astype(F32)).astype(BF16)


def pick(head, owner, own, spare, zero):
    return jnp.where(owner == head, own, jnp.where(owner == (head + 1) % GROUP, spare, zero))


def spare_columns(seg_rows, sums, group, width):
    owner, lane = lanes(width)
    row8 = lax.broadcasted_iota(jnp.int32, (8, 1), 0)
    equal = jnp.where(seg_rows == row8, 1.0, 0.0)
    rows = [equal]
    wanted = [jnp.where(lane == row8, FAR, 0.0)]
    if sums is not None:
        head = row8 % GROUP
        here = (row8 // GROUP == group) & ((head + 1) % GROUP == owner)
        for n, value in enumerate(split(sums)):
            rows.append(value.astype(F32))
            wanted.append(jnp.where(here & (lane == DOCS + n), -1.0, 0.0))
    placed = jnp.concatenate(wanted, axis=0).astype(BF16)
    queries = dot(jnp.concatenate(rows, axis=0).astype(BF16), placed, 0, 0).astype(BF16)
    ones = jnp.where((lane >= DOCS) & (lane < DOCS + 3), 1.0, 0.0)
    placed = jnp.where((lane == row8) & (row8 < DOCS), 1.0, 0.0).astype(BF16)
    differ = jnp.where(seg_rows == row8, 0.0, 1.0).astype(BF16)
    keys = (dot(differ, placed, 0, 0) + ones).astype(BF16)
    return queries, keys


def shape(dims, dtype):
    return jax.ShapeDtypeStruct(tuple(dims), dtype)


def whole_block(array):
    zeros = (0,) * len(array.shape)
    return pl.BlockSpec(tuple(array.shape), lambda i, w: zeros)


def rows_block(rows, columns):
    return pl.BlockSpec((rows, columns), lambda i, w: (i, 0))


class Order:
    def __init__(self):
        self.token, self.stored = None, False

    def taken(self):
        if self.token is None:
            return []
        if self.stored:
            return [pltpu.with_memory_space_constraint(self.token, pltpu.HBM)]
        return [self.token]

    def give(self, results, stored):
        sizes = [r.size * r.dtype.itemsize for r in results]
        index = sizes.index(min(sizes))
        self.token, self.stored = results[index], index in stored


def launch(
    kernel, name, where, inputs, in_specs, outs, out_specs, grid, vmem, after,
    scratch=(), aliases=None, streamed=(), stored=(),
):
    count = len(inputs)
    tokens = after.taken()
    inputs = [
        pltpu.with_memory_space_constraint(value, pltpu.HBM) if i in streamed else value
        for i, value in enumerate(inputs)
    ]
    outs = [
        pltpu.HBM(value.shape, value.dtype) if i in stored else value
        for i, value in enumerate(outs)
    ]

    def run(where_ref, *refs):
        kernel(where_ref, *refs[:count], *refs[count + len(tokens) :])

    results = pl.pallas_call(
        run,
        grid_spec=pltpu.PrefetchScalarGridSpec(
            num_scalar_prefetch=1,
            grid=grid,
            in_specs=list(in_specs) + [ANY] * len(tokens),
            out_specs=list(out_specs),
            scratch_shapes=list(scratch),
        ),
        out_shape=outs,
        input_output_aliases=aliases or {},
        compiler_params=pltpu.CompilerParams(
            vmem_limit_bytes=vmem * MIB, dimension_semantics=("arbitrary",) * len(grid)
        ),
        cost_estimate=pl.CostEstimate(flops=1, bytes_accessed=1, transcendentals=0),
        name=name,
    )(where, *inputs, *tokens)
    after.give(results, stored)
    return results


def gate_kernel(*refs):
    del refs


def gate(where, *values, after):
    outs = [shape(v.shape, v.dtype) for v in values]
    return launch(
        gate_kernel, "gate", where, values, [ANY] * len(values), outs, [ANY] * len(values), (1,),
        2, after, aliases={i + 1: i for i in range(len(values))},
    )


def widen_heads_kernel(where_ref, wq_ref, wk_ref, wv_ref, wo_ref, own, wide, wo):
    width = wq_ref.shape[1]
    for index, ref in enumerate((wq_ref, wk_ref, wv_ref)):
        columns = slice(index * width, (index + 1) * width)
        value = ref[...]
        own[:, columns] = value
        wide[:, columns] = value.astype(F32)
    rows, depth = wo_ref.shape
    for index in range(depth // width):
        wide[index * rows : (index + 1) * rows, 3 * width :] = wo_ref[
            :, index * width : (index + 1) * width
        ].astype(F32)
    half = rows // 2
    wo[...] = wo_ref[pl.ds(pl.multiple_of((where_ref[3] % 2) * half, half), half), :].astype(F32)


def widen_heads(where, wq, wk, wv, wo, after):
    depth, width = wq.shape
    outs = [
        shape((depth, 3 * width), BF16),
        shape((depth, 4 * width), F32),
        shape((wo.shape[0] // 2, depth), F32),
    ]
    inputs = (wq, wk, wv, wo)
    return launch(
        widen_heads_kernel, "widen_heads", where, inputs, [whole_block(a) for a in inputs], outs,
        [whole_block(o) for o in outs], (1,), 12, after, streamed=range(4),
    )


def assemble_kernel(where_ref, own_ref, near_ref, *refs):
    *halves, out_ref = refs
    rows = own_ref.shape[0]
    half = rows // 2
    mine = where_ref[2] * 2 * rows
    other = (1 - where_ref[2]) * 2 * rows
    out_ref[pl.ds(pl.multiple_of(mine, rows), rows), :] = own_ref[...]
    out_ref[pl.ds(pl.multiple_of(mine + rows, rows), rows), :] = near_ref[...]
    parity = where_ref[3] % 2
    for start, first, second in ((other, *halves[0:2]), (other + rows, *halves[2:4])):
        for ref, place in ((first, parity), (second, 1 - parity)):
            begin = pl.multiple_of(start + place * half, half)
            out_ref[pl.ds(begin, half), :] = ref[...].astype(BF16)


def assemble(where, own, near, far, both, after):
    rows, columns = own.shape
    out = shape((4 * rows, columns), BF16)
    inputs = (own, near, *far, *both)
    return launch(
        assemble_kernel, "assemble", where, inputs, [whole_block(a) for a in inputs], [out],
        [whole_block(out)], (1,), 14, after,
    )[0]


def narrow_near_kernel(where_ref, own_ref, wide_ref, heads_ref, wo_ref):
    width = own_ref.shape[1] // 3
    heads_ref[0] = own_ref[...]
    heads_ref[1] = wide_ref[:, 0 : 3 * width].astype(BF16)
    rows, depth = wo_ref.shape
    for index in range(depth // width):
        wo_ref[:, index * width : (index + 1) * width] = wide_ref[
            index * rows : (index + 1) * rows, 3 * width :
        ].astype(BF16)


def narrow_near(where, own, wide, wo, after):
    outs = [shape((2, *own.shape), BF16), shape(wo.shape, BF16)]
    return launch(
        narrow_near_kernel, "narrow_near", where, (own, wide),
        [whole_block(own), whole_block(wide)], outs, [whole_block(o) for o in outs], (1,), 16,
        after,
    )


def convert_kernel(where_ref, *refs):
    half = len(refs) // 2
    for source, target in zip(refs[:half], refs[half:]):
        target[...] = source[...].astype(target.dtype)


def convert(where, *values, dtype, after):
    specs = [rows_block(v.shape[0] // 4, v.shape[1]) for v in values]
    held = range(len(values))
    return launch(
        convert_kernel, "convert", where, values, specs, [shape(v.shape, dtype) for v in values],
        specs, (4,), 10, after, streamed=held if dtype == F32 else (), stored=held,
    )


def project_group(x, weights):
    width = weights.shape[1] // 3
    q = (dot(x, weights[:, 0:width]).astype(BF16) * SCALE).astype(BF16)
    k = dot(x, weights[:, width : 2 * width]).astype(BF16)
    v = dot(x, weights[:, 2 * width : 3 * width]).astype(BF16)
    return q, k, v


def attend_kernel(
    where_ref, x_ref, weights_ref, seg_ref, low_ref, qkv_ref, top_ref, o_ref, held_ref
):
    x = x_ref[0]
    width = weights_ref.shape[2] // 3
    owner, _ = lanes(width)
    spare_q, spare_k = spare_columns(seg_ref[0], None, 0, width)
    zero = jnp.zeros((), BF16)
    held_ref[...] = jnp.zeros_like(held_ref)
    groups = [project_group(x, weights_ref.at[group]) for group in range(2)]
    for group, values in enumerate(groups):
        for index, value in enumerate(values):
            start = (3 * group + index) * width
            qkv_ref[0, :, start : start + width] = value

    def scores_of(group, head):
        queries, keys, _ = groups[group]
        return dot(
            pick(head, owner, queries, spare_q, zero),
            jnp.where(owner == head, keys, spare_k), 1, 1,
        )

    for group in range(2):
        total = jnp.zeros(groups[group][0].shape, F32)
        for head in range(GROUP):
            row = group * GROUP + head
            scores = scores_of(group, head)
            top = jnp.max(scores, axis=-1, keepdims=True)
            raised = jnp.exp(scores - top)
            summed = jnp.sum(raised, axis=-1, keepdims=True)
            chances = raised * (1.0 / summed)
            total = total + dot(
                chances.astype(BF16), jnp.where(owner == head, groups[group][2], zero)
            )
            held_ref[:, row : row + 1] = top + jnp.log(summed)
            top_ref[row : row + 1, :] = jnp.broadcast_to(
                jnp.max(top, axis=0, keepdims=True), (1, top_ref.shape[1])
            )
        low = total.astype(BF16)
        low_ref[0, :, group * width : (group + 1) * width] = low
        o_ref[0 : x.shape[0], group * width : (group + 1) * width] = low.astype(F32)
    o_ref[x.shape[0] :, :] = held_ref[...].T[0:8, :]


def sequence(i, dims):
    return pl.BlockSpec((1, *dims), lambda g, w: (2 * w[1] + i, 0, 0))


def attend(i, where, x, weights, seg, after):
    _, length, depth = x.shape
    columns = weights.shape[2]
    width = columns // 3
    outs = [
        shape((1, length, 2 * width), BF16),
        shape((1, length, 2 * columns), BF16),
        shape((2 * GROUP, 128), F32),
        shape((length + 2 * GROUP, 2 * width), F32),
    ]
    out_specs = [whole_block(o) for o in outs]
    return launch(
        attend_kernel, "attend", where, (x, weights, seg),
        [sequence(i, (length, depth)), RESIDENT, sequence(i, (8, length))],
        outs, out_specs, (1,), 20, after, streamed=(0,), stored=(0, 1),
        scratch=[pltpu.VMEM((length, 128), F32)],
    )


def fetch(sources, held_ref, arrived):
    first = pl.program_id(0) == 0
    copies = [
        pltpu.make_async_copy(source, held_ref.at[n], arrived.at[n])
        for n, source in enumerate(sources)
    ]

    @pl.when(first)
    def _():
        for copy in copies:
            copy.start()

    def get(n):
        @pl.when(first)
        def _():
            copies[n].wait()

        return held_ref[n]

    return get


def forward_kernel(
    where_ref, x_ref, mixed_ref, mixed_far_ref, wo_ref, gain_ref,
    shift_ref, up_own, up_near, down_own, down_near,
    normed_ref, scaled_ref, low_ref, active_ref, pull_ref, part_ref, both_ref, held_ref, arrived,
):
    weight = fetch((up_own, down_own, up_near, down_near), held_ref, arrived)
    width = mixed_ref.shape[1]
    chip = where_ref[2]
    both_ref[:, pl.ds(pl.multiple_of(chip * width, width), width)] = mixed_ref[...].astype(BF16)
    both_ref[:, pl.ds(pl.multiple_of((1 - chip) * width, width), width)] = mixed_far_ref[
        ...
    ].astype(BF16)
    normed, scaled = normalize(x_ref[0].astype(F32) + dot(both_ref[...], wo_ref[...]))
    normed_ref[...] = normed
    scaled_ref[...] = jnp.broadcast_to(scaled, scaled_ref.shape)
    low = (normed * gain_ref[...] + shift_ref[...]).astype(BF16)
    low_ref[...] = low
    hidden = up_own.shape[1]
    parts = []
    for group in range(2):
        columns = slice(group * hidden, (group + 1) * hidden)
        before = dot(low, weight(2 * group))
        chance = 0.5 * (1.0 + lax.erf(before * ROOT_HALF))
        active = (before * chance).astype(BF16)
        active_ref[:, columns] = active
        pull_ref[:, columns] = chance + before * (jnp.exp(-0.5 * before * before) * BELL)
        parts.append(dot(active, weight(2 * group + 1)))
    part_ref[...] = parts[0] + parts[1]


def fetched(array):
    return [pltpu.VMEM((4, *array.shape), array.dtype), pltpu.SemaphoreType.DMA((4,))]


def forward(i, where, x, mixed, mixed_far, wo, gain, shift, ups, downs, after):
    _, length, depth = x.shape
    width = mixed.shape[1]
    hidden = 2 * ups[0].shape[1]
    half = length // 2
    pieces = rows_block(half, width)
    outs = [
        shape((length, depth), F32),
        shape((length, 128), F32),
        shape((length, depth), BF16),
        shape((length, hidden), BF16),
        shape((length, hidden), F32),
    ]
    out_specs = [rows_block(half, o.shape[1]) for o in outs]
    outs.append(shape((length, depth), F32))
    out_specs.append(rows_block(half, depth))
    return launch(
        forward_kernel, "forward", where, (x, mixed, mixed_far, wo, gain, shift, *ups, *downs),
        [
            pl.BlockSpec((1, half, depth), lambda g, w: (2 * w[1] + i, g, 0)),
            pieces,
            pieces,
            RESIDENT,
            whole_block(gain),
            whole_block(shift),
            *[ANY] * 4,
        ],
        outs, out_specs, (2,), 30, after,
        streamed=(0, 6, 7, 8, 9), stored=(0, 1, 2, 3, 4),
        scratch=[pltpu.VMEM((half, 2 * width), BF16), *fetched(ups[0])],
    )


def backward_kernel(
    where_ref, normed_ref, gain_ref, shift_ref, grad_ref, second_gain_ref, second_shift_ref,
    pull_ref, up_own, up_near, down_own, down_near, part_ref, part_far_ref, *rest,
):
    (
        final_ref, out_ref, slope_ref, slope_low_ref, before_ref, sums_ref, part_out_ref, held_ref,
        arrived,
    ) = rest[-9:]
    weight = fetch((down_own, up_own, down_near, up_near), held_ref, arrived)
    step = pl.program_id(0)
    hidden = normed_ref[...] * gain_ref[...] + shift_ref[...]
    normed, scaled = normalize(hidden + (part_ref[...] + part_far_ref[...]))
    out = (normed * second_gain_ref[...] + second_shift_ref[...]).astype(BF16)
    final_ref[0] = out
    out_ref[...] = out.astype(F32)
    upstream = grad_ref[0].astype(F32)

    @pl.when(step == 0)
    def _():
        sums_ref[...] = jnp.zeros_like(sums_ref)

    sums_ref[0:1, :] += jnp.sum(upstream * normed, axis=0, keepdims=True)
    sums_ref[1:2, :] += jnp.sum(upstream, axis=0, keepdims=True)
    slope = norm_back(upstream, normed, scaled, second_gain_ref[...])
    slope_ref[...] = slope
    low = slope.astype(BF16)
    slope_low_ref[...] = low
    units = up_own.shape[1]
    parts = []
    for group in range(2):
        columns = slice(group * units, (group + 1) * units)
        before = (dot(low, weight(2 * group), 1, 1) * pull_ref[:, columns]).astype(BF16)
        before_ref[:, columns] = before
        parts.append(dot(before, weight(2 * group + 1), 1, 1))
    part_out_ref[...] = parts[0] + parts[1]


def backward(
    i, where, normed, gain, shift, part, part_far, out_grad, second_gain, second_shift, pull,
    ups, downs, final, after,
):
    count, length, depth = out_grad.shape
    hidden = 2 * ups[0].shape[1]
    half = length // 2
    outs = [
        shape((length, depth), F32),
        shape((length, depth), F32),
        shape((length, depth), BF16),
        shape((length, hidden), BF16),
        shape((8, depth), F32),
        shape((length, depth), F32),
    ]
    out_specs = [rows_block(half, o.shape[1]) for o in outs]
    out_specs[4] = whole_block(outs[4])
    block = pl.BlockSpec((1, half, depth), lambda g, w: (2 * w[1] + i, g, 0))
    vector = whole_block(gain)
    rows = rows_block(half, depth)
    carried = [] if final is None else [final]
    last = 13
    return launch(
        backward_kernel, "backward", where,
        (
            normed, gain, shift, out_grad, second_gain, second_shift, pull, *ups, *downs, part,
            part_far, *carried,
        ),
        [
            rows,
            vector,
            vector,
            block,
            vector,
            vector,
            rows_block(half, hidden),
            *[ANY] * 4,
            rows,
            rows,
            *[ANY] * len(carried),
        ],
        [shape((count, length, depth), BF16), *outs], [block, *out_specs], (2,), 34, after,
        streamed=(0, 3, *range(6, 11), *[last] * len(carried)), stored=(0, 1, 2, 3, 4),
        scratch=fetched(ups[0]), aliases={last + 1: 0} if carried else {},
    )


def products_kernel(where_ref, *refs, count):
    def take(number):
        nonlocal refs
        taken, refs = refs[:number], refs[number:]
        return taken

    lows, slopes = take(2 * count), take(2 * count)
    befores, actives = take(count), take(count)
    kept_ref, *sent_refs = refs
    width = kept_ref.shape[3]
    for place, (lefts, rights) in enumerate(((lows, befores), (slopes, actives))):
        for group in range(2):
            columns = slice(group * width, (group + 1) * width)
            total = None
            for n in range(count):
                left = jnp.concatenate([lefts[2 * n][...], lefts[2 * n + 1][...]], axis=1)
                part = dot(left, rights[n][:, columns], 0, 0)
                total = part if total is None else total + part
            for step in range(2):
                value = total[step * BLOCK : (step + 1) * BLOCK, :]
                if group == 0:
                    kept_ref[step, place] = value
                else:
                    sent_refs[2 * step + place][...] = value


def products(pair, where, lows, slopes, befores, actives, after):
    length, depth = lows[0].shape
    width = befores[0].shape[1] // 2
    count = len(lows)
    tiles, values = [], []
    for way, arrays in enumerate((lows, slopes)):
        for array in arrays:
            for step in range(2):
                place = 4 + 2 * (2 * pair + step) + way
                values.append(array)
                tiles.append(
                    pl.BlockSpec((length, BLOCK), lambda i, w, place=place: (0, w[place]))
                )
    outs = [shape((2, 2, BLOCK, width), F32)] + [shape((BLOCK, width), F32)] * 4
    return launch(
        functools.partial(products_kernel, count=count), "products", where,
        (*values, *befores, *actives), tiles + [RESIDENT] * (2 * count), outs,
        [whole_block(o) for o in outs], (1,), 18, after, streamed=range(4 * count),
    )


def first_kernel(
    where_ref, part_ref, part_far_ref, slope_ref, normed_ref, scaled_ref, gain_ref,
    wo_ref, one_ref, low_ref, mixed_ref, sums_ref,
):
    step = pl.program_id(0)
    upstream = slope_ref[...] + (part_ref[...] + part_far_ref[...])
    normed = normed_ref[...]

    @pl.when(step == 0)
    def _():
        sums_ref[...] = jnp.zeros_like(sums_ref)

    sums_ref[0:1, :] += jnp.sum(upstream * normed, axis=0, keepdims=True)
    sums_ref[1:2, :] += jnp.sum(upstream, axis=0, keepdims=True)
    slope = norm_back(upstream, normed, scaled_ref[:, 0:1], gain_ref[...])
    one_ref[...] = slope
    low = slope.astype(BF16)
    low_ref[...] = low
    width = mixed_ref.shape[1]
    weights = wo_ref[pl.ds(pl.multiple_of(where_ref[2] * width, width), width), :]
    mixed_ref[...] = dot(low, weights, 1, 1).astype(BF16)


def first(where, part, part_far, slope, normed, scaled, gain, wo, after):
    length, depth = slope.shape
    both = wo.shape[0] // 2
    half = length // 2
    outs = [
        shape((length, depth), F32),
        shape((length, depth), BF16),
        shape((length, both), BF16),
        shape((8, depth), F32),
    ]
    out_specs = [rows_block(half, o.shape[1]) for o in outs]
    out_specs[3] = whole_block(outs[3])
    rows = rows_block(half, depth)
    return launch(
        first_kernel, "first", where, (part, part_far, slope, normed, scaled, gain, wo),
        [rows, rows, rows, rows, rows_block(half, 128), whole_block(gain), RESIDENT],
        outs, out_specs, (2,), 18, after, streamed=(2, 3, 4), stored=(0, 1),
    )


def attend_back_kernel(
    where_ref, qkv_ref, go_ref, sums_ref, seg_ref, weights_ref, out_ref, grads_ref,
    key_slope, value_slope,
):
    width = weights_ref.shape[2] // 3
    owner, _ = lanes(width)
    zero = jnp.zeros((), BF16)
    spares = [spare_columns(seg_ref[0], sums_ref[...], group, width) for group in range(2)]

    def part_of(group, n):
        start = (3 * group + n) * width
        return qkv_ref[0, :, start : start + width]

    def products_of(group, head):
        spare_q, spare_k = spares[group]
        mine = owner == head
        score = dot(
            pick(head, owner, part_of(group, 0), spare_q, zero),
            jnp.where(mine, part_of(group, 1), spare_k), 1, 1,
        )
        upstream = go_ref[:, group * width : (group + 1) * width]
        return score, dot(jnp.where(mine, upstream, zero), part_of(group, 2), 1, 1)

    ahead = products_of(0, 0)
    for group in range(2):
        keys = part_of(group, 1)
        queries_t = part_of(group, 0).T
        upstream_t = go_ref[:, group * width : (group + 1) * width].T
        query_slope = jnp.zeros(keys.shape, F32)
        for head in range(GROUP):
            row = group * GROUP + head
            score, drift = ahead
            if row + 1 < 2 * GROUP:
                ahead = products_of((row + 1) // GROUP, (row + 1) % GROUP)
            place = slice(head * HEAD_DIM, (head + 1) * HEAD_DIM)
            chances = jnp.exp(score)
            slopes = chances * (drift - jnp.sum(drift * chances, axis=-1, keepdims=True))
            slopes = slopes.astype(BF16)
            query_slope = query_slope + dot(slopes, jnp.where(owner == head, keys, zero))
            key_slope[place, :] = dot(queries_t[place, :], slopes)
            value_slope[place, :] = dot(upstream_t[place, :], chances.astype(BF16))
        start = 3 * group * width
        grads_ref[:, start : start + width] = (query_slope * SCALE).astype(BF16)
        grads_ref[:, start + width : start + 2 * width] = key_slope[...].T.astype(BF16)
        grads_ref[:, start + 2 * width : start + 3 * width] = value_slope[...].T.astype(BF16)
        part = dot(grads_ref[:, start : start + 3 * width], weights_ref[group], 1, 1)
        if group == 0:
            out_ref[...] = part
        else:
            out_ref[...] += part


def attend_back(i, where, qkv, go, mixed, seg, weights, after):
    _, length, columns = qkv.shape
    _, depth, width = weights.shape
    outs = [shape((length, depth), F32), shape((length, columns), BF16)]
    return launch(
        attend_back_kernel, "attend_back", where, (qkv, go, mixed, seg, weights),
        [
            whole_block(qkv),
            whole_block(go),
            pl.BlockSpec((8, columns // 3), lambda g, w: (length // 8, 0)),
            sequence(i, (8, length)),
            RESIDENT,
        ],
        outs, [whole_block(o) for o in outs], (1,), 22, after,
        scratch=[pltpu.VMEM((width // 3, length), F32)] * 2, streamed=(0,), stored=(1,),
    )


def total_kernel(where_ref, one_ref, part_ref, far_ref, *rest):
    final_ref, out_ref = rest[-2:]
    final = (one_ref[...] + (part_ref[...] + far_ref[...])).astype(BF16)
    final_ref[0] = final
    out_ref[...] = final.astype(F32)


def total(i, count, where, one, part, far, final, after):
    length, depth = one.shape
    quarter = length // 4
    rows = rows_block(quarter, depth)
    carried = [] if final is None else [final]
    return launch(
        total_kernel, "total", where, (one, part, far, *carried),
        [rows] * 3 + [ANY] * len(carried),
        [shape((count, length, depth), BF16), shape((length, depth), F32)],
        [pl.BlockSpec((1, quarter, depth), lambda g, w: (2 * w[1] + i, g, 0)), rows],
        (4,), 10, after, streamed=(0, 3) if carried else (0,), stored=(0,),
        aliases={4: 0} if carried else {},
    )


def head_products_kernel(where_ref, *refs, count):
    def take(number):
        nonlocal refs
        taken, refs = refs[:number], refs[number:]
        return taken

    def summed(lefts, rights):
        total = None
        for n in range(count):
            left = jnp.concatenate([lefts[2 * n], lefts[2 * n + 1]], axis=1)
            part = dot(left, rights[n], 0, 0)
            total = part if total is None else total + part
        return total

    firsts, seconds, ones = take(2 * count), take(2 * count), take(2 * count)
    grads, mixed, first_sums, second_sums = take(count), take(count), take(2 * count), take(2 * count)
    width = mixed[0].shape[2] // 2
    x_first, x_second = ([ref[0] for ref in group] for group in (firsts, seconds))
    for group, out in enumerate(refs):
        start = 3 * group * width
        pairs = [ref[:, start : start + 2 * width] for ref in grads]
        heads = summed(x_first, pairs)
        values = summed(x_second, [ref[:, start + 2 * width : start + 3 * width] for ref in grads])
        outputs = summed(
            [ref[...] for ref in ones], [ref[0, :, group * width : (group + 1) * width] for ref in mixed]
        )
        for step in range(2):
            rows = slice(step * BLOCK, (step + 1) * BLOCK)
            out[step, 0:BLOCK, :] = heads[rows, 0:width]
            out[step, BLOCK : 2 * BLOCK, :] = heads[rows, width:]
            out[step, 2 * BLOCK : 3 * BLOCK, :] = values[rows, :]
            out[step, 3 * BLOCK : 4 * BLOCK, :] = outputs[rows, :]
            out[step, 4 * BLOCK :, :] = jnp.zeros((8, width), F32)
            for row, sums in ((0, first_sums), (2, second_sums)):
                gains = sums[step][0:2, :]
                for n in range(1, count):
                    gains = gains + sums[2 * n + step][0:2, :]
                out[step, 4 * BLOCK + row : 4 * BLOCK + row + 2, 0:BLOCK] = gains


def head_products(where, x, ones, grads, mixed, firsts, seconds, after):
    _, length, depth = x.shape
    count = len(ones)
    width = mixed[0].shape[2] // 2

    def tile(way, step, dims, lead=()):
        return pl.BlockSpec(
            (*dims, BLOCK), lambda j, w: (*[f(w) for f in lead], 0, w[4 + 2 * (2 * j + step) + way])
        )

    def inputs_of(way):
        return [
            tile(way, step, (1, length), (lambda w, i=i: 2 * w[1] + i,))
            for i in range(count) for step in range(2)
        ]

    out = shape((depth // BLOCK, 4 * BLOCK + 8, width), F32)
    twice = lambda arrays: [a for a in arrays for _ in range(2)]
    return launch(
        functools.partial(head_products_kernel, count=count), "head_products", where,
        (
            *[x] * (4 * count), *twice(ones), *grads, *mixed, *twice(firsts), *twice(seconds)
        ),
        inputs_of(0) + inputs_of(1) + [tile(1, step, (length,)) for _ in ones for step in range(2)]
        + [whole_block(a) for a in (*grads, *mixed)]
        + [tile(1, step, (8,)) for _ in range(2 * count) for step in range(2)],
        [out] * 2, [pl.BlockSpec((2, *out.shape[1:]), lambda j, w: (j, 0, 0))] * 2,
        (depth // BLOCK // 2,), 16, after, streamed=range(8 * count), stored=(0, 1),
    )


def ring_kernel(where_ref, *refs, arrivals, sizes):
    outs = refs[-2:]
    sources = refs[arrivals : -2]
    for way in range(2):
        mine, start = [], 0
        count = sizes[way]
        kept = sources[way * sizes[0] : way * sizes[0] + count]
        base = sizes[0] + sizes[1]
        near = sources[base + way * sizes[0] : base + way * sizes[0] + count]
        for left, right in zip(kept, near):
            value = left[...].reshape(left.shape[-2:]) + right[...].reshape(right.shape[-2:])
            rows = slice(start, start + value.shape[0])
            if arrivals:
                value = refs[way][rows, :] + value
            outs[way][rows, :] = value
            start += value.shape[0]


def ring_step(where, arrived, kept, near, after):
    entries = [*kept[0], *kept[1], *near[0], *near[1]]
    specs = [whole_block(a) for a in arrived]
    specs += [pl.BlockSpec(dims, lambda i, w, at=at: at) for _, dims, at in entries]
    outs = [
        shape((sum(e[1][-2] for e in way), way[0][1][-1]), F32) for way in kept
    ]
    count = len(arrived)
    return launch(
        functools.partial(ring_kernel, arrivals=count, sizes=(len(kept[0]), len(kept[1]))),
        "ring_step", where, (*arrived, *[e[0] for e in entries]), specs, outs,
        [whole_block(o) for o in outs], (1,), 8, after,
        streamed=[count + n for n, e in enumerate(entries) if len(e[0].shape) > 2],
    )


def finish_kernel(where_ref, value_ref, final_ref, out_ref):
    del final_ref
    out_ref[0] = value_ref[...].astype(BF16)


def finish(i, where, value, final, after):
    length, depth = value.shape
    half = length // 2
    return launch(
        finish_kernel, "finish", where, (value, final), [rows_block(half, depth), ANY],
        [shape(final.shape, BF16)],
        [pl.BlockSpec((1, half, depth), lambda g, w: (2 * (1 - w[1]) + i, g, 0))],
        (2,), 8, after, aliases={2: 0}, stored=(0,), streamed=(1,),
    )[0]


def solution(mesh):
    ranks = mesh.shape["dp"]
    group = mesh.shape["tensor"]
    assert group == 4 and ranks % 8 == 0
    near_pairs = [(t, t ^ 1) for t in range(group)]
    far_pairs = [(t, t ^ 2) for t in range(group)]
    turns = (
        [(RING[p], RING[(p + 1) % 8]) for p in range(8)],
        [(RING[p], RING[(p - 1) % 8]) for p in range(8)],
    )

    def near(value):
        return lax.ppermute(value, "tensor", near_pairs)

    def scatter(value):
        return lax.psum_scatter(value, "dp", scatter_dimension=0, tiled=True)

    def far(value):
        return lax.ppermute(value, "tensor", far_pairs)

    def body(
        block_input, segment_ids, query_weight, key_weight, value_weight, output_weight,
        first_gain, first_shift, up_weight, down_weight, second_gain, second_shift, out_grad,
    ):
        count, length, depth = block_input.shape
        width = query_weight.shape[1]
        part = depth // ranks
        mine = range(count // 2)
        me = lax.axis_index("tensor")
        rank = lax.axis_index("dp")
        natural = [n for n in range(8) for _ in range(2)]
        owners = jnp.asarray(OWNERS if ranks == 8 else [natural], jnp.int32)
        owners = lax.dynamic_index_in_dim(owners, rank if ranks == 8 else 0, 0, False)
        where = jnp.concatenate(
            [jnp.stack([me, me % 2, me // 2, rank]).astype(jnp.int32), owners]
        )
        seg = jnp.broadcast_to(segment_ids[:, None, :], (count, 8, length))
        gain_one, shift_one = first_gain[None], first_shift[None]
        gain_two, shift_two = second_gain[None], second_shift[None]
        order = Order()

        def then(call, *args, **kwargs):
            return call(*args, after=order, **kwargs)

        own_low, own_wide, wo_half = then(
            widen_heads, where, query_weight, key_weight, value_weight, output_weight
        )
        near_wide, wo_first = near(own_wide), far(wo_half)
        weights, wo_near = then(narrow_near, where, own_low, near_wide, output_weight)
        (wo_first,) = then(gate, where, wo_first)
        wide = then(convert, where, up_weight, down_weight, dtype=F32)
        wide_near = [near(w) for w in wide]
        wo_second = lax.ppermute(wo_first, "dp", [(r, r ^ 1) for r in range(ranks)])
        wo_both = [near(wo_first)]
        heads, mixed_far = [], []
        for i in mine:
            heads.append(then(attend, i, where, block_input, weights, seg))
            mixed_far.append(far(heads[i][3]))
        mixed_low, qkv, tops, mixed = zip(*heads)
        up_near, down_near = then(convert, where, *wide_near, dtype=BF16)
        ups, downs = (up_weight, up_near), (down_weight, down_near)
        (wo_second,) = then(gate, where, wo_second)
        wo_both.append(near(wo_second))
        wo = then(assemble, where, output_weight, wo_near, (wo_first, wo_second), wo_both)

        forwards, part_far = [], []
        for i in mine:
            forwards.append(
                then(
                    forward, i, where, block_input, mixed[i], mixed_far[i], wo, gain_one,
                    shift_one, ups, downs,
                )
            )
            part_far.append(far(forwards[i][5]))

        heads_own = width // HEAD_DIM
        peak = functools.reduce(jnp.maximum, tops)
        peak = jnp.maximum(peak[:heads_own], near(peak)[heads_own:])
        step = 1
        while step < ranks:
            peak = jnp.maximum(peak, lax.ppermute(peak, "dp", [(i, i ^ step) for i in range(ranks)]))
            step *= 2
        (peak,) = then(gate, where, peak)

        written = {"layer_out": None, "input_grad": None}
        backs, slope_far = [], []
        for i in mine:
            normed, scaled, low, active, pull, part_sum = forwards[i]
            backs.append(
                then(
                    backward, i, where, normed, gain_one, shift_one, part_sum, part_far[i],
                    out_grad, gain_two, shift_two, pull, ups, downs, written["layer_out"],
                )
            )
            written["layer_out"], *backs[i] = backs[i]
            slope_far.append(far(backs[i][5]))

        lows, actives = [f[2] for f in forwards], [f[3] for f in forwards]
        slope_lows, befores = [b[2] for b in backs], [b[3] for b in backs]
        def ff_part(pair):
            kept, *sent = then(products, pair, where, lows, slope_lows, befores, actives)
            return kept, [near(a) for a in sent]

        def send(held):
            return [lax.ppermute(h, "dp", t) for h, t in zip(held, turns)]

        ff_parts = []

        def ff_step(n, arrived):
            kept, sent = ff_parts[n // 2]
            dims = (1, 1, BLOCK, kept.shape[3])
            return then(
                ring_step, where, arrived,
                [[(kept, dims, (n % 2, way, 0, 0))] for way in range(2)],
                [[(sent[2 * (n % 2) + way], dims[2:], (0, 0))] for way in range(2)],
            )

        def ff_ring():
            held = ff_step(0, ())
            for n in range(1, 8):
                arrived = send(held)
                yield None
                held = ff_step(n, arrived)
            yield held

        def head_ring(kept, near):
            width = kept.shape[2]

            def entries(array, n):
                block = lambda rows, at: (array, (1, rows, width), (n, at, 0))
                return [[block(2 * BLOCK, 0)], [block(2 * BLOCK, 1), block(8, 4 * BLOCK // 8)]]

            held = then(ring_step, where, (), entries(kept, 0), entries(near, 0))
            for n in range(1, 8):
                arrived = send(held)
                yield None
                held = then(ring_step, where, arrived, entries(kept, n), entries(near, n))
            yield held

        def finish_layer(i, value):
            written["layer_out"] = then(finish, i, where, near(value), written["layer_out"])

        def total_input(i):
            written["input_grad"], result = then(
                total, i, count, where, firsts[i][0], owns[i][0], input_far[i],
                written["input_grad"],
            )
            return result

        def finish_input(i, value):
            written["input_grad"] = then(finish, i, where, near(value), written["input_grad"])

        def first_back(i):
            firsts.append(
                then(
                    first, where, backs[i][5], slope_far[i], backs[i][1], *forwards[i][:2],
                    gain_one, wo,
                )
            )

        def own_back(i):
            owns.append(then(attend_back, i, where, qkv[i], firsts[i][2], mixed[i], seg, weights))
            input_far.append(far(owns[i][0]))

        firsts, owns, input_far = [], [], []
        ring = ff_ring() if ranks == 8 else iter(())
        ff_parts.append(ff_part(0))
        next(ring, None)
        ff_parts.append(ff_part(1))
        next(ring, None)
        first_back(0)
        own_back(0)
        next(ring, None)
        ff_parts.append(ff_part(2))
        ff_parts.append(ff_part(3))
        next(ring, None)
        first_back(1)
        next(ring, None)
        own_back(1)
        next(ring, None)
        kept, sent = then(
            head_products, where, block_input, [f[1] for f in firsts], [o[1] for o in owns],
            mixed_low, [f[3] for f in firsts], [b[4] for b in backs],
        )
        next(ring, None)
        input_rows = [total_input(0)]
        if ranks == 8:
            *_, (up_grad, down_grad) = ring
        sent, *layers = then(gate, where, sent, backs[0][0], backs[1][0])
        sent = near(sent)
        ring = head_ring(kept, sent) if ranks == 8 else iter(())
        next(ring, None)
        finish_layer(0, layers[0])
        next(ring, None)
        finish_layer(1, layers[1])
        next(ring, None)
        finish_input(0, input_rows[0])
        next(ring, None)
        next(ring, None)
        input_rows.append(total_input(1))
        next(ring, None)
        next(ring, None)
        finish_input(1, input_rows[1])

        if ranks == 8:
            *_, (left, right) = ring
            query_grad, key_grad = left[:BLOCK], left[BLOCK:]
            value_grad, output_grad = right[:BLOCK], right[BLOCK : 2 * BLOCK].T
            gains = right[2 * BLOCK : 2 * BLOCK + 4, :BLOCK]
        else:
            def rows_of(value, start, rows=BLOCK):
                return scatter(value[:, start : start + rows].reshape(8 * rows, width))

            up, down = [
                jnp.concatenate(
                    [
                        k[n, way] + s[2 * n + way]
                        for k, s in ff_parts for n in range(2)
                    ], axis=0,
                )
                for way in range(2)
            ]
            up_grad, down_grad = scatter(up), scatter(down)
            value = kept + sent
            query_grad, key_grad, value_grad = (rows_of(value, n * BLOCK) for n in range(3))
            output_grad = rows_of(value, 3 * BLOCK).T
            gains = value[:, 4 * BLOCK : 4 * BLOCK + 4, :BLOCK].transpose(0, 2, 1)
            gains = scatter(gains.reshape(depth, 4)).T

        factor = jnp.sqrt(CLIP / jnp.maximum(peak[:, 0], CLIP))
        column_factor = jnp.repeat(factor, HEAD_DIM)
        query_clipped = query_weight.astype(F32) * column_factor[None, :]
        key_clipped = key_weight.astype(F32) * column_factor[None, :]
        return (
            written["layer_out"], written["input_grad"], query_grad, key_grad, value_grad, output_grad,
            gains[0], gains[1], up_grad, down_grad.T, gains[2], gains[3],
            query_clipped, key_clipped,
        )

    batch = P("dp", None, None)
    in_specs = (
        batch, P("dp", None), P(None, "tensor"), P(None, "tensor"), P(None, "tensor"),
        P("tensor", None), P(), P(), P(None, "tensor"), P("tensor", None), P(), P(), batch,
    )
    out_specs = (
        batch, batch, P("dp", "tensor"), P("dp", "tensor"), P("dp", "tensor"), P("tensor", "dp"),
        P("dp"), P("dp"), P("dp", "tensor"), P("tensor", "dp"), P("dp"), P("dp"),
        P(None, "tensor"), P(None, "tensor"),
    )
    return jax.shard_map(body, mesh=mesh, in_specs=in_specs, out_specs=out_specs, check_vma=False)
```

```python
import functools

import jax
import jax.numpy as jnp
from jax import lax
from jax.experimental import pallas as pl
from jax.experimental.pallas import tpu as pltpu
from jax.sharding import PartitionSpec as P

F32 = jnp.float32
BF16 = jnp.bfloat16
HEAD_DIM = 64
FAR = -1e30
EPS = 1e-06
CLIP = 10.0
SCALE = HEAD_DIM**-0.5
ROOT_HALF = 0.5**0.5
BELL = 0.3989422804014327
GROUP = 4
BLOCK = 128
DOCS = 4
MIB = 1 << 20
RING = (0, 2, 4, 6, 7, 5, 3, 1)
OWNERS = tuple(
    tuple(RING[(RING.index(r) + way * (1 + n)) % 8] for n in range(8) for way in (-1, 1))
    for r in range(8)
)
ANY = pl.BlockSpec(memory_space=pl.ANY)
RESIDENT = pl.BlockSpec(memory_space=pltpu.VMEM)


def dot(left, right, left_dim=1, right_dim=0):
    return lax.dot_general(
        left, right, (((left_dim,), (right_dim,)), ((), ())), preferred_element_type=F32
    )


def normalize(total):
    average = jnp.mean(total, axis=-1, keepdims=True)
    centred = total - average
    variance = jnp.mean(centred * centred, axis=-1, keepdims=True)
    scaled = lax.rsqrt(variance + EPS)
    return centred * scaled, scaled


def norm_back(upstream, normed, scaled, gain):
    weighted = upstream * gain
    first = jnp.mean(weighted, axis=-1, keepdims=True)
    second = jnp.mean(weighted * normed, axis=-1, keepdims=True)
    return scaled * (weighted - first - normed * second)


def lanes(width):
    lane = lax.broadcasted_iota(jnp.int32, (1, width), 1)
    return lane // HEAD_DIM, lane % HEAD_DIM


def split(value):
    high = value.astype(BF16)
    rest = value - high.astype(F32)
    middle = rest.astype(BF16)
    return high, middle, (rest - middle.astype(F32)).astype(BF16)


def pick(head, owner, own, spare, zero):
    return jnp.where(owner == head, own, jnp.where(owner == (head + 1) % GROUP, spare, zero))


def spare_columns(seg_rows, sums, group, width):
    owner, lane = lanes(width)
    row8 = lax.broadcasted_iota(jnp.int32, (8, 1), 0)
    equal = jnp.where(seg_rows == row8, 1.0, 0.0)
    rows = [equal]
    wanted = [jnp.where(lane == row8, FAR, 0.0)]
    if sums is not None:
        head = row8 % GROUP
        here = (row8 // GROUP == group) & ((head + 1) % GROUP == owner)
        for n, value in enumerate(split(sums)):
            rows.append(value.astype(F32))
            wanted.append(jnp.where(here & (lane == DOCS + n), -1.0, 0.0))
    placed = jnp.concatenate(wanted, axis=0).astype(BF16)
    queries = dot(jnp.concatenate(rows, axis=0).astype(BF16), placed, 0, 0).astype(BF16)
    ones = jnp.where((lane >= DOCS) & (lane < DOCS + 3), 1.0, 0.0)
    placed = jnp.where((lane == row8) & (row8 < DOCS), 1.0, 0.0).astype(BF16)
    differ = jnp.where(seg_rows == row8, 0.0, 1.0).astype(BF16)
    keys = (dot(differ, placed, 0, 0) + ones).astype(BF16)
    return queries, keys


def shape(dims, dtype):
    return jax.ShapeDtypeStruct(tuple(dims), dtype)


def whole_block(array):
    zeros = (0,) * len(array.shape)
    return pl.BlockSpec(tuple(array.shape), lambda i, w: zeros)


def rows_block(rows, columns):
    return pl.BlockSpec((rows, columns), lambda i, w: (i, 0))


class Order:
    def __init__(self):
        self.token, self.stored = None, False

    def taken(self):
        if self.token is None:
            return []
        if self.stored:
            return [pltpu.with_memory_space_constraint(self.token, pltpu.HBM)]
        return [self.token]

    def give(self, results, stored):
        sizes = [r.size * r.dtype.itemsize for r in results]
        index = sizes.index(min(sizes))
        self.token, self.stored = results[index], index in stored


def launch(
    kernel, name, where, inputs, in_specs, outs, out_specs, grid, vmem, after,
    scratch=(), aliases=None, streamed=(), stored=(),
):
    count = len(inputs)
    tokens = after.taken()
    inputs = [
        pltpu.with_memory_space_constraint(value, pltpu.HBM) if i in streamed else value
        for i, value in enumerate(inputs)
    ]
    outs = [
        pltpu.HBM(value.shape, value.dtype) if i in stored else value
        for i, value in enumerate(outs)
    ]

    def run(where_ref, *refs):
        kernel(where_ref, *refs[:count], *refs[count + len(tokens) :])

    results = pl.pallas_call(
        run,
        grid_spec=pltpu.PrefetchScalarGridSpec(
            num_scalar_prefetch=1,
            grid=grid,
            in_specs=list(in_specs) + [ANY] * len(tokens),
            out_specs=list(out_specs),
            scratch_shapes=list(scratch),
        ),
        out_shape=outs,
        input_output_aliases=aliases or {},
        compiler_params=pltpu.CompilerParams(
            vmem_limit_bytes=vmem * MIB, dimension_semantics=("arbitrary",) * len(grid)
        ),
        cost_estimate=pl.CostEstimate(flops=1, bytes_accessed=1, transcendentals=0),
        name=name,
    )(where, *inputs, *tokens)
    after.give(results, stored)
    return results


def gate_kernel(*refs):
    del refs


def gate(where, *values, after):
    outs = [shape(v.shape, v.dtype) for v in values]
    return launch(
        gate_kernel, "gate", where, values, [ANY] * len(values), outs, [ANY] * len(values), (1,),
        2, after, aliases={i + 1: i for i in range(len(values))},
    )


def widen_heads_kernel(where_ref, wq_ref, wk_ref, wv_ref, wo_ref, own, wide, wo):
    width = wq_ref.shape[1]
    for index, ref in enumerate((wq_ref, wk_ref, wv_ref)):
        columns = slice(index * width, (index + 1) * width)
        value = ref[...]
        own[:, columns] = value
        wide[:, columns] = value.astype(F32)
    rows, depth = wo_ref.shape
    for index in range(depth // width):
        wide[index * rows : (index + 1) * rows, 3 * width :] = wo_ref[
            :, index * width : (index + 1) * width
        ].astype(F32)
    half = rows // 2
    wo[...] = wo_ref[pl.ds(pl.multiple_of((where_ref[3] % 2) * half, half), half), :].astype(F32)


def widen_heads(where, wq, wk, wv, wo, after):
    depth, width = wq.shape
    outs = [
        shape((depth, 3 * width), BF16),
        shape((depth, 4 * width), F32),
        shape((wo.shape[0] // 2, depth), F32),
    ]
    inputs = (wq, wk, wv, wo)
    return launch(
        widen_heads_kernel, "widen_heads", where, inputs, [whole_block(a) for a in inputs], outs,
        [whole_block(o) for o in outs], (1,), 12, after, streamed=range(4),
    )


def assemble_kernel(where_ref, own_ref, near_ref, *refs):
    *halves, out_ref = refs
    rows = own_ref.shape[0]
    half = rows // 2
    mine = where_ref[2] * 2 * rows
    other = (1 - where_ref[2]) * 2 * rows
    out_ref[pl.ds(pl.multiple_of(mine, rows), rows), :] = own_ref[...]
    out_ref[pl.ds(pl.multiple_of(mine + rows, rows), rows), :] = near_ref[...]
    parity = where_ref[3] % 2
    for start, first, second in ((other, *halves[0:2]), (other + rows, *halves[2:4])):
        for ref, place in ((first, parity), (second, 1 - parity)):
            begin = pl.multiple_of(start + place * half, half)
            out_ref[pl.ds(begin, half), :] = ref[...].astype(BF16)


def assemble(where, own, near, far, both, after):
    rows, columns = own.shape
    out = shape((4 * rows, columns), BF16)
    inputs = (own, near, *far, *both)
    return launch(
        assemble_kernel, "assemble", where, inputs, [whole_block(a) for a in inputs], [out],
        [whole_block(out)], (1,), 14, after,
    )[0]


def narrow_near_kernel(where_ref, own_ref, wide_ref, heads_ref, wo_ref):
    width = own_ref.shape[1] // 3
    heads_ref[0] = own_ref[...]
    heads_ref[1] = wide_ref[:, 0 : 3 * width].astype(BF16)
    rows, depth = wo_ref.shape
    for index in range(depth // width):
        wo_ref[:, index * width : (index + 1) * width] = wide_ref[
            index * rows : (index + 1) * rows, 3 * width :
        ].astype(BF16)


def narrow_near(where, own, wide, wo, after):
    outs = [shape((2, *own.shape), BF16), shape(wo.shape, BF16)]
    return launch(
        narrow_near_kernel, "narrow_near", where, (own, wide),
        [whole_block(own), whole_block(wide)], outs, [whole_block(o) for o in outs], (1,), 16,
        after,
    )


def convert_kernel(where_ref, *refs):
    half = len(refs) // 2
    for source, target in zip(refs[:half], refs[half:]):
        target[...] = source[...].astype(target.dtype)


def convert(where, *values, dtype, after):
    specs = [rows_block(v.shape[0] // 4, v.shape[1]) for v in values]
    held = range(len(values))
    wide = dtype == F32
    return launch(
        convert_kernel, "convert", where, values, specs, [shape(v.shape, dtype) for v in values],
        specs, (4,), 10, after, streamed=held if wide else (), stored=() if wide else held,
    )


def project_group(x, weights):
    width = weights.shape[1] // 3
    q = (dot(x, weights[:, 0:width]).astype(BF16) * SCALE).astype(BF16)
    k = dot(x, weights[:, width : 2 * width]).astype(BF16)
    v = dot(x, weights[:, 2 * width : 3 * width]).astype(BF16)
    return q, k, v


def attend_kernel(
    where_ref, x_ref, weights_ref, seg_ref, low_ref, qkv_ref, top_ref, o_ref, held_ref
):
    x = x_ref[0]
    width = weights_ref.shape[2] // 3
    owner, _ = lanes(width)
    spare_q, spare_k = spare_columns(seg_ref[0], None, 0, width)
    zero = jnp.zeros((), BF16)
    held_ref[...] = jnp.zeros_like(held_ref)
    groups = [project_group(x, weights_ref.at[group]) for group in range(2)]
    for group, values in enumerate(groups):
        for index, value in enumerate(values):
            start = (3 * group + index) * width
            qkv_ref[0, :, start : start + width] = value

    def scores_of(group, head):
        queries, keys, _ = groups[group]
        return dot(
            pick(head, owner, queries, spare_q, zero),
            jnp.where(owner == head, keys, spare_k), 1, 1,
        )

    for group in range(2):
        total = jnp.zeros(groups[group][0].shape, F32)
        for head in range(GROUP):
            row = group * GROUP + head
            scores = scores_of(group, head)
            top = jnp.max(scores, axis=-1, keepdims=True)
            raised = jnp.exp(scores - top)
            summed = jnp.sum(raised, axis=-1, keepdims=True)
            chances = raised * (1.0 / summed)
            total = total + dot(
                chances.astype(BF16), jnp.where(owner == head, groups[group][2], zero)
            )
            held_ref[:, row : row + 1] = top + jnp.log(summed)
            top_ref[row : row + 1, :] = jnp.broadcast_to(
                jnp.max(top, axis=0, keepdims=True), (1, top_ref.shape[1])
            )
        low = total.astype(BF16)
        low_ref[0, :, group * width : (group + 1) * width] = low
        o_ref[0 : x.shape[0], group * width : (group + 1) * width] = low.astype(F32)
    o_ref[x.shape[0] :, :] = held_ref[...].T[0:8, :]


def sequence(i, dims):
    return pl.BlockSpec((1, *dims), lambda g, w: (2 * w[1] + i, 0, 0))


def attend(i, where, x, weights, seg, after):
    _, length, depth = x.shape
    columns = weights.shape[2]
    width = columns // 3
    outs = [
        shape((1, length, 2 * width), BF16),
        shape((1, length, 2 * columns), BF16),
        shape((2 * GROUP, 128), F32),
        shape((length + 2 * GROUP, 2 * width), F32),
    ]
    out_specs = [whole_block(o) for o in outs]
    return launch(
        attend_kernel, "attend", where, (x, weights, seg),
        [sequence(i, (length, depth)), RESIDENT, sequence(i, (8, length))],
        outs, out_specs, (1,), 20, after, streamed=(0,), stored=(0, 1),
        scratch=[pltpu.VMEM((length, 128), F32)],
    )


def fetch(sources, held_ref, arrived):
    first = pl.program_id(0) == 0
    copies = [
        pltpu.make_async_copy(source, held_ref.at[n], arrived.at[n])
        for n, source in enumerate(sources)
    ]

    @pl.when(first)
    def _():
        for copy in copies:
            copy.start()

    def get(n):
        @pl.when(first)
        def _():
            copies[n].wait()

        return held_ref[n]

    return get


def forward_kernel(
    where_ref, x_ref, mixed_ref, mixed_far_ref, wo_ref, gain_ref,
    shift_ref, up_own, up_near, down_own, down_near,
    normed_ref, scaled_ref, low_ref, active_ref, pull_ref, part_ref, both_ref, held_ref, arrived,
):
    weight = fetch((up_own, down_own, up_near, down_near), held_ref, arrived)
    width = mixed_ref.shape[1]
    chip = where_ref[2]
    both_ref[:, pl.ds(pl.multiple_of(chip * width, width), width)] = mixed_ref[...].astype(BF16)
    both_ref[:, pl.ds(pl.multiple_of((1 - chip) * width, width), width)] = mixed_far_ref[
        ...
    ].astype(BF16)
    normed, scaled = normalize(x_ref[0].astype(F32) + dot(both_ref[...], wo_ref[...]))
    normed_ref[...] = normed
    scaled_ref[...] = jnp.broadcast_to(scaled, scaled_ref.shape)
    low = (normed * gain_ref[...] + shift_ref[...]).astype(BF16)
    low_ref[...] = low
    hidden = up_own.shape[1]
    parts = []
    for group in range(2):
        columns = slice(group * hidden, (group + 1) * hidden)
        before = dot(low, weight(2 * group))
        chance = 0.5 * (1.0 + lax.erf(before * ROOT_HALF))
        active = (before * chance).astype(BF16)
        active_ref[:, columns] = active
        pull_ref[:, columns] = chance + before * (jnp.exp(-0.5 * before * before) * BELL)
        parts.append(dot(active, weight(2 * group + 1)))
    part_ref[...] = parts[0] + parts[1]


def fetched(array):
    return [pltpu.VMEM((4, *array.shape), array.dtype), pltpu.SemaphoreType.DMA((4,))]


def forward(i, where, x, mixed, mixed_far, wo, gain, shift, ups, downs, after):
    _, length, depth = x.shape
    width = mixed.shape[1]
    hidden = 2 * ups[0].shape[1]
    half = length // 2
    pieces = rows_block(half, width)
    outs = [
        shape((length, depth), F32),
        shape((length, 128), F32),
        shape((length, depth), BF16),
        shape((length, hidden), BF16),
        shape((length, hidden), F32),
    ]
    out_specs = [rows_block(half, o.shape[1]) for o in outs]
    outs.append(shape((length, depth), F32))
    out_specs.append(rows_block(half, depth))
    return launch(
        forward_kernel, "forward", where, (x, mixed, mixed_far, wo, gain, shift, *ups, *downs),
        [
            pl.BlockSpec((1, half, depth), lambda g, w: (2 * w[1] + i, g, 0)),
            pieces,
            pieces,
            RESIDENT,
            whole_block(gain),
            whole_block(shift),
            *[ANY] * 4,
        ],
        outs, out_specs, (2,), 30, after,
        streamed=(0, 6, 7, 8, 9), stored=(0, 1, 2, 3, 4),
        scratch=[pltpu.VMEM((half, 2 * width), BF16), *fetched(ups[0])],
    )


def backward_kernel(
    where_ref, normed_ref, gain_ref, shift_ref, grad_ref, second_gain_ref, second_shift_ref,
    pull_ref, up_own, up_near, down_own, down_near, part_ref, part_far_ref, *rest, carried,
):
    (
        final_ref, *out_refs, slope_ref, slope_low_ref, before_ref, sums_ref, part_out_ref, held_ref,
        arrived,
    ) = rest[carried:]
    weight = fetch((down_own, up_own, down_near, up_near), held_ref, arrived)
    step = pl.program_id(0)
    hidden = normed_ref[...] * gain_ref[...] + shift_ref[...]
    normed, scaled = normalize(hidden + (part_ref[...] + part_far_ref[...]))
    out = (normed * second_gain_ref[...] + second_shift_ref[...]).astype(BF16)
    final_ref[0] = out
    if len(out_refs) == 1:
        out_refs[0][...] = out.astype(F32)
    for index, ref in enumerate(out_refs if len(out_refs) == 2 else ()):

        @pl.when(step == index)
        def _(ref=ref):
            ref[...] = out.astype(F32)

    upstream = grad_ref[0].astype(F32)

    @pl.when(step == 0)
    def _():
        sums_ref[...] = jnp.zeros_like(sums_ref)

    sums_ref[0:1, :] += jnp.sum(upstream * normed, axis=0, keepdims=True)
    sums_ref[1:2, :] += jnp.sum(upstream, axis=0, keepdims=True)
    slope = norm_back(upstream, normed, scaled, second_gain_ref[...])
    slope_ref[...] = slope
    low = slope.astype(BF16)
    slope_low_ref[...] = low
    units = up_own.shape[1]
    parts = []
    for group in range(2):
        columns = slice(group * units, (group + 1) * units)
        before = (dot(low, weight(2 * group), 1, 1) * pull_ref[:, columns]).astype(BF16)
        before_ref[:, columns] = before
        parts.append(dot(before, weight(2 * group + 1), 1, 1))
    part_out_ref[...] = parts[0] + parts[1]


def backward(
    i, where, normed, gain, shift, part, part_far, out_grad, second_gain, second_shift, pull,
    ups, downs, final, after,
):
    count, length, depth = out_grad.shape
    hidden = 2 * ups[0].shape[1]
    half = length // 2
    outs = [
        shape((length, depth), F32),
        shape((length, depth), BF16),
        shape((length, hidden), BF16),
        shape((8, depth), F32),
        shape((length, depth), F32),
    ]
    out_specs = [rows_block(half, o.shape[1]) for o in outs]
    out_specs[3] = whole_block(outs[3])
    halves = 2 if final is None else 1
    value = shape((length // halves, depth), F32)
    outs = [value] * halves + outs
    out_specs = [whole_block(value) if halves == 2 else rows_block(half, depth)] * halves + out_specs
    block = pl.BlockSpec((1, half, depth), lambda g, w: (2 * w[1] + i, g, 0))
    vector = whole_block(gain)
    rows = rows_block(half, depth)
    carried = [] if final is None else [final]
    last = 13
    return launch(
        functools.partial(backward_kernel, carried=len(carried)), "backward", where,
        (
            normed, gain, shift, out_grad, second_gain, second_shift, pull, *ups, *downs, part,
            part_far, *carried,
        ),
        [
            rows,
            vector,
            vector,
            block,
            vector,
            vector,
            rows_block(half, hidden),
            *[ANY] * 4,
            rows,
            rows,
            *[ANY] * len(carried),
        ],
        [shape((count, length, depth), BF16), *outs], [block, *out_specs], (2,), 34, after,
        streamed=(0, 3, *range(6, 11), *[last] * len(carried)),
        stored=(0, *range(1 + halves, 4 + halves)),
        scratch=fetched(ups[0]), aliases={last + 1: 0} if carried else {},
    )


def products_kernel(where_ref, *refs, count):
    def take(number):
        nonlocal refs
        taken, refs = refs[:number], refs[number:]
        return taken

    lows, slopes = take(2 * count), take(2 * count)
    befores, actives = take(count), take(count)
    kept_ref, *sent_refs = refs
    width = kept_ref.shape[3]
    for place, (lefts, rights) in enumerate(((lows, befores), (slopes, actives))):
        for group in range(2):
            columns = slice(group * width, (group + 1) * width)
            total = None
            for n in range(count):
                left = jnp.concatenate([lefts[2 * n][...], lefts[2 * n + 1][...]], axis=1)
                part = dot(left, rights[n][:, columns], 0, 0)
                total = part if total is None else total + part
            for step in range(2):
                value = total[step * BLOCK : (step + 1) * BLOCK, :]
                if group == 0:
                    kept_ref[step, place] = value
                elif len(sent_refs) == 4:
                    sent_refs[2 * step + place][...] = value
                else:
                    sent_refs[step][place] = value


def products(pair, where, lows, slopes, befores, actives, after):
    length, depth = lows[0].shape
    width = befores[0].shape[1] // 2
    count = len(lows)
    tiles, values = [], []
    for way, arrays in enumerate((lows, slopes)):
        for array in arrays:
            for step in range(2):
                place = 4 + 2 * (2 * pair + step) + way
                values.append(array)
                tiles.append(
                    pl.BlockSpec((length, BLOCK), lambda i, w, place=place: (0, w[place]))
                )
    outs = [shape((2, 2, BLOCK, width), F32)]
    outs += [shape((BLOCK, width), F32)] * 4 if pair < 2 else [shape((2, BLOCK, width), F32)] * 2
    return launch(
        functools.partial(products_kernel, count=count), "products", where,
        (*values, *befores, *actives), tiles + [RESIDENT] * (2 * count), outs,
        [whole_block(o) for o in outs], (1,), 18, after, streamed=range(4 * count),
    )


def first_kernel(
    where_ref, part_ref, part_far_ref, slope_ref, normed_ref, scaled_ref, gain_ref,
    wo_ref, one_ref, low_ref, mixed_ref, sums_ref,
):
    step = pl.program_id(0)
    upstream = slope_ref[...] + (part_ref[...] + part_far_ref[...])
    normed = normed_ref[...]

    @pl.when(step == 0)
    def _():
        sums_ref[...] = jnp.zeros_like(sums_ref)

    sums_ref[0:1, :] += jnp.sum(upstream * normed, axis=0, keepdims=True)
    sums_ref[1:2, :] += jnp.sum(upstream, axis=0, keepdims=True)
    slope = norm_back(upstream, normed, scaled_ref[:, 0:1], gain_ref[...])
    one_ref[...] = slope
    low = slope.astype(BF16)
    low_ref[...] = low
    width = mixed_ref.shape[1]
    weights = wo_ref[pl.ds(pl.multiple_of(where_ref[2] * width, width), width), :]
    mixed_ref[...] = dot(low, weights, 1, 1).astype(BF16)


def first(where, part, part_far, slope, normed, scaled, gain, wo, after):
    length, depth = slope.shape
    both = wo.shape[0] // 2
    half = length // 2
    outs = [
        shape((length, depth), F32),
        shape((length, depth), BF16),
        shape((length, both), BF16),
        shape((8, depth), F32),
    ]
    out_specs = [rows_block(half, o.shape[1]) for o in outs]
    out_specs[3] = whole_block(outs[3])
    rows = rows_block(half, depth)
    return launch(
        first_kernel, "first", where, (part, part_far, slope, normed, scaled, gain, wo),
        [rows, rows, rows, rows, rows_block(half, 128), whole_block(gain), RESIDENT],
        outs, out_specs, (2,), 18, after, streamed=(2, 3, 4), stored=(0, 1),
    )


def attend_back_kernel(
    where_ref, qkv_ref, go_ref, sums_ref, seg_ref, weights_ref, out_ref, grads_ref,
    key_slope, value_slope,
):
    width = weights_ref.shape[2] // 3
    owner, _ = lanes(width)
    zero = jnp.zeros((), BF16)
    spares = [spare_columns(seg_ref[0], sums_ref[...], group, width) for group in range(2)]

    def part_of(group, n):
        start = (3 * group + n) * width
        return qkv_ref[0, :, start : start + width]

    def products_of(group, head):
        spare_q, spare_k = spares[group]
        mine = owner == head
        score = dot(
            pick(head, owner, part_of(group, 0), spare_q, zero),
            jnp.where(mine, part_of(group, 1), spare_k), 1, 1,
        )
        upstream = go_ref[:, group * width : (group + 1) * width]
        return score, dot(jnp.where(mine, upstream, zero), part_of(group, 2), 1, 1)

    ahead = products_of(0, 0)
    for group in range(2):
        keys = part_of(group, 1)
        queries_t = part_of(group, 0).T
        upstream_t = go_ref[:, group * width : (group + 1) * width].T
        query_slope = jnp.zeros(keys.shape, F32)
        for head in range(GROUP):
            row = group * GROUP + head
            score, drift = ahead
            if row + 1 < 2 * GROUP:
                ahead = products_of((row + 1) // GROUP, (row + 1) % GROUP)
            place = slice(head * HEAD_DIM, (head + 1) * HEAD_DIM)
            chances = jnp.exp(score)
            slopes = chances * (drift - jnp.sum(drift * chances, axis=-1, keepdims=True))
            slopes = slopes.astype(BF16)
            query_slope = query_slope + dot(slopes, jnp.where(owner == head, keys, zero))
            key_slope[place, :] = dot(queries_t[place, :], slopes)
            value_slope[place, :] = dot(upstream_t[place, :], chances.astype(BF16))
        start = 3 * group * width
        grads_ref[:, start : start + width] = (query_slope * SCALE).astype(BF16)
        grads_ref[:, start + width : start + 2 * width] = key_slope[...].T.astype(BF16)
        grads_ref[:, start + 2 * width : start + 3 * width] = value_slope[...].T.astype(BF16)
        part = dot(grads_ref[:, start : start + 3 * width], weights_ref[group], 1, 1)
        if group == 0:
            out_ref[...] = part
        else:
            out_ref[...] += part


def attend_back(i, where, qkv, go, mixed, seg, weights, after):
    _, length, columns = qkv.shape
    _, depth, width = weights.shape
    outs = [shape((length, depth), F32), shape((length, columns), BF16)]
    return launch(
        attend_back_kernel, "attend_back", where, (qkv, go, mixed, seg, weights),
        [
            whole_block(qkv),
            whole_block(go),
            pl.BlockSpec((8, columns // 3), lambda g, w: (length // 8, 0)),
            sequence(i, (8, length)),
            RESIDENT,
        ],
        outs, [whole_block(o) for o in outs], (1,), 22, after,
        scratch=[pltpu.VMEM((width // 3, length), F32)] * 2, streamed=(0,), stored=(1,),
    )


def total_kernel(where_ref, one_ref, part_ref, far_ref, *rest):
    final_ref, out_ref = rest[-2:]
    final = (one_ref[...] + (part_ref[...] + far_ref[...])).astype(BF16)
    final_ref[0] = final
    out_ref[...] = final.astype(F32)


def total(i, count, where, one, part, far, final, after):
    length, depth = one.shape
    quarter = length // 4
    rows = rows_block(quarter, depth)
    carried = [] if final is None else [final]
    return launch(
        total_kernel, "total", where, (one, part, far, *carried),
        [rows] * 3 + [ANY] * len(carried),
        [shape((count, length, depth), BF16), shape((length, depth), F32)],
        [pl.BlockSpec((1, quarter, depth), lambda g, w: (2 * w[1] + i, g, 0)), rows],
        (4,), 10, after, streamed=(0, 3) if carried else (0,), stored=(0,),
        aliases={4: 0} if carried else {},
    )


def head_products_kernel(where_ref, *refs, count):
    def take(number):
        nonlocal refs
        taken, refs = refs[:number], refs[number:]
        return taken

    def summed(lefts, rights):
        total = None
        for n in range(count):
            left = jnp.concatenate([lefts[2 * n], lefts[2 * n + 1]], axis=1)
            part = dot(left, rights[n], 0, 0)
            total = part if total is None else total + part
        return total

    firsts, seconds, ones = take(2 * count), take(2 * count), take(2 * count)
    grads, mixed, first_sums, second_sums = take(count), take(count), take(2 * count), take(2 * count)
    width = mixed[0].shape[2] // 2
    x_first, x_second = ([ref[0] for ref in group] for group in (firsts, seconds))
    kept_ref, *sent_refs = refs
    for group in range(2):
        start = 3 * group * width
        pairs = [ref[:, start : start + 2 * width] for ref in grads]
        heads = summed(x_first, pairs)
        values = summed(x_second, [ref[:, start + 2 * width : start + 3 * width] for ref in grads])
        outputs = summed(
            [ref[...] for ref in ones], [ref[0, :, group * width : (group + 1) * width] for ref in mixed]
        )
        for step in range(2):
            rows = slice(step * BLOCK, (step + 1) * BLOCK)
            out = sent_refs[step] if group else kept_ref.at[step]
            out[0:BLOCK, :] = heads[rows, 0:width]
            out[BLOCK : 2 * BLOCK, :] = heads[rows, width:]
            out[2 * BLOCK : 3 * BLOCK, :] = values[rows, :]
            out[3 * BLOCK : 4 * BLOCK, :] = outputs[rows, :]
            out[4 * BLOCK :, :] = jnp.zeros((8, width), F32)
            for row, sums in ((0, first_sums), (2, second_sums)):
                gains = sums[step][0:2, :]
                for n in range(1, count):
                    gains = gains + sums[2 * n + step][0:2, :]
                out[4 * BLOCK + row : 4 * BLOCK + row + 2, 0:BLOCK] = gains


def head_products(pair, where, x, ones, grads, mixed, firsts, seconds, after):
    _, length, depth = x.shape
    count = len(ones)
    width = mixed[0].shape[2] // 2

    def tile(way, step, dims, lead=()):
        return pl.BlockSpec(
            (*dims, BLOCK),
            lambda j, w: (*[f(w) for f in lead], 0, w[4 + 2 * (2 * pair + step) + way]),
        )

    def inputs_of(way):
        return [
            tile(way, step, (1, length), (lambda w, i=i: 2 * w[1] + i,))
            for i in range(count) for step in range(2)
        ]

    out = shape((4 * BLOCK + 8, width), F32)
    outs = [shape((2, *out.shape), F32), out, out]
    twice = lambda arrays: [a for a in arrays for _ in range(2)]
    return launch(
        functools.partial(head_products_kernel, count=count), "head_products", where,
        (
            *[x] * (4 * count), *twice(ones), *grads, *mixed, *twice(firsts), *twice(seconds)
        ),
        inputs_of(0) + inputs_of(1) + [tile(1, step, (length,)) for _ in ones for step in range(2)]
        + [RESIDENT] * (2 * count)
        + [tile(1, step, (8,)) for _ in range(2 * count) for step in range(2)],
        outs, [whole_block(o) for o in outs], (1,), 12, after, streamed=range(6 * count),
    )


def ring_kernel(where_ref, *refs, arrivals, sizes):
    outs = refs[-2:]
    sources = refs[arrivals : -2]
    for way in range(2):
        mine, start = [], 0
        count = sizes[way]
        kept = sources[way * sizes[0] : way * sizes[0] + count]
        base = sizes[0] + sizes[1]
        near = sources[base + way * sizes[0] : base + way * sizes[0] + count]
        for left, right in zip(kept, near):
            value = left[...].reshape(left.shape[-2:]) + right[...].reshape(right.shape[-2:])
            rows = slice(start, start + value.shape[0])
            if arrivals:
                value = refs[way][rows, :] + value
            outs[way][rows, :] = value
            start += value.shape[0]


def ring_step(where, arrived, kept, near, after):
    entries = [*kept[0], *kept[1], *near[0], *near[1]]
    specs = [whole_block(a) for a in arrived]
    specs += [pl.BlockSpec(dims, lambda i, w, at=at: at) for _, dims, at in entries]
    outs = [
        shape((sum(e[1][-2] for e in way), way[0][1][-1]), F32) for way in kept
    ]
    return launch(
        functools.partial(ring_kernel, arrivals=len(arrived), sizes=(len(kept[0]), len(kept[1]))),
        "ring_step", where, (*arrived, *[e[0] for e in entries]), specs, outs,
        [whole_block(o) for o in outs], (1,), 8, after,
    )


def finish_kernel(where_ref, *refs):
    *halves, final_ref, out_ref, token_ref = refs
    del final_ref
    value = halves[0][...].reshape(out_ref.shape[1:])
    if len(halves) == 2:
        value = jnp.where(pl.program_id(0) == 0, value, halves[1][...])
    out_ref[0] = value.astype(BF16)
    token_ref[...] = jnp.zeros_like(token_ref)


def finish(i, where, values, final, after):
    half, depth = final.shape[1] // 2, final.shape[2]
    specs = [rows_block(half, depth)]
    if len(values) == 2:
        specs = [whole_block(v) for v in values]
    last = len(values)
    token = shape((8, 128), F32)
    return launch(
        finish_kernel, "finish", where, (*values, final), [*specs, ANY],
        [shape(final.shape, BF16), token],
        [
            pl.BlockSpec((1, half, depth), lambda g, w: (2 * (1 - w[1]) + i, g, 0)),
            whole_block(token),
        ],
        (2,), 10, after, aliases={last + 1: 0}, stored=(0,), streamed=(last,),
    )[0]


def solution(mesh):
    ranks = mesh.shape["dp"]
    group = mesh.shape["tensor"]
    assert group == 4 and ranks % 8 == 0
    near_pairs = [(t, t ^ 1) for t in range(group)]
    far_pairs = [(t, t ^ 2) for t in range(group)]
    turns = (
        [(RING[p], RING[(p + 1) % 8]) for p in range(8)],
        [(RING[p], RING[(p - 1) % 8]) for p in range(8)],
    )

    def near(value):
        return lax.ppermute(value, "tensor", near_pairs)

    def scatter(value):
        return lax.psum_scatter(value, "dp", scatter_dimension=0, tiled=True)

    def far(value):
        return lax.ppermute(value, "tensor", far_pairs)

    def body(
        block_input, segment_ids, query_weight, key_weight, value_weight, output_weight,
        first_gain, first_shift, up_weight, down_weight, second_gain, second_shift, out_grad,
    ):
        count, length, depth = block_input.shape
        width = query_weight.shape[1]
        part = depth // ranks
        mine = range(count // 2)
        me = lax.axis_index("tensor")
        rank = lax.axis_index("dp")
        natural = [n for n in range(8) for _ in range(2)]
        owners = jnp.asarray(OWNERS if ranks == 8 else [natural], jnp.int32)
        owners = lax.dynamic_index_in_dim(owners, rank if ranks == 8 else 0, 0, False)
        where = jnp.concatenate(
            [jnp.stack([me, me % 2, me // 2, rank]).astype(jnp.int32), owners]
        )
        seg = jnp.broadcast_to(segment_ids[:, None, :], (count, 8, length))
        gain_one, shift_one = first_gain[None], first_shift[None]
        gain_two, shift_two = second_gain[None], second_shift[None]
        order = Order()

        def then(call, *args, **kwargs):
            return call(*args, after=order, **kwargs)

        own_low, own_wide, wo_half = then(
            widen_heads, where, query_weight, key_weight, value_weight, output_weight
        )
        near_wide, wo_first = near(own_wide), far(wo_half)
        wide = convert(where, up_weight, down_weight, dtype=F32, after=Order())
        wide_near = [near(w) for w in wide]
        weights, wo_near = then(narrow_near, where, own_low, near_wide, output_weight)
        heads, mixed_far = [], []
        for i in mine:
            heads.append(then(attend, i, where, block_input, weights, seg))
            mixed_far.append(far(heads[i][3]))
            if i == 0:
                (wo_first,) = then(gate, where, wo_first)
                wo_second = lax.ppermute(wo_first, "dp", [(r, r ^ 1) for r in range(ranks)])
                wo_both = [near(wo_first)]
        mixed_low, qkv, tops, mixed = zip(*heads)
        up_near, down_near = then(convert, where, *wide_near, dtype=BF16)
        ups, downs = (up_weight, up_near), (down_weight, down_near)
        (wo_second,) = then(gate, where, wo_second)
        wo_both.append(near(wo_second))
        wo = then(assemble, where, output_weight, wo_near, (wo_first, wo_second), wo_both)

        forwards, part_far = [], []
        for i in mine:
            forwards.append(
                then(
                    forward, i, where, block_input, mixed[i], mixed_far[i], wo, gain_one,
                    shift_one, ups, downs,
                )
            )
            part_far.append(far(forwards[i][5]))

        heads_own = width // HEAD_DIM
        peak = functools.reduce(jnp.maximum, tops)
        peak = jnp.maximum(peak[:heads_own], near(peak)[heads_own:])
        step = 1
        while step < ranks:
            peak = jnp.maximum(peak, lax.ppermute(peak, "dp", [(i, i ^ step) for i in range(ranks)]))
            step *= 2
        (peak,) = then(gate, where, peak)

        written = {"layer_out": None, "input_grad": None}
        def finish_layer(i, values):
            written["layer_out"] = then(finish, i, where, values, written["layer_out"])

        backs, slope_parts, slope_far = [], [], []
        for i in mine:
            normed, scaled, low, active, pull, part_sum = forwards[i]
            backs.append(
                then(
                    backward, i, where, normed, gain_one, shift_one, part_sum, part_far[i],
                    out_grad, gain_two, shift_two, pull, ups, downs, written["layer_out"],
                )
            )
            written["layer_out"], *out, slope, slope_low, before, sums, part_sum = backs[i]
            backs[i] = (out, slope, slope_low, before, sums)
            slope_parts.append(part_sum)
            slope_far.append(far(part_sum))
            if i == 0:
                finish_layer(0, [near(v) for v in out])

        lows, actives = [f[2] for f in forwards], [f[3] for f in forwards]
        slope_lows, befores = [b[2] for b in backs], [b[3] for b in backs]
        def ff_part(pair):
            kept, *sent = then(products, pair, where, lows, slope_lows, befores, actives)
            return kept, [near(a) for a in sent]

        def send(held):
            return [lax.ppermute(h, "dp", t) for h, t in zip(held, turns)]

        ff_parts = []

        def ff_step(n, arrived):
            kept, sent = ff_parts[n // 2]
            dims = (1, 1, BLOCK, kept.shape[3])
            if len(sent) == 4:
                near = [[(sent[2 * (n % 2) + way], dims[2:], (0, 0))] for way in range(2)]
            else:
                near = [[(sent[n % 2], dims[1:], (way, 0, 0))] for way in range(2)]
            return then(
                ring_step, where, arrived,
                [[(kept, dims, (n % 2, way, 0, 0))] for way in range(2)], near,
            )

        def ff_ring():
            held = ff_step(0, ())
            for n in range(1, 8):
                arrived = send(held)
                yield None
                held = ff_step(n, arrived)
            yield held

        head_parts = []

        def head_part(pair):
            kept, *sent = then(
                head_products, pair, where, block_input, [f[1] for f in firsts],
                [o[1] for o in owns], mixed_low, [f[3] for f in firsts], [b[4] for b in backs],
            )
            head_parts.append((kept, [near(a) for a in sent]))

        def head_step(n, arrived):
            kept, sent = head_parts[n // 2]

            def entries(array, lead):
                block = lambda rows, at: (
                    array, (*[1 for _ in lead], rows, width), (*lead, at, 0)
                )
                return [[block(2 * BLOCK, 0)], [block(2 * BLOCK, 1), block(8, 4 * BLOCK // 8)]]

            return then(
                ring_step, where, arrived, entries(kept, (n % 2,)), entries(sent[n % 2], ())
            )

        def head_ring():
            held = head_step(0, ())
            for n in range(1, 8):
                arrived = send(held)
                yield None
                held = head_step(n, arrived)
            yield held

        def total_input(i):
            written["input_grad"], result = then(
                total, i, count, where, firsts[i][0], owns[i][0], input_far[i],
                written["input_grad"],
            )
            return result

        def finish_input(i, value):
            written["input_grad"] = then(finish, i, where, [value], written["input_grad"])

        def first_back(i):
            firsts.append(
                then(
                    first, where, slope_parts[i], slope_far[i], backs[i][1], *forwards[i][:2],
                    gain_one, wo,
                )
            )

        def own_back(i):
            owns.append(then(attend_back, i, where, qkv[i], firsts[i][2], mixed[i], seg, weights))
            input_far.append(far(owns[i][0]))

        firsts, owns, input_far = [], [], []
        ring = ff_ring() if ranks == 8 else iter(())
        ff_parts.append(ff_part(0))
        next(ring, None)
        ff_parts.append(ff_part(1))
        next(ring, None)
        first_back(0)
        ff_parts.append(ff_part(2))
        next(ring, None)
        own_back(0)
        next(ring, None)
        ff_parts.append(ff_part(3))
        next(ring, None)
        first_back(1)
        next(ring, None)
        own_back(1)
        head_part(0)
        ff_parts[3] = (ff_parts[3][0], then(gate, where, *ff_parts[3][1]))
        next(ring, None)
        heads_ring = head_ring() if ranks == 8 else iter(())
        head_parts[0] = (head_parts[0][0], then(gate, where, *head_parts[0][1]))
        next(heads_ring, None)
        head_part(1)
        if ranks == 8:
            *_, (up_grad, down_grad) = ring
        ring = heads_ring
        next(ring, None)
        rows = total_input(0)
        next(ring, None)
        (rows,) = then(gate, where, rows)
        rows = near(rows)
        head_part(2)
        next(ring, None)
        next(ring, None)
        head_part(3)
        next(ring, None)
        result = total_input(1)
        next(ring, None)
        result, layer = then(gate, where, result, *backs[1][0])
        result, layer = near(result), near(layer)
        finish_input(0, rows)
        finish_input(1, result)
        finish_layer(1, [layer])

        if ranks == 8:
            *_, (left, right) = ring
            query_grad, key_grad = left[:BLOCK], left[BLOCK:]
            value_grad, output_grad = right[:BLOCK], right[BLOCK : 2 * BLOCK].T
            gains = right[2 * BLOCK : 2 * BLOCK + 4, :BLOCK]
        else:
            def rows_of(value, start, rows=BLOCK):
                return scatter(value[:, start : start + rows].reshape(8 * rows, width))

            up, down = [
                jnp.concatenate(
                    [
                        k[n, way] + (s[2 * n + way] if len(s) == 4 else s[n][way])
                        for k, s in ff_parts for n in range(2)
                    ], axis=0,
                )
                for way in range(2)
            ]
            up_grad, down_grad = scatter(up), scatter(down)
            value = jnp.concatenate([k + jnp.stack(s) for k, s in head_parts], axis=0)
            query_grad, key_grad, value_grad = (rows_of(value, n * BLOCK) for n in range(3))
            output_grad = rows_of(value, 3 * BLOCK).T
            gains = value[:, 4 * BLOCK : 4 * BLOCK + 4, :BLOCK].transpose(0, 2, 1)
            gains = scatter(gains.reshape(depth, 4)).T

        factor = jnp.sqrt(CLIP / jnp.maximum(peak[:, 0], CLIP))
        column_factor = jnp.repeat(factor, HEAD_DIM)
        query_clipped = query_weight.astype(F32) * column_factor[None, :]
        key_clipped = key_weight.astype(F32) * column_factor[None, :]
        return (
            written["layer_out"], written["input_grad"], query_grad, key_grad, value_grad, output_grad,
            gains[0], gains[1], up_grad, down_grad.T, gains[2], gains[3],
            query_clipped, key_clipped,
        )

    batch = P("dp", None, None)
    in_specs = (
        batch, P("dp", None), P(None, "tensor"), P(None, "tensor"), P(None, "tensor"),
        P("tensor", None), P(), P(), P(None, "tensor"), P("tensor", None), P(), P(), batch,
    )
    out_specs = (
        batch, batch, P("dp", "tensor"), P("dp", "tensor"), P("dp", "tensor"), P("tensor", "dp"),
        P("dp"), P("dp"), P("dp", "tensor"), P("tensor", "dp"), P("dp"), P("dp"),
        P(None, "tensor"), P(None, "tensor"),
    )
    return jax.shard_map(body, mesh=mesh, in_specs=in_specs, out_specs=out_specs, check_vma=False)
```

```python
import functools

import jax
import jax.numpy as jnp
from jax import lax
from jax.experimental import pallas as pl
from jax.experimental.pallas import tpu as pltpu
from jax.sharding import PartitionSpec as P

F32 = jnp.float32
BF16 = jnp.bfloat16
HEAD_DIM = 64
FAR = -1e30
EPS = 1e-06
CLIP = 10.0
SCALE = HEAD_DIM**-0.5
ROOT_HALF = 0.5**0.5
BELL = 0.3989422804014327
GROUP = 4
BLOCK = 128
DOCS = 4
MIB = 1 << 20
RING = (0, 2, 4, 6, 7, 5, 3, 1)
OWNERS = tuple(
    tuple(RING[(RING.index(r) + way * (1 + n)) % 8] for n in range(8) for way in (-1, 1))
    for r in range(8)
)
ANY = pl.BlockSpec(memory_space=pl.ANY)
RESIDENT = pl.BlockSpec(memory_space=pltpu.VMEM)


def dot(left, right, left_dim=1, right_dim=0):
    return lax.dot_general(
        left, right, (((left_dim,), (right_dim,)), ((), ())), preferred_element_type=F32
    )


def normalize(total):
    average = jnp.mean(total, axis=-1, keepdims=True)
    centred = total - average
    variance = jnp.mean(centred * centred, axis=-1, keepdims=True)
    scaled = lax.rsqrt(variance + EPS)
    return centred * scaled, scaled


def norm_back(upstream, normed, scaled, gain):
    weighted = upstream * gain
    first = jnp.mean(weighted, axis=-1, keepdims=True)
    second = jnp.mean(weighted * normed, axis=-1, keepdims=True)
    return scaled * (weighted - first - normed * second)


def lanes(width):
    lane = lax.broadcasted_iota(jnp.int32, (1, width), 1)
    return lane // HEAD_DIM, lane % HEAD_DIM


def split(value):
    high = value.astype(BF16)
    rest = value - high.astype(F32)
    middle = rest.astype(BF16)
    return high, middle, (rest - middle.astype(F32)).astype(BF16)


def pick(head, owner, own, spare, zero):
    return jnp.where(owner == head, own, jnp.where(owner == (head + 1) % GROUP, spare, zero))


def spare_columns(seg_rows, sums, group, width):
    owner, lane = lanes(width)
    row8 = lax.broadcasted_iota(jnp.int32, (8, 1), 0)
    equal = jnp.where(seg_rows == row8, 1.0, 0.0)
    rows = [equal]
    wanted = [jnp.where(lane == row8, FAR, 0.0)]
    if sums is not None:
        head = row8 % GROUP
        here = (row8 // GROUP == group) & ((head + 1) % GROUP == owner)
        for n, value in enumerate(split(sums)):
            rows.append(value.astype(F32))
            wanted.append(jnp.where(here & (lane == DOCS + n), -1.0, 0.0))
    placed = jnp.concatenate(wanted, axis=0).astype(BF16)
    queries = dot(jnp.concatenate(rows, axis=0).astype(BF16), placed, 0, 0).astype(BF16)
    ones = jnp.where((lane >= DOCS) & (lane < DOCS + 3), 1.0, 0.0)
    placed = jnp.where((lane == row8) & (row8 < DOCS), 1.0, 0.0).astype(BF16)
    differ = jnp.where(seg_rows == row8, 0.0, 1.0).astype(BF16)
    keys = (dot(differ, placed, 0, 0) + ones).astype(BF16)
    return queries, keys


def shape(dims, dtype):
    return jax.ShapeDtypeStruct(tuple(dims), dtype)


def whole_block(array):
    zeros = (0,) * len(array.shape)
    return pl.BlockSpec(tuple(array.shape), lambda i, w: zeros)


def rows_block(rows, columns):
    return pl.BlockSpec((rows, columns), lambda i, w: (i, 0))


class Order:
    def __init__(self):
        self.token, self.stored = None, False

    def taken(self):
        if self.token is None:
            return []
        if self.stored:
            return [pltpu.with_memory_space_constraint(self.token, pltpu.HBM)]
        return [self.token]

    def give(self, results, stored):
        sizes = [r.size * jnp.dtype(r.dtype).itemsize for r in results]
        index = sizes.index(min(sizes))
        self.token, self.stored = results[index], index in stored


def launch(
    kernel, name, where, inputs, in_specs, outs, out_specs, grid, vmem, after,
    scratch=(), aliases=None, streamed=(), stored=(),
):
    count = len(inputs)
    tokens = after.taken()
    inputs = [
        pltpu.with_memory_space_constraint(value, pltpu.HBM) if i in streamed else value
        for i, value in enumerate(inputs)
    ]
    outs = [
        pltpu.HBM(value.shape, value.dtype) if i in stored else value
        for i, value in enumerate(outs)
    ]

    def run(where_ref, *refs):
        kernel(where_ref, *refs[:count], *refs[count + len(tokens) :])

    results = pl.pallas_call(
        run,
        grid_spec=pltpu.PrefetchScalarGridSpec(
            num_scalar_prefetch=1,
            grid=grid,
            in_specs=list(in_specs) + [ANY] * len(tokens),
            out_specs=list(out_specs),
            scratch_shapes=list(scratch),
        ),
        out_shape=outs,
        input_output_aliases=aliases or {},
        compiler_params=pltpu.CompilerParams(
            vmem_limit_bytes=vmem * MIB, dimension_semantics=("arbitrary",) * len(grid)
        ),
        cost_estimate=pl.CostEstimate(flops=1, bytes_accessed=1, transcendentals=0),
        name=name,
    )(where, *inputs, *tokens)
    after.give(results, stored)
    return results


def gate_kernel(*refs):
    del refs


def gate(where, *values, after):
    outs = [shape(v.shape, v.dtype) for v in values]
    return launch(
        gate_kernel, "gate", where, values, [ANY] * len(values), outs, [ANY] * len(values), (1,),
        2, after, aliases={i + 1: i for i in range(len(values))},
    )


def widen_heads_kernel(where_ref, wq_ref, wk_ref, wv_ref, wo_ref, own, wide, wo):
    width = wq_ref.shape[1]
    for index, ref in enumerate((wq_ref, wk_ref, wv_ref)):
        columns = slice(index * width, (index + 1) * width)
        value = ref[...]
        own[:, columns] = value
        wide[:, columns] = value.astype(F32)
    rows, depth = wo_ref.shape
    for index in range(depth // width):
        wide[index * rows : (index + 1) * rows, 3 * width :] = wo_ref[
            :, index * width : (index + 1) * width
        ].astype(F32)
    half = rows // 2
    wo[...] = wo_ref[pl.ds(pl.multiple_of((where_ref[3] % 2) * half, half), half), :].astype(F32)


def widen_heads(where, wq, wk, wv, wo, after):
    depth, width = wq.shape
    outs = [
        shape((depth, 3 * width), BF16),
        shape((depth, 4 * width), F32),
        shape((wo.shape[0] // 2, depth), F32),
    ]
    inputs = (wq, wk, wv, wo)
    return launch(
        widen_heads_kernel, "widen_heads", where, inputs, [whole_block(a) for a in inputs], outs,
        [whole_block(o) for o in outs], (1,), 12, after, streamed=range(4),
    )


def assemble_kernel(where_ref, own_ref, near_ref, *refs):
    *halves, out_ref = refs
    rows = own_ref.shape[0]
    half = rows // 2
    mine = where_ref[2] * 2 * rows
    other = (1 - where_ref[2]) * 2 * rows
    out_ref[pl.ds(pl.multiple_of(mine, rows), rows), :] = own_ref[...]
    out_ref[pl.ds(pl.multiple_of(mine + rows, rows), rows), :] = near_ref[...]
    parity = where_ref[3] % 2
    for start, first, second in ((other, *halves[0:2]), (other + rows, *halves[2:4])):
        for ref, place in ((first, parity), (second, 1 - parity)):
            begin = pl.multiple_of(start + place * half, half)
            out_ref[pl.ds(begin, half), :] = ref[...].astype(BF16)


def assemble(where, own, near, far, both, after):
    rows, columns = own.shape
    out = shape((4 * rows, columns), BF16)
    inputs = (own, near, *far, *both)
    return launch(
        assemble_kernel, "assemble", where, inputs, [whole_block(a) for a in inputs], [out],
        [whole_block(out)], (1,), 14, after,
    )[0]


def narrow_near_kernel(where_ref, own_ref, wide_ref, heads_ref, wo_ref):
    width = own_ref.shape[1] // 3
    heads_ref[0] = own_ref[...]
    heads_ref[1] = wide_ref[:, 0 : 3 * width].astype(BF16)
    rows, depth = wo_ref.shape
    for index in range(depth // width):
        wo_ref[:, index * width : (index + 1) * width] = wide_ref[
            index * rows : (index + 1) * rows, 3 * width :
        ].astype(BF16)


def narrow_near(where, own, wide, wo, after):
    outs = [shape((2, *own.shape), BF16), shape(wo.shape, BF16)]
    return launch(
        narrow_near_kernel, "narrow_near", where, (own, wide),
        [whole_block(own), whole_block(wide)], outs, [whole_block(o) for o in outs], (1,), 16,
        after,
    )


def convert_kernel(where_ref, *refs):
    half = len(refs) // 2
    for source, target in zip(refs[:half], refs[half:]):
        target[...] = source[...].astype(target.dtype)


def convert(where, *values, dtype, after):
    specs = [rows_block(v.shape[0] // 4, v.shape[1]) for v in values]
    held = range(len(values))
    wide = dtype == F32
    return launch(
        convert_kernel, "convert", where, values, specs, [shape(v.shape, dtype) for v in values],
        specs, (4,), 10, after, streamed=held if wide else (), stored=() if wide else held,
    )


def project_group(x, weights):
    width = weights.shape[1] // 3
    q = (dot(x, weights[:, 0:width]).astype(BF16) * SCALE).astype(BF16)
    k = dot(x, weights[:, width : 2 * width]).astype(BF16)
    v = dot(x, weights[:, 2 * width : 3 * width]).astype(BF16)
    return q, k, v


def attend_kernel(
    where_ref, x_ref, weights_ref, seg_ref, low_ref, qkv_ref, top_ref, o_ref, held_ref
):
    x = x_ref[0]
    width = weights_ref.shape[2] // 3
    owner, _ = lanes(width)
    spare_q, spare_k = spare_columns(seg_ref[0], None, 0, width)
    zero = jnp.zeros((), BF16)
    held_ref[...] = jnp.zeros_like(held_ref)
    groups = [project_group(x, weights_ref.at[group]) for group in range(2)]
    for group, values in enumerate(groups):
        for index, value in enumerate(values):
            start = (3 * group + index) * width
            qkv_ref[0, :, start : start + width] = value

    def scores_of(group, head):
        queries, keys, _ = groups[group]
        return dot(
            pick(head, owner, queries, spare_q, zero),
            jnp.where(owner == head, keys, spare_k), 1, 1,
        )

    for group in range(2):
        total = jnp.zeros(groups[group][0].shape, F32)
        for head in range(GROUP):
            row = group * GROUP + head
            scores = scores_of(group, head)
            top = jnp.max(scores, axis=-1, keepdims=True)
            raised = jnp.exp(scores - top)
            summed = jnp.sum(raised, axis=-1, keepdims=True)
            chances = raised * (1.0 / summed)
            total = total + dot(
                chances.astype(BF16), jnp.where(owner == head, groups[group][2], zero)
            )
            held_ref[:, row : row + 1] = top + jnp.log(summed)
            top_ref[row : row + 1, :] = jnp.broadcast_to(
                jnp.max(top, axis=0, keepdims=True), (1, top_ref.shape[1])
            )
        low = total.astype(BF16)
        low_ref[0, :, group * width : (group + 1) * width] = low
        o_ref[0 : x.shape[0], group * width : (group + 1) * width] = low.astype(F32)
    o_ref[x.shape[0] :, :] = held_ref[...].T[0:8, :]


def sequence(i, dims):
    return pl.BlockSpec((1, *dims), lambda g, w: (2 * w[1] + i, 0, 0))


def attend(i, where, x, weights, seg, after):
    _, length, depth = x.shape
    columns = weights.shape[2]
    width = columns // 3
    outs = [
        shape((1, length, 2 * width), BF16),
        shape((1, length, 2 * columns), BF16),
        shape((2 * GROUP, 128), F32),
        shape((length + 2 * GROUP, 2 * width), F32),
    ]
    out_specs = [whole_block(o) for o in outs]
    return launch(
        attend_kernel, "attend", where, (x, weights, seg),
        [sequence(i, (length, depth)), RESIDENT, sequence(i, (8, length))],
        outs, out_specs, (1,), 20, after, streamed=(0,), stored=(0, 1),
        scratch=[pltpu.VMEM((length, 128), F32)],
    )


def fetch(sources, held_ref, arrived):
    first = pl.program_id(0) == 0
    copies = [
        pltpu.make_async_copy(source, held_ref.at[n], arrived.at[n])
        for n, source in enumerate(sources)
    ]

    @pl.when(first)
    def _():
        for copy in copies:
            copy.start()

    def get(n):
        @pl.when(first)
        def _():
            copies[n].wait()

        return held_ref[n]

    return get


def forward_kernel(
    where_ref, x_ref, mixed_ref, mixed_far_ref, wo_ref, gain_ref,
    shift_ref, up_own, up_near, down_own, down_near,
    normed_ref, scaled_ref, low_ref, active_ref, pull_ref, part_ref, both_ref, held_ref, arrived,
):
    weight = fetch((up_own, down_own, up_near, down_near), held_ref, arrived)
    width = mixed_ref.shape[1]
    chip = where_ref[2]
    both_ref[:, pl.ds(pl.multiple_of(chip * width, width), width)] = mixed_ref[...].astype(BF16)
    both_ref[:, pl.ds(pl.multiple_of((1 - chip) * width, width), width)] = mixed_far_ref[
        ...
    ].astype(BF16)
    normed, scaled = normalize(x_ref[0].astype(F32) + dot(both_ref[...], wo_ref[...]))
    normed_ref[...] = normed
    scaled_ref[...] = jnp.broadcast_to(scaled, scaled_ref.shape)
    low = (normed * gain_ref[...] + shift_ref[...]).astype(BF16)
    low_ref[...] = low
    hidden = up_own.shape[1]
    parts = []
    for group in range(2):
        columns = slice(group * hidden, (group + 1) * hidden)
        before = dot(low, weight(2 * group))
        chance = 0.5 * (1.0 + lax.erf(before * ROOT_HALF))
        active = (before * chance).astype(BF16)
        active_ref[:, columns] = active
        pull_ref[:, columns] = chance + before * (jnp.exp(-0.5 * before * before) * BELL)
        parts.append(dot(active, weight(2 * group + 1)))
    part_ref[...] = parts[0] + parts[1]


def fetched(array):
    return [pltpu.VMEM((4, *array.shape), array.dtype), pltpu.SemaphoreType.DMA((4,))]


def forward(i, where, x, mixed, mixed_far, wo, gain, shift, ups, downs, after):
    _, length, depth = x.shape
    width = mixed.shape[1]
    hidden = 2 * ups[0].shape[1]
    half = length // 2
    pieces = rows_block(half, width)
    outs = [
        shape((length, depth), F32),
        shape((length, 128), F32),
        shape((length, depth), BF16),
        shape((length, hidden), BF16),
        shape((length, hidden), F32),
    ]
    out_specs = [rows_block(half, o.shape[1]) for o in outs]
    outs.append(shape((length, depth), F32))
    out_specs.append(rows_block(half, depth))
    return launch(
        forward_kernel, "forward", where, (x, mixed, mixed_far, wo, gain, shift, *ups, *downs),
        [
            pl.BlockSpec((1, half, depth), lambda g, w: (2 * w[1] + i, g, 0)),
            pieces,
            pieces,
            RESIDENT,
            whole_block(gain),
            whole_block(shift),
            *[ANY] * 4,
        ],
        outs, out_specs, (2,), 30, after,
        streamed=(0, 6, 7, 8, 9), stored=(0, 1, 2, 3, 4),
        scratch=[pltpu.VMEM((half, 2 * width), BF16), *fetched(ups[0])],
    )


def backward_kernel(
    where_ref, normed_ref, gain_ref, shift_ref, grad_ref, second_gain_ref, second_shift_ref,
    pull_ref, up_own, up_near, down_own, down_near, part_ref, part_far_ref, *rest, carried, resident,
):
    (
        final_ref, *out_refs, slope_ref, slope_low_ref, before_ref, sums_ref, part_out_ref
    ) = rest[carried : len(rest) - (0 if resident else 2)]
    scratch = rest[-2:]
    weights = (down_own, up_own, down_near, up_near)
    if resident:
        weight = lambda n: weights[n][...]
    else:
        weight = fetch(weights, *scratch)
    step = pl.program_id(0)
    hidden = normed_ref[...] * gain_ref[...] + shift_ref[...]
    normed, scaled = normalize(hidden + (part_ref[...] + part_far_ref[...]))
    out = (normed * second_gain_ref[...] + second_shift_ref[...]).astype(BF16)
    final_ref[0] = out
    if len(out_refs) == 1:
        out_refs[0][...] = out.astype(F32)
    for index, ref in enumerate(out_refs if len(out_refs) == 2 else ()):

        @pl.when(step == index)
        def _(ref=ref):
            ref[...] = out.astype(F32)

    upstream = grad_ref[0].astype(F32)

    @pl.when(step == 0)
    def _():
        sums_ref[...] = jnp.zeros_like(sums_ref)

    sums_ref[0:1, :] += jnp.sum(upstream * normed, axis=0, keepdims=True)
    sums_ref[1:2, :] += jnp.sum(upstream, axis=0, keepdims=True)
    slope = norm_back(upstream, normed, scaled, second_gain_ref[...])
    slope_ref[...] = slope
    low = slope.astype(BF16)
    slope_low_ref[...] = low
    units = up_own.shape[1]
    parts = []
    for group in range(2):
        columns = slice(group * units, (group + 1) * units)
        before = (dot(low, weight(2 * group), 1, 1) * pull_ref[:, columns]).astype(BF16)
        before_ref[:, columns] = before
        parts.append(dot(before, weight(2 * group + 1), 1, 1))
    part_out_ref[...] = parts[0] + parts[1]


def backward(
    i, where, normed, gain, shift, part, part_far, out_grad, second_gain, second_shift, pull,
    ups, downs, final, after, resident,
):
    count, length, depth = out_grad.shape
    hidden = 2 * ups[0].shape[1]
    half = length // 2
    outs = [
        shape((length, depth), F32),
        shape((length, depth), BF16),
        shape((length, hidden), BF16),
        shape((8, depth), F32),
        shape((length, depth), F32),
    ]
    out_specs = [rows_block(half, o.shape[1]) for o in outs]
    out_specs[3] = whole_block(outs[3])
    halves = 2 if final is None else 1
    value = shape((length // halves, depth), F32)
    outs = [value] * halves + outs
    out_specs = [whole_block(value) if halves == 2 else rows_block(half, depth)] * halves + out_specs
    block = pl.BlockSpec((1, half, depth), lambda g, w: (2 * w[1] + i, g, 0))
    vector = whole_block(gain)
    rows = rows_block(half, depth)
    carried = [] if final is None else [final]
    last = 13
    return launch(
        functools.partial(backward_kernel, carried=len(carried), resident=resident), "backward",
        where,
        (
            normed, gain, shift, out_grad, second_gain, second_shift, pull, *ups, *downs, part,
            part_far, *carried,
        ),
        [
            rows,
            vector,
            vector,
            block,
            vector,
            vector,
            rows_block(half, hidden),
            *[RESIDENT if resident else ANY] * 4,
            rows,
            rows,
            *[ANY] * len(carried),
        ],
        [shape((count, length, depth), BF16), *outs], [block, *out_specs], (2,), 34, after,
        streamed=(3, *(() if resident else (0, *range(6, 11))), *[last] * len(carried)),
        stored=(0, 1 + halves, *(() if resident else (2 + halves, 3 + halves))),
        scratch=() if resident else fetched(ups[0]), aliases={last + 1: 0} if carried else {},
    )


def products_kernel(where_ref, *refs, count, steps, apart):
    def take(number):
        nonlocal refs
        taken, refs = refs[:number], refs[number:]
        return taken

    lows, slopes = take(steps * count), take(steps * count)
    befores, actives = take(count), take(count)
    kept_ref, *sent_refs = refs
    width = kept_ref.shape[3]
    for place, (lefts, rights) in enumerate(((lows, befores), (slopes, actives))):
        for group in range(2):
            columns = slice(group * width, (group + 1) * width)
            total = None
            for n in range(count):
                left = [ref[...] for ref in lefts[steps * n : steps * (n + 1)]]
                left = jnp.concatenate(left, axis=1) if steps > 1 else left[0]
                part = dot(left, rights[n][:, columns], 0, 0)
                total = part if total is None else total + part
            for step in range(steps):
                value = total[step * BLOCK : (step + 1) * BLOCK, :]
                if group == 0:
                    kept_ref[step, place] = value
                elif step == 0 and apart:
                    sent_refs[place][...] = value
                else:
                    sent_refs[step + int(apart)][place] = value


def products(steps, apart, where, lows, slopes, befores, actives, after):
    length, depth = lows[0].shape
    width = befores[0].shape[1] // 2
    count = len(lows)
    tiles, values = [], []
    for way, arrays in enumerate((lows, slopes)):
        for array in arrays:
            for step in steps:
                place = 4 + 2 * step + way
                values.append(array)
                tiles.append(
                    pl.BlockSpec((length, BLOCK), lambda i, w, place=place: (0, w[place]))
                )
    outs = [shape((len(steps), 2, BLOCK, width), F32)]
    outs += [shape((BLOCK, width), F32)] * (2 * int(apart))
    outs += [shape((2, BLOCK, width), F32)] * (len(steps) - int(apart))
    return launch(
        functools.partial(products_kernel, count=count, steps=len(steps), apart=apart), "products",
        where, (*values, *befores, *actives), tiles + [RESIDENT] * (2 * count), outs,
        [whole_block(o) for o in outs], (1,), 24, after, streamed=range(2 * len(steps) * count),
    )


def first_kernel(
    where_ref, part_ref, part_far_ref, slope_ref, normed_ref, scaled_ref, gain_ref,
    wo_ref, one_ref, low_ref, mixed_ref, sums_ref,
):
    step = pl.program_id(0)
    upstream = slope_ref[...] + (part_ref[...] + part_far_ref[...])
    normed = normed_ref[...]

    @pl.when(step == 0)
    def _():
        sums_ref[...] = jnp.zeros_like(sums_ref)

    sums_ref[0:1, :] += jnp.sum(upstream * normed, axis=0, keepdims=True)
    sums_ref[1:2, :] += jnp.sum(upstream, axis=0, keepdims=True)
    slope = norm_back(upstream, normed, scaled_ref[:, 0:1], gain_ref[...])
    one_ref[...] = slope
    low = slope.astype(BF16)
    low_ref[...] = low
    width = mixed_ref.shape[1]
    weights = wo_ref[pl.ds(pl.multiple_of(where_ref[2] * width, width), width), :]
    mixed_ref[...] = dot(low, weights, 1, 1).astype(BF16)


def first(where, part, part_far, slope, normed, scaled, gain, wo, after):
    length, depth = slope.shape
    both = wo.shape[0] // 2
    half = length // 2
    outs = [
        shape((length, depth), F32),
        shape((length, depth), BF16),
        shape((length, both), BF16),
        shape((8, depth), F32),
    ]
    out_specs = [rows_block(half, o.shape[1]) for o in outs]
    out_specs[3] = whole_block(outs[3])
    rows = rows_block(half, depth)
    return launch(
        first_kernel, "first", where, (part, part_far, slope, normed, scaled, gain, wo),
        [rows, rows, rows, rows, rows_block(half, 128), whole_block(gain), RESIDENT],
        outs, out_specs, (2,), 18, after, streamed=(2, 3, 4), stored=(0, 1),
    )


def attend_back_kernel(
    where_ref, qkv_ref, go_ref, sums_ref, seg_ref, weights_ref, out_ref, grads_ref,
    key_slope, value_slope,
):
    width = weights_ref.shape[2] // 3
    owner, _ = lanes(width)
    zero = jnp.zeros((), BF16)
    spares = [spare_columns(seg_ref[0], sums_ref[...], group, width) for group in range(2)]

    def part_of(group, n):
        start = (3 * group + n) * width
        return qkv_ref[0, :, start : start + width]

    def products_of(group, head):
        spare_q, spare_k = spares[group]
        mine = owner == head
        score = dot(
            pick(head, owner, part_of(group, 0), spare_q, zero),
            jnp.where(mine, part_of(group, 1), spare_k), 1, 1,
        )
        upstream = go_ref[:, group * width : (group + 1) * width]
        return score, dot(jnp.where(mine, upstream, zero), part_of(group, 2), 1, 1)

    ahead = products_of(0, 0)
    for group in range(2):
        keys = part_of(group, 1)
        queries_t = part_of(group, 0).T
        upstream_t = go_ref[:, group * width : (group + 1) * width].T
        query_slope = jnp.zeros(keys.shape, F32)
        for head in range(GROUP):
            row = group * GROUP + head
            score, drift = ahead
            if row + 1 < 2 * GROUP:
                ahead = products_of((row + 1) // GROUP, (row + 1) % GROUP)
            place = slice(head * HEAD_DIM, (head + 1) * HEAD_DIM)
            chances = jnp.exp(score)
            slopes = chances * (drift - jnp.sum(drift * chances, axis=-1, keepdims=True))
            slopes = slopes.astype(BF16)
            query_slope = query_slope + dot(slopes, jnp.where(owner == head, keys, zero))
            key_slope[place, :] = dot(queries_t[place, :], slopes)
            value_slope[place, :] = dot(upstream_t[place, :], chances.astype(BF16))
        start = 3 * group * width
        grads_ref[:, start : start + width] = (query_slope * SCALE).astype(BF16)
        grads_ref[:, start + width : start + 2 * width] = key_slope[...].T.astype(BF16)
        grads_ref[:, start + 2 * width : start + 3 * width] = value_slope[...].T.astype(BF16)
        part = dot(grads_ref[:, start : start + 3 * width], weights_ref[group], 1, 1)
        if group == 0:
            out_ref[...] = part
        else:
            out_ref[...] += part


def attend_back(i, where, qkv, go, mixed, seg, weights, after):
    _, length, columns = qkv.shape
    _, depth, width = weights.shape
    outs = [shape((length, depth), F32), shape((length, columns), BF16)]
    return launch(
        attend_back_kernel, "attend_back", where, (qkv, go, mixed, seg, weights),
        [
            whole_block(qkv),
            whole_block(go),
            pl.BlockSpec((8, columns // 3), lambda g, w: (length // 8, 0)),
            sequence(i, (8, length)),
            RESIDENT,
        ],
        outs, [whole_block(o) for o in outs], (1,), 22, after,
        scratch=[pltpu.VMEM((width // 3, length), F32)] * 2, streamed=(0,), stored=(1,),
    )


def total_kernel(where_ref, one_ref, part_ref, far_ref, *rest):
    final_ref, out_ref = rest[-2:]
    final = (one_ref[...] + (part_ref[...] + far_ref[...])).astype(BF16)
    final_ref[0] = final
    out_ref[...] = final.astype(F32)


def total(i, count, where, one, part, far, final, after):
    length, depth = one.shape
    quarter = length // 4
    rows = rows_block(quarter, depth)
    carried = [] if final is None else [final]
    return launch(
        total_kernel, "total", where, (one, part, far, *carried),
        [rows] * 3 + [ANY] * len(carried),
        [shape((count, length, depth), BF16), shape((length, depth), F32)],
        [pl.BlockSpec((1, quarter, depth), lambda g, w: (2 * w[1] + i, g, 0)), rows],
        (4,), 10, after, streamed=(0, 3) if carried else (0,), stored=(0,),
        aliases={4: 0} if carried else {},
    )


def head_products_kernel(where_ref, *refs, count):
    def take(number):
        nonlocal refs
        taken, refs = refs[:number], refs[number:]
        return taken

    def summed(lefts, rights):
        total = None
        for n in range(count):
            left = jnp.concatenate([lefts[2 * n], lefts[2 * n + 1]], axis=1)
            part = dot(left, rights[n], 0, 0)
            total = part if total is None else total + part
        return total

    firsts, seconds, ones = take(2 * count), take(2 * count), take(2 * count)
    grads, mixed, first_sums, second_sums = take(count), take(count), take(2 * count), take(2 * count)
    width = mixed[0].shape[2] // 2
    x_first, x_second = ([ref[0] for ref in group] for group in (firsts, seconds))
    kept_ref, *sent_refs = refs
    for group in range(2):
        start = 3 * group * width
        pairs = [ref[:, start : start + 2 * width] for ref in grads]
        heads = summed(x_first, pairs)
        values = summed(x_second, [ref[:, start + 2 * width : start + 3 * width] for ref in grads])
        outputs = summed(
            [ref[...] for ref in ones], [ref[0, :, group * width : (group + 1) * width] for ref in mixed]
        )
        for step in range(2):
            rows = slice(step * BLOCK, (step + 1) * BLOCK)
            out = sent_refs[step] if group else kept_ref.at[step]
            out[0:BLOCK, :] = heads[rows, 0:width]
            out[BLOCK : 2 * BLOCK, :] = heads[rows, width:]
            out[2 * BLOCK : 3 * BLOCK, :] = values[rows, :]
            out[3 * BLOCK : 4 * BLOCK, :] = outputs[rows, :]
            out[4 * BLOCK :, :] = jnp.zeros((8, width), F32)
            for row, sums in ((0, first_sums), (2, second_sums)):
                gains = sums[step][0:2, :]
                for n in range(1, count):
                    gains = gains + sums[2 * n + step][0:2, :]
                last = 4 * BLOCK + row
                out[last : last + 2, 0:BLOCK] = gains


def head_products(pair, where, x, ones, grads, mixed, firsts, seconds, after):
    _, length, depth = x.shape
    count = len(ones)
    width = mixed[0].shape[2] // 2

    def tile(way, step, dims, lead=()):
        return pl.BlockSpec(
            (*dims, BLOCK),
            lambda j, w: (*[f(w) for f in lead], 0, w[4 + 2 * (2 * pair + step) + way]),
        )

    def inputs_of(way):
        return [
            tile(way, step, (1, length), (lambda w, i=i: 2 * w[1] + i,))
            for i in range(count) for step in range(2)
        ]

    out = shape((4 * BLOCK + 8, width), F32)
    outs = [shape((2, *out.shape), F32), out, out]
    twice = lambda arrays: [a for a in arrays for _ in range(2)]
    return launch(
        functools.partial(head_products_kernel, count=count), "head_products", where,
        (
            *[x] * (4 * count), *twice(ones), *grads, *mixed, *twice(firsts), *twice(seconds)
        ),
        inputs_of(0) + inputs_of(1) + [tile(1, step, (length,)) for _ in ones for step in range(2)]
        + [RESIDENT] * (2 * count)
        + [tile(1, step, (8,)) for _ in range(2 * count) for step in range(2)],
        outs, [whole_block(o) for o in outs], (1,), 12, after, streamed=range(6 * count),
    )


def ring_kernel(where_ref, *refs, arrivals, sizes):
    outs = refs[-2:]
    sources = refs[arrivals : -2]
    for way in range(2):
        mine, start = [], 0
        count = sizes[way]
        kept = sources[way * sizes[0] : way * sizes[0] + count]
        base = sizes[0] + sizes[1]
        near = sources[base + way * sizes[0] : base + way * sizes[0] + count]
        for left, right in zip(kept, near):
            value = left[...].reshape(left.shape[-2:]) + right[...].reshape(right.shape[-2:])
            rows = slice(start, start + value.shape[0])
            if arrivals:
                value = refs[way][rows, :] + value
            outs[way][rows, :] = value
            start += value.shape[0]


def ring_step(where, arrived, kept, near, after):
    entries = [*kept[0], *kept[1], *near[0], *near[1]]
    specs = [whole_block(a) for a in arrived]
    specs += [pl.BlockSpec(dims, lambda i, w, at=at: at) for _, dims, at in entries]
    outs = [
        shape((sum(e[1][-2] for e in way), way[0][1][-1]), F32) for way in kept
    ]
    return launch(
        functools.partial(ring_kernel, arrivals=len(arrived), sizes=(len(kept[0]), len(kept[1]))),
        "ring_step", where, (*arrived, *[e[0] for e in entries]), specs, outs,
        [whole_block(o) for o in outs], (1,), 8, after,
    )


def turn_kernel(where_ref, value_ref, out_ref):
    out_ref[...] = value_ref[...].T


def turn(where, value, after):
    out = shape(value.shape[::-1], F32)
    return launch(
        turn_kernel, "turn", where, (value,), [whole_block(value)], [out], [whole_block(out)],
        (1,), 6, after, stored=(0,),
    )[0]


def hold_kernel(where_ref, *refs):
    *pairs, arrived = refs
    count = len(pairs) // 2
    copies = [
        pltpu.make_async_copy(pairs[n], pairs[count + n], arrived.at[n]) for n in range(count)
    ]
    for copy in copies:
        copy.start()
    for copy in copies:
        copy.wait()


def hold(where, *values, after):
    count = len(values)
    token = shape((8, 128), F32)

    def run(where_ref, *refs):
        refs[2 * count][...] = jnp.zeros((8, 128), F32)
        hold_kernel(where_ref, *refs[: 2 * count], refs[-1])

    return launch(
        run, "hold", where, values, [ANY] * count,
        [*[pltpu.VMEM(v.shape, v.dtype) for v in values], token],
        [*[RESIDENT] * count, whole_block(token)], (1,), 4, after, streamed=range(count),
        scratch=[pltpu.SemaphoreType.DMA((count,))],
    )[:count]


def clip_kernel(where_ref, query_ref, key_ref, factor_ref, query_out, key_out):
    query_out[...] = query_ref[...].astype(F32) * factor_ref[...]
    key_out[...] = key_ref[...].astype(F32) * factor_ref[...]


def clip(where, query, key, factor, after):
    specs = [rows_block(query.shape[0] // 4, query.shape[1])] * 2
    return launch(
        clip_kernel, "clip", where, (query, key, factor), [*specs, whole_block(factor)],
        [shape(query.shape, F32)] * 2, specs, (4,), 8, after, streamed=(0, 1), stored=(0, 1),
    )


def finish_kernel(where_ref, *refs):
    *halves, final_ref, out_ref, token_ref = refs
    del final_ref
    value = halves[0][...].reshape(out_ref.shape[1:])
    if len(halves) == 2:
        value = jnp.where(pl.program_id(0) == 0, value, halves[1][...])
    out_ref[0] = value.astype(BF16)
    token_ref[...] = jnp.zeros_like(token_ref)


def finish(i, where, values, final, after):
    half, depth = final.shape[1] // 2, final.shape[2]
    specs = [rows_block(half, depth)]
    if len(values) == 2:
        specs = [whole_block(v) for v in values]
    last = len(values)
    token = shape((8, 128), F32)
    return launch(
        finish_kernel, "finish", where, (*values, final), [*specs, ANY],
        [shape(final.shape, BF16), token],
        [
            pl.BlockSpec((1, half, depth), lambda g, w: (2 * (1 - w[1]) + i, g, 0)),
            whole_block(token),
        ],
        (2,), 10, after, aliases={last + 1: 0}, stored=(0,), streamed=(last,),
    )[0]


def solution(mesh):
    ranks = mesh.shape["dp"]
    group = mesh.shape["tensor"]
    assert group == 4 and ranks % 8 == 0
    near_pairs = [(t, t ^ 1) for t in range(group)]
    far_pairs = [(t, t ^ 2) for t in range(group)]
    turns = (
        [(RING[p], RING[(p + 1) % 8]) for p in range(8)],
        [(RING[p], RING[(p - 1) % 8]) for p in range(8)],
    )

    def near(value):
        return lax.ppermute(value, "tensor", near_pairs)

    def scatter(value):
        return lax.psum_scatter(value, "dp", scatter_dimension=0, tiled=True)

    def far(value):
        return lax.ppermute(value, "tensor", far_pairs)

    def body(
        block_input, segment_ids, query_weight, key_weight, value_weight, output_weight,
        first_gain, first_shift, up_weight, down_weight, second_gain, second_shift, out_grad,
    ):
        count, length, depth = block_input.shape
        width = query_weight.shape[1]
        part = depth // ranks
        mine = range(count // 2)
        me = lax.axis_index("tensor")
        rank = lax.axis_index("dp")
        natural = [n for n in range(8) for _ in range(2)]
        owners = jnp.asarray(OWNERS if ranks == 8 else [natural], jnp.int32)
        owners = lax.dynamic_index_in_dim(owners, rank if ranks == 8 else 0, 0, False)
        where = jnp.concatenate(
            [jnp.stack([me, me % 2, me // 2, rank]).astype(jnp.int32), owners]
        )
        seg = jnp.broadcast_to(segment_ids[:, None, :], (count, 8, length))
        gain_one, shift_one = first_gain[None], first_shift[None]
        gain_two, shift_two = second_gain[None], second_shift[None]
        order = Order()

        def then(call, *args, **kwargs):
            return call(*args, after=order, **kwargs)

        own_low, own_wide, wo_half = then(
            widen_heads, where, query_weight, key_weight, value_weight, output_weight
        )
        near_wide, wo_first = near(own_wide), far(wo_half)
        wide = convert(where, up_weight, down_weight, dtype=F32, after=Order())
        wide_near = [near(w) for w in wide]
        weights, wo_near = then(narrow_near, where, own_low, near_wide, output_weight)
        heads, mixed_far = [], []
        for i in mine:
            heads.append(then(attend, i, where, block_input, weights, seg))
            mixed_far.append(far(heads[i][3]))
            if i == 0:
                (wo_first,) = then(gate, where, wo_first)
                wo_second = lax.ppermute(wo_first, "dp", [(r, r ^ 1) for r in range(ranks)])
                wo_both = [near(wo_first)]
        mixed_low, qkv, tops, mixed = zip(*heads)
        up_near, down_near = then(convert, where, *wide_near, dtype=BF16)
        ups, downs = (up_weight, up_near), (down_weight, down_near)
        (wo_second,) = then(gate, where, wo_second)
        wo_both.append(near(wo_second))
        wo = then(assemble, where, output_weight, wo_near, (wo_first, wo_second), wo_both)

        forwards, part_far = [], []
        for i in mine:
            forwards.append(
                then(
                    forward, i, where, block_input, mixed[i], mixed_far[i], wo, gain_one,
                    shift_one, ups, downs,
                )
            )
            part_far.append(far(forwards[i][5]))

        heads_own = width // HEAD_DIM
        peak = functools.reduce(jnp.maximum, tops)
        peak = jnp.maximum(peak[:heads_own], near(peak)[heads_own:])
        step = 1
        while step < ranks:
            peak = jnp.maximum(peak, lax.ppermute(peak, "dp", [(i, i ^ step) for i in range(ranks)]))
            step *= 2
        factor = jnp.sqrt(CLIP / jnp.maximum(peak[:, 0], CLIP))
        factor = jnp.repeat(factor, HEAD_DIM)[None]
        query_clipped, key_clipped = then(clip, where, query_weight, key_weight, factor)

        written = {"layer_out": None, "input_grad": None}
        def finish_layer(i, values):
            written["layer_out"] = then(finish, i, where, values, written["layer_out"])

        backs, slope_parts, slope_far = [], [], []
        for i in mine:
            normed, scaled, low, active, pull, part_sum = forwards[i]
            weights_of = ups, downs
            if i > 0:
                normed, pull, *held = then(hold, where, normed, pull, *ups, *downs)
                weights_of = held[0:2], held[2:4]
            backs.append(
                then(
                    backward, i, where, normed, gain_one, shift_one, part_sum, part_far[i],
                    out_grad, gain_two, shift_two, pull, *weights_of, written["layer_out"],
                    resident=i > 0,
                )
            )
            written["layer_out"], *out, slope, slope_low, before, sums, part_sum = backs[i]
            backs[i] = (out, slope, slope_low, before, sums)
            slope_parts.append(part_sum)
            slope_far.append(far(part_sum))
            if i == 0:
                finish_layer(0, [near(v) for v in out])

        lows, actives = [f[2] for f in forwards], [f[3] for f in forwards]
        slope_lows, befores = [b[2] for b in backs], [b[3] for b in backs]
        def send(held):
            return [lax.ppermute(h, "dp", t) for h, t in zip(held, turns)]

        ff_blocks = {}

        def ff_part(*steps, apart=True):
            kept, *sent = then(products, steps, apart, where, lows, slope_lows, befores, actives)
            sent = [near(a) for a in sent]
            for index, n in enumerate(steps):
                mine = sent[:2] if index == 0 and apart else sent[index + int(apart)]
                ff_blocks[n] = (kept, index, mine)

        def ff_step(n, arrived):
            kept, index, sent = ff_blocks[n]
            dims = (1, 1, BLOCK, kept.shape[3])
            if isinstance(sent, list):
                near = [[(array, dims[2:], (0, 0))] for array in sent]
            else:
                near = [[(sent, dims[1:], (way, 0, 0))] for way in range(2)]
            return then(
                ring_step, where, arrived,
                [[(kept, dims, (index, way, 0, 0))] for way in range(2)], near,
            )

        def ff_ring():
            held = ff_step(0, ())
            for n in range(1, 8):
                arrived = send(held)
                yield None
                held = ff_step(n, arrived)
            yield held

        head_parts = []

        def head_part(pair):
            kept, *sent = then(
                head_products, pair, where, block_input, [f[1] for f in firsts],
                [o[1] for o in owns], mixed_low, [f[3] for f in firsts], [b[4] for b in backs],
            )
            head_parts.append((kept, [near(a) for a in sent]))

        def head_step(n, arrived):
            kept, sent = head_parts[n // 2]

            def entries(array, lead):
                block = lambda rows, at: (
                    array, (*[1 for _ in lead], rows, width), (*lead, at, 0)
                )
                return [[block(2 * BLOCK, 0)], [block(2 * BLOCK, 1), block(8, 4 * BLOCK // 8)]]

            return then(
                ring_step, where, arrived, entries(kept, (n % 2,)), entries(sent[n % 2], ())
            )

        def head_ring():
            held = head_step(0, ())
            for n in range(1, 8):
                arrived = send(held)
                yield None
                held = head_step(n, arrived)
            yield held

        def total_input(i):
            written["input_grad"], result = then(
                total, i, count, where, firsts[i][0], owns[i][0], input_far[i],
                written["input_grad"],
            )
            return result

        def finish_input(i, value):
            written["input_grad"] = then(finish, i, where, [value], written["input_grad"])

        def first_back(i):
            firsts.append(
                then(
                    first, where, slope_parts[i], slope_far[i], backs[i][1], *forwards[i][:2],
                    gain_one, wo,
                )
            )

        def own_back(i):
            owns.append(then(attend_back, i, where, qkv[i], firsts[i][2], mixed[i], seg, weights))

        firsts, owns, input_far = [], [], []
        ring = ff_ring() if ranks == 8 else iter(())
        ff_part(0)
        ff_part(1, 2)
        next(ring, None)
        next(ring, None)
        ff_part(3, 4)
        first_back(0)
        next(ring, None)
        own_back(0)
        next(ring, None)
        ff_part(5, 6, 7)
        next(ring, None)
        slope_far[1], own_part = then(gate, where, slope_far[1], owns[0][0])
        owns[0] = (own_part, owns[0][1])
        input_far.append(far(own_part))
        first_back(1)
        next(ring, None)
        own_back(1)
        next(ring, None)
        head_part(0)
        head_part(1)
        head_part(2)
        if ranks == 8:
            *_, (up_grad, down_grad) = ring
        (own_part,) = then(gate, where, owns[1][0])
        owns[1] = (own_part, owns[1][1])
        input_far.append(far(own_part))
        ring = head_ring() if ranks == 8 else iter(())
        next(ring, None)
        head_part(3)
        next(ring, None)
        next(ring, None)
        rows = total_input(0)
        next(ring, None)
        (rows,) = then(gate, where, rows)
        rows = near(rows)
        next(ring, None)
        if ranks == 8:
            down_grad = then(turn, where, down_grad)
        next(ring, None)
        result = total_input(1)
        next(ring, None)
        result, layer = then(gate, where, result, *backs[1][0])
        result, layer = near(result), near(layer)
        finish_input(0, rows)
        finish_input(1, result)
        finish_layer(1, [layer])

        if ranks == 8:
            *_, (left, right) = ring
            query_grad, key_grad = left[:BLOCK], left[BLOCK:]
            value_grad, output_grad = right[:BLOCK], right[BLOCK : 2 * BLOCK].T
            gains = right[2 * BLOCK : 2 * BLOCK + 4, :BLOCK]
        else:
            def rows_of(value, start, rows=BLOCK):
                return scatter(value[:, start : start + rows].reshape(8 * rows, width))

            up, down = [
                jnp.concatenate(
                    [kept[at, way] + sent[way] for kept, at, sent in map(ff_blocks.get, range(8))],
                    axis=0,
                )
                for way in range(2)
            ]
            up_grad, down_grad = scatter(up), scatter(down).T
            value = jnp.concatenate([k + jnp.stack(s) for k, s in head_parts], axis=0)
            query_grad, key_grad, value_grad = (rows_of(value, n * BLOCK) for n in range(3))
            output_grad = rows_of(value, 3 * BLOCK).T
            gains = value[:, 4 * BLOCK : 4 * BLOCK + 4, :BLOCK].transpose(0, 2, 1)
            gains = scatter(gains.reshape(depth, 4)).T

        return (
            written["layer_out"], written["input_grad"], query_grad, key_grad, value_grad, output_grad,
            gains[0], gains[1], up_grad, down_grad, gains[2], gains[3],
            query_clipped, key_clipped,
        )

    batch = P("dp", None, None)
    in_specs = (
        batch, P("dp", None), P(None, "tensor"), P(None, "tensor"), P(None, "tensor"),
        P("tensor", None), P(), P(), P(None, "tensor"), P("tensor", None), P(), P(), batch,
    )
    out_specs = (
        batch, batch, P("dp", "tensor"), P("dp", "tensor"), P("dp", "tensor"), P("tensor", "dp"),
        P("dp"), P("dp"), P("dp", "tensor"), P("tensor", "dp"), P("dp"), P("dp"),
        P(None, "tensor"), P(None, "tensor"),
    )
    return jax.shard_map(body, mesh=mesh, in_specs=in_specs, out_specs=out_specs, check_vma=False)
```

```python
import functools

import jax
import jax.numpy as jnp
from jax import lax
from jax.experimental import pallas as pl
from jax.experimental.pallas import tpu as pltpu
from jax.sharding import PartitionSpec as P

F32 = jnp.float32
BF16 = jnp.bfloat16
HEAD_DIM = 64
FAR = -1e30
EPS = 1e-06
CLIP = 10.0
SCALE = HEAD_DIM**-0.5
ROOT_HALF = 0.5**0.5
BELL = 0.3989422804014327
GROUP = 4
BLOCK = 128
DOCS = 4
MIB = 1 << 20
RING = (0, 2, 4, 6, 7, 5, 3, 1)
OWNERS = tuple(
    tuple(RING[(RING.index(r) + way * (1 + n)) % 8] for n in range(8) for way in (-1, 1))
    for r in range(8)
)
ANY = pl.BlockSpec(memory_space=pl.ANY)
RESIDENT = pl.BlockSpec(memory_space=pltpu.VMEM)


def dot(left, right, left_dim=1, right_dim=0):
    return lax.dot_general(
        left, right, (((left_dim,), (right_dim,)), ((), ())), preferred_element_type=F32
    )


def normalize(total):
    average = jnp.mean(total, axis=-1, keepdims=True)
    centred = total - average
    variance = jnp.mean(centred * centred, axis=-1, keepdims=True)
    scaled = lax.rsqrt(variance + EPS)
    return centred * scaled, scaled


def norm_back(upstream, normed, scaled, gain):
    weighted = upstream * gain
    first = jnp.mean(weighted, axis=-1, keepdims=True)
    second = jnp.mean(weighted * normed, axis=-1, keepdims=True)
    return scaled * (weighted - first - normed * second)


def lanes(width):
    lane = lax.broadcasted_iota(jnp.int32, (1, width), 1)
    return lane // HEAD_DIM, lane % HEAD_DIM


def split(value):
    high = value.astype(BF16)
    rest = value - high.astype(F32)
    middle = rest.astype(BF16)
    return high, middle, (rest - middle.astype(F32)).astype(BF16)


def pick(head, owner, own, spare, zero):
    return jnp.where(owner == head, own, jnp.where(owner == (head + 1) % GROUP, spare, zero))


def spare_columns(seg_rows, sums, group, width):
    owner, lane = lanes(width)
    row8 = lax.broadcasted_iota(jnp.int32, (8, 1), 0)
    equal = jnp.where(seg_rows == row8, 1.0, 0.0)
    rows = [equal]
    wanted = [jnp.where(lane == row8, FAR, 0.0)]
    if sums is not None:
        head = row8 % GROUP
        here = (row8 // GROUP == group) & ((head + 1) % GROUP == owner)
        for n, value in enumerate(split(sums)):
            rows.append(value.astype(F32))
            wanted.append(jnp.where(here & (lane == DOCS + n), -1.0, 0.0))
    placed = jnp.concatenate(wanted, axis=0).astype(BF16)
    queries = dot(jnp.concatenate(rows, axis=0).astype(BF16), placed, 0, 0).astype(BF16)
    ones = jnp.where((lane >= DOCS) & (lane < DOCS + 3), 1.0, 0.0)
    placed = jnp.where((lane == row8) & (row8 < DOCS), 1.0, 0.0).astype(BF16)
    differ = jnp.where(seg_rows == row8, 0.0, 1.0).astype(BF16)
    keys = (dot(differ, placed, 0, 0) + ones).astype(BF16)
    return queries, keys


def shape(dims, dtype):
    return jax.ShapeDtypeStruct(tuple(dims), dtype)


def whole_block(array):
    zeros = (0,) * len(array.shape)
    return pl.BlockSpec(tuple(array.shape), lambda i, w: zeros)


def rows_block(rows, columns):
    return pl.BlockSpec((rows, columns), lambda i, w: (i, 0))


class Order:
    def __init__(self):
        self.token, self.stored = None, False

    def taken(self):
        if self.token is None:
            return []
        if self.stored:
            return [pltpu.with_memory_space_constraint(self.token, pltpu.HBM)]
        return [self.token]

    def give(self, results, stored):
        sizes = [r.size * jnp.dtype(r.dtype).itemsize for r in results]
        index = sizes.index(min(sizes))
        self.token, self.stored = results[index], index in stored


def launch(
    kernel, name, where, inputs, in_specs, outs, out_specs, grid, vmem, after,
    scratch=(), aliases=None, streamed=(), stored=(),
):
    count = len(inputs)
    tokens = after.taken()
    inputs = [
        pltpu.with_memory_space_constraint(value, pltpu.HBM) if i in streamed else value
        for i, value in enumerate(inputs)
    ]
    outs = [
        pltpu.HBM(value.shape, value.dtype) if i in stored else value
        for i, value in enumerate(outs)
    ]

    def run(where_ref, *refs):
        kernel(where_ref, *refs[:count], *refs[count + len(tokens) :])

    results = pl.pallas_call(
        run,
        grid_spec=pltpu.PrefetchScalarGridSpec(
            num_scalar_prefetch=1,
            grid=grid,
            in_specs=list(in_specs) + [ANY] * len(tokens),
            out_specs=list(out_specs),
            scratch_shapes=list(scratch),
        ),
        out_shape=outs,
        input_output_aliases=aliases or {},
        compiler_params=pltpu.CompilerParams(
            vmem_limit_bytes=vmem * MIB, dimension_semantics=("arbitrary",) * len(grid)
        ),
        cost_estimate=pl.CostEstimate(flops=1, bytes_accessed=1, transcendentals=0),
        name=name,
    )(where, *inputs, *tokens)
    after.give(results, stored)
    return results


def gate_kernel(*refs):
    del refs


def gate(where, *values, after):
    outs = [shape(v.shape, v.dtype) for v in values]
    return launch(
        gate_kernel, "gate", where, values, [ANY] * len(values), outs, [ANY] * len(values), (1,),
        2, after, aliases={i + 1: i for i in range(len(values))},
    )


def widen_heads_kernel(where_ref, wq_ref, wk_ref, wv_ref, wo_ref, own, wide, wo):
    width = wq_ref.shape[1]
    for index, ref in enumerate((wq_ref, wk_ref, wv_ref)):
        columns = slice(index * width, (index + 1) * width)
        value = ref[...]
        own[:, columns] = value
        wide[:, columns] = value.astype(F32)
    rows, depth = wo_ref.shape
    for index in range(depth // width):
        wide[index * rows : (index + 1) * rows, 3 * width :] = wo_ref[
            :, index * width : (index + 1) * width
        ].astype(F32)
    half = rows // 2
    wo[...] = wo_ref[pl.ds(pl.multiple_of((where_ref[3] % 2) * half, half), half), :].astype(F32)


def widen_heads(where, wq, wk, wv, wo, after):
    depth, width = wq.shape
    outs = [
        shape((depth, 3 * width), BF16),
        shape((depth, 4 * width), F32),
        shape((wo.shape[0] // 2, depth), F32),
    ]
    inputs = (wq, wk, wv, wo)
    return launch(
        widen_heads_kernel, "widen_heads", where, inputs, [whole_block(a) for a in inputs], outs,
        [whole_block(o) for o in outs], (1,), 12, after, streamed=range(4),
    )


def assemble_kernel(where_ref, own_ref, near_ref, *refs):
    *halves, out_ref = refs
    rows = own_ref.shape[0]
    half = rows // 2
    mine = where_ref[2] * 2 * rows
    other = (1 - where_ref[2]) * 2 * rows
    out_ref[pl.ds(pl.multiple_of(mine, rows), rows), :] = own_ref[...]
    out_ref[pl.ds(pl.multiple_of(mine + rows, rows), rows), :] = near_ref[...]
    parity = where_ref[3] % 2
    for start, first, second in ((other, *halves[0:2]), (other + rows, *halves[2:4])):
        for ref, place in ((first, parity), (second, 1 - parity)):
            begin = pl.multiple_of(start + place * half, half)
            out_ref[pl.ds(begin, half), :] = ref[...].astype(BF16)


def assemble(where, own, near, far, both, after):
    rows, columns = own.shape
    out = shape((4 * rows, columns), BF16)
    inputs = (own, near, *far, *both)
    return launch(
        assemble_kernel, "assemble", where, inputs, [whole_block(a) for a in inputs], [out],
        [whole_block(out)], (1,), 14, after,
    )[0]


def narrow_near_kernel(where_ref, own_ref, wide_ref, heads_ref, wo_ref):
    width = own_ref.shape[1] // 3
    heads_ref[0] = own_ref[...]
    heads_ref[1] = wide_ref[:, 0 : 3 * width].astype(BF16)
    rows, depth = wo_ref.shape
    for index in range(depth // width):
        wo_ref[:, index * width : (index + 1) * width] = wide_ref[
            index * rows : (index + 1) * rows, 3 * width :
        ].astype(BF16)


def narrow_near(where, own, wide, wo, after):
    outs = [shape((2, *own.shape), BF16), shape(wo.shape, BF16)]
    return launch(
        narrow_near_kernel, "narrow_near", where, (own, wide),
        [whole_block(own), whole_block(wide)], outs, [whole_block(o) for o in outs], (1,), 16,
        after,
    )


def convert_kernel(where_ref, *refs):
    half = len(refs) // 2
    for source, target in zip(refs[:half], refs[half:]):
        target[...] = source[...].astype(target.dtype)


def convert(where, *values, dtype, after):
    specs = [rows_block(v.shape[0] // 4, v.shape[1]) for v in values]
    held = range(len(values))
    wide = dtype == F32
    return launch(
        convert_kernel, "convert", where, values, specs, [shape(v.shape, dtype) for v in values],
        specs, (4,), 10, after, streamed=held if wide else (), stored=() if wide else held,
    )


def project_group(x, weights):
    width = weights.shape[1] // 3
    q = (dot(x, weights[:, 0:width]).astype(BF16) * SCALE).astype(BF16)
    k = dot(x, weights[:, width : 2 * width]).astype(BF16)
    v = dot(x, weights[:, 2 * width : 3 * width]).astype(BF16)
    return q, k, v


def attend_kernel(
    where_ref, x_ref, weights_ref, seg_ref, low_ref, qkv_ref, top_ref, o_ref, held_ref
):
    x = x_ref[0]
    width = weights_ref.shape[2] // 3
    owner, _ = lanes(width)
    spare_q, spare_k = spare_columns(seg_ref[0], None, 0, width)
    zero = jnp.zeros((), BF16)
    held_ref[...] = jnp.zeros_like(held_ref)
    groups = [project_group(x, weights_ref.at[group]) for group in range(2)]
    for group, values in enumerate(groups):
        for index, value in enumerate(values):
            start = (3 * group + index) * width
            qkv_ref[0, :, start : start + width] = value

    def scores_of(group, head):
        queries, keys, _ = groups[group]
        return dot(
            pick(head, owner, queries, spare_q, zero),
            jnp.where(owner == head, keys, spare_k), 1, 1,
        )

    for group in range(2):
        total = jnp.zeros(groups[group][0].shape, F32)
        for head in range(GROUP):
            row = group * GROUP + head
            scores = scores_of(group, head)
            top = jnp.max(scores, axis=-1, keepdims=True)
            raised = jnp.exp(scores - top)
            summed = jnp.sum(raised, axis=-1, keepdims=True)
            chances = raised * (1.0 / summed)
            total = total + dot(
                chances.astype(BF16), jnp.where(owner == head, groups[group][2], zero)
            )
            held_ref[:, row : row + 1] = top + jnp.log(summed)
            top_ref[row : row + 1, :] = jnp.broadcast_to(
                jnp.max(top, axis=0, keepdims=True), (1, top_ref.shape[1])
            )
        low = total.astype(BF16)
        low_ref[0, :, group * width : (group + 1) * width] = low
        o_ref[0 : x.shape[0], group * width : (group + 1) * width] = low.astype(F32)
    o_ref[x.shape[0] :, :] = held_ref[...].T[0:8, :]


def sequence(i, dims):
    return pl.BlockSpec((1, *dims), lambda g, w: (2 * w[1] + i, 0, 0))


def attend(i, where, x, weights, seg, after):
    _, length, depth = x.shape
    columns = weights.shape[2]
    width = columns // 3
    outs = [
        shape((1, length, 2 * width), BF16),
        shape((1, length, 2 * columns), BF16),
        shape((2 * GROUP, 128), F32),
        shape((length + 2 * GROUP, 2 * width), F32),
    ]
    out_specs = [whole_block(o) for o in outs]
    return launch(
        attend_kernel, "attend", where, (x, weights, seg),
        [sequence(i, (length, depth)), RESIDENT, sequence(i, (8, length))],
        outs, out_specs, (1,), 20, after, streamed=(0,), stored=(0, 1),
        scratch=[pltpu.VMEM((length, 128), F32)],
    )


def fetch(sources, held_ref, arrived):
    first = pl.program_id(0) == 0
    copies = [
        pltpu.make_async_copy(source, held_ref.at[n], arrived.at[n])
        for n, source in enumerate(sources)
    ]

    @pl.when(first)
    def _():
        for copy in copies:
            copy.start()

    def get(n):
        @pl.when(first)
        def _():
            copies[n].wait()

        return held_ref[n]

    return get


def forward_kernel(
    where_ref, x_ref, mixed_ref, mixed_far_ref, wo_ref, gain_ref,
    shift_ref, up_own, up_near, down_own, down_near,
    normed_ref, scaled_ref, low_ref, active_ref, pull_ref, part_ref, both_ref, held_ref, arrived,
):
    weight = fetch((up_own, down_own, up_near, down_near), held_ref, arrived)
    width = mixed_ref.shape[1]
    chip = where_ref[2]
    both_ref[:, pl.ds(pl.multiple_of(chip * width, width), width)] = mixed_ref[...].astype(BF16)
    both_ref[:, pl.ds(pl.multiple_of((1 - chip) * width, width), width)] = mixed_far_ref[
        ...
    ].astype(BF16)
    normed, scaled = normalize(x_ref[0].astype(F32) + dot(both_ref[...], wo_ref[...]))
    normed_ref[...] = normed
    scaled_ref[...] = jnp.broadcast_to(scaled, scaled_ref.shape)
    low = (normed * gain_ref[...] + shift_ref[...]).astype(BF16)
    low_ref[...] = low
    hidden = up_own.shape[1]
    parts = []
    for group in range(2):
        columns = slice(group * hidden, (group + 1) * hidden)
        before = dot(low, weight(2 * group))
        chance = 0.5 * (1.0 + lax.erf(before * ROOT_HALF))
        active = (before * chance).astype(BF16)
        active_ref[:, columns] = active
        pull_ref[:, columns] = chance + before * (jnp.exp(-0.5 * before * before) * BELL)
        parts.append(dot(active, weight(2 * group + 1)))
    part_ref[...] = parts[0] + parts[1]


def fetched(array):
    return [pltpu.VMEM((4, *array.shape), array.dtype), pltpu.SemaphoreType.DMA((4,))]


def forward(i, where, x, mixed, mixed_far, wo, gain, shift, ups, downs, after):
    _, length, depth = x.shape
    width = mixed.shape[1]
    hidden = 2 * ups[0].shape[1]
    half = length // 2
    pieces = rows_block(half, width)
    outs = [
        shape((length, depth), F32),
        shape((length, 128), F32),
        shape((length, depth), BF16),
        shape((length, hidden), BF16),
        shape((length, hidden), F32),
    ]
    out_specs = [rows_block(half, o.shape[1]) for o in outs]
    outs.append(shape((length, depth), F32))
    out_specs.append(rows_block(half, depth))
    return launch(
        forward_kernel, "forward", where, (x, mixed, mixed_far, wo, gain, shift, *ups, *downs),
        [
            pl.BlockSpec((1, half, depth), lambda g, w: (2 * w[1] + i, g, 0)),
            pieces,
            pieces,
            RESIDENT,
            whole_block(gain),
            whole_block(shift),
            *[ANY] * 4,
        ],
        outs, out_specs, (2,), 30, after,
        streamed=(0, 6, 7, 8, 9), stored=(0, 1, 2, 3, 4),
        scratch=[pltpu.VMEM((half, 2 * width), BF16), *fetched(ups[0])],
    )


def backward_kernel(
    where_ref, normed_ref, gain_ref, shift_ref, grad_ref, second_gain_ref, second_shift_ref,
    pull_ref, up_own, up_near, down_own, down_near, part_ref, part_far_ref, *rest, carried, resident,
):
    (
        final_ref, *out_refs, slope_ref, slope_low_ref, before_ref, sums_ref, part_out_ref
    ) = rest[carried : len(rest) - (0 if resident else 2)]
    scratch = rest[-2:]
    weights = (down_own, up_own, down_near, up_near)
    if resident:
        weight = lambda n: weights[n][...]
    else:
        weight = fetch(weights, *scratch)
    step = pl.program_id(0)
    hidden = normed_ref[...] * gain_ref[...] + shift_ref[...]
    normed, scaled = normalize(hidden + (part_ref[...] + part_far_ref[...]))
    out = (normed * second_gain_ref[...] + second_shift_ref[...]).astype(BF16)
    final_ref[0] = out
    if len(out_refs) == 1:
        out_refs[0][...] = out.astype(F32)
    for index, ref in enumerate(out_refs if len(out_refs) == 2 else ()):

        @pl.when(step == index)
        def _(ref=ref):
            ref[...] = out.astype(F32)

    upstream = grad_ref[0].astype(F32)

    @pl.when(step == 0)
    def _():
        sums_ref[...] = jnp.zeros_like(sums_ref)

    sums_ref[0:1, :] += jnp.sum(upstream * normed, axis=0, keepdims=True)
    sums_ref[1:2, :] += jnp.sum(upstream, axis=0, keepdims=True)
    slope = norm_back(upstream, normed, scaled, second_gain_ref[...])
    slope_ref[...] = slope
    low = slope.astype(BF16)
    slope_low_ref[...] = low
    units = up_own.shape[1]
    parts = []
    for group in range(2):
        columns = slice(group * units, (group + 1) * units)
        before = (dot(low, weight(2 * group), 1, 1) * pull_ref[:, columns]).astype(BF16)
        before_ref[:, columns] = before
        parts.append(dot(before, weight(2 * group + 1), 1, 1))
    part_out_ref[...] = parts[0] + parts[1]


def backward(
    i, where, normed, gain, shift, part, part_far, out_grad, second_gain, second_shift, pull,
    ups, downs, final, after, resident,
):
    count, length, depth = out_grad.shape
    hidden = 2 * ups[0].shape[1]
    half = length // 2
    outs = [
        shape((length, depth), F32),
        shape((length, depth), BF16),
        shape((length, hidden), BF16),
        shape((8, depth), F32),
        shape((length, depth), F32),
    ]
    out_specs = [rows_block(half, o.shape[1]) for o in outs]
    out_specs[3] = whole_block(outs[3])
    halves = 2 if final is None else 1
    value = shape((length // halves, depth), F32)
    outs = [value] * halves + outs
    out_specs = [whole_block(value) if halves == 2 else rows_block(half, depth)] * halves + out_specs
    block = pl.BlockSpec((1, half, depth), lambda g, w: (2 * w[1] + i, g, 0))
    vector = whole_block(gain)
    rows = rows_block(half, depth)
    carried = [] if final is None else [final]
    last = 13
    return launch(
        functools.partial(backward_kernel, carried=len(carried), resident=resident), "backward",
        where,
        (
            normed, gain, shift, out_grad, second_gain, second_shift, pull, *ups, *downs, part,
            part_far, *carried,
        ),
        [
            rows,
            vector,
            vector,
            block,
            vector,
            vector,
            rows_block(half, hidden),
            *[RESIDENT if resident else ANY] * 4,
            rows,
            rows,
            *[ANY] * len(carried),
        ],
        [shape((count, length, depth), BF16), *outs], [block, *out_specs], (2,), 34, after,
        streamed=(3, *(() if resident else (0, *range(6, 11))), *[last] * len(carried)),
        stored=(0, 1 + halves, *(() if resident else (2 + halves, 3 + halves))),
        scratch=() if resident else fetched(ups[0]), aliases={last + 1: 0} if carried else {},
    )


def products_kernel(where_ref, *refs, count, steps, apart):
    def take(number):
        nonlocal refs
        taken, refs = refs[:number], refs[number:]
        return taken

    lows, slopes = take(steps * count), take(steps * count)
    befores, actives = take(count), take(count)
    kept_ref, *sent_refs = refs
    width = kept_ref.shape[3]
    for place, (lefts, rights) in enumerate(((lows, befores), (slopes, actives))):
        for group in range(2):
            columns = slice(group * width, (group + 1) * width)
            total = None
            for n in range(count):
                left = [ref[...] for ref in lefts[steps * n : steps * (n + 1)]]
                left = jnp.concatenate(left, axis=1) if steps > 1 else left[0]
                part = dot(left, rights[n][:, columns], 0, 0)
                total = part if total is None else total + part
            for step in range(steps):
                value = total[step * BLOCK : (step + 1) * BLOCK, :]
                if group == 0:
                    kept_ref[step, place] = value
                elif step == 0 and apart:
                    sent_refs[place][...] = value
                else:
                    sent_refs[step + int(apart)][place] = value


def products(steps, apart, where, lows, slopes, befores, actives, after):
    length, depth = lows[0].shape
    width = befores[0].shape[1] // 2
    count = len(lows)
    tiles, values = [], []
    for way, arrays in enumerate((lows, slopes)):
        for array in arrays:
            for step in steps:
                place = 4 + 2 * step + way
                values.append(array)
                tiles.append(
                    pl.BlockSpec((length, BLOCK), lambda i, w, place=place: (0, w[place]))
                )
    outs = [shape((len(steps), 2, BLOCK, width), F32)]
    outs += [shape((BLOCK, width), F32)] * (2 * int(apart))
    outs += [shape((2, BLOCK, width), F32)] * (len(steps) - int(apart))
    return launch(
        functools.partial(products_kernel, count=count, steps=len(steps), apart=apart), "products",
        where, (*values, *befores, *actives), tiles + [RESIDENT] * (2 * count), outs,
        [whole_block(o) for o in outs], (1,), 24, after, streamed=range(2 * len(steps) * count),
    )


def first_kernel(
    where_ref, part_ref, part_far_ref, slope_ref, normed_ref, scaled_ref, gain_ref,
    wo_ref, one_ref, low_ref, mixed_ref, sums_ref,
):
    step = pl.program_id(0)
    upstream = slope_ref[...] + (part_ref[...] + part_far_ref[...])
    normed = normed_ref[...]

    @pl.when(step == 0)
    def _():
        sums_ref[...] = jnp.zeros_like(sums_ref)

    sums_ref[0:1, :] += jnp.sum(upstream * normed, axis=0, keepdims=True)
    sums_ref[1:2, :] += jnp.sum(upstream, axis=0, keepdims=True)
    slope = norm_back(upstream, normed, scaled_ref[:, 0:1], gain_ref[...])
    one_ref[...] = slope
    low = slope.astype(BF16)
    low_ref[...] = low
    width = mixed_ref.shape[1]
    weights = wo_ref[pl.ds(pl.multiple_of(where_ref[2] * width, width), width), :]
    mixed_ref[...] = dot(low, weights, 1, 1).astype(BF16)


def first(where, part, part_far, slope, normed, scaled, gain, wo, after):
    length, depth = slope.shape
    both = wo.shape[0] // 2
    half = length // 2
    outs = [
        shape((length, depth), F32),
        shape((length, depth), BF16),
        shape((length, both), BF16),
        shape((8, depth), F32),
    ]
    out_specs = [rows_block(half, o.shape[1]) for o in outs]
    out_specs[3] = whole_block(outs[3])
    rows = rows_block(half, depth)
    return launch(
        first_kernel, "first", where, (part, part_far, slope, normed, scaled, gain, wo),
        [rows, rows, rows, rows, rows_block(half, 128), whole_block(gain), RESIDENT],
        outs, out_specs, (2,), 18, after, streamed=(2, 3, 4), stored=(0, 1),
    )


def attend_back_kernel(
    where_ref, qkv_ref, go_ref, sums_ref, seg_ref, weights_ref, out_ref, grads_ref,
    key_slope, value_slope,
):
    width = weights_ref.shape[2] // 3
    owner, _ = lanes(width)
    zero = jnp.zeros((), BF16)
    spares = [spare_columns(seg_ref[0], sums_ref[...], group, width) for group in range(2)]

    def part_of(group, n):
        start = (3 * group + n) * width
        return qkv_ref[0, :, start : start + width]

    def products_of(group, head):
        spare_q, spare_k = spares[group]
        mine = owner == head
        score = dot(
            pick(head, owner, part_of(group, 0), spare_q, zero),
            jnp.where(mine, part_of(group, 1), spare_k), 1, 1,
        )
        upstream = go_ref[:, group * width : (group + 1) * width]
        return score, dot(jnp.where(mine, upstream, zero), part_of(group, 2), 1, 1)

    ahead = products_of(0, 0)
    for group in range(2):
        keys = part_of(group, 1)
        queries_t = part_of(group, 0).T
        upstream_t = go_ref[:, group * width : (group + 1) * width].T
        query_slope = jnp.zeros(keys.shape, F32)
        for head in range(GROUP):
            row = group * GROUP + head
            score, drift = ahead
            if row + 1 < 2 * GROUP:
                ahead = products_of((row + 1) // GROUP, (row + 1) % GROUP)
            place = slice(head * HEAD_DIM, (head + 1) * HEAD_DIM)
            chances = jnp.exp(score)
            slopes = chances * (drift - jnp.sum(drift * chances, axis=-1, keepdims=True))
            slopes = slopes.astype(BF16)
            query_slope = query_slope + dot(slopes, jnp.where(owner == head, keys, zero))
            key_slope[place, :] = dot(queries_t[place, :], slopes)
            value_slope[place, :] = dot(upstream_t[place, :], chances.astype(BF16))
        start = 3 * group * width
        grads_ref[:, start : start + width] = (query_slope * SCALE).astype(BF16)
        grads_ref[:, start + width : start + 2 * width] = key_slope[...].T.astype(BF16)
        grads_ref[:, start + 2 * width : start + 3 * width] = value_slope[...].T.astype(BF16)
        part = dot(grads_ref[:, start : start + 3 * width], weights_ref[group], 1, 1)
        if group == 0:
            out_ref[...] = part
        else:
            out_ref[...] += part


def attend_back(i, where, qkv, go, mixed, seg, weights, after):
    _, length, columns = qkv.shape
    _, depth, width = weights.shape
    outs = [shape((length, depth), F32), shape((length, columns), BF16)]
    return launch(
        attend_back_kernel, "attend_back", where, (qkv, go, mixed, seg, weights),
        [
            whole_block(qkv),
            whole_block(go),
            pl.BlockSpec((8, columns // 3), lambda g, w: (length // 8, 0)),
            sequence(i, (8, length)),
            RESIDENT,
        ],
        outs, [whole_block(o) for o in outs], (1,), 22, after,
        scratch=[pltpu.VMEM((width // 3, length), F32)] * 2, streamed=(0,), stored=(1,),
    )


def total_kernel(where_ref, one_ref, part_ref, far_ref, *rest):
    final_ref, out_ref = rest[-2:]
    final = (one_ref[...] + (part_ref[...] + far_ref[...])).astype(BF16)
    final_ref[0] = final
    out_ref[...] = final.astype(F32)


def total(i, count, where, one, part, far, final, after):
    length, depth = one.shape
    quarter = length // 4
    rows = rows_block(quarter, depth)
    carried = [] if final is None else [final]
    return launch(
        total_kernel, "total", where, (one, part, far, *carried),
        [rows] * 3 + [ANY] * len(carried),
        [shape((count, length, depth), BF16), shape((length, depth), F32)],
        [pl.BlockSpec((1, quarter, depth), lambda g, w: (2 * w[1] + i, g, 0)), rows],
        (4,), 10, after, streamed=(3,) if carried else (0,), stored=(0,),
        aliases={4: 0} if carried else {},
    )


def head_products_kernel(where_ref, *refs, count):
    def take(number):
        nonlocal refs
        taken, refs = refs[:number], refs[number:]
        return taken

    def summed(lefts, rights):
        total = None
        for n in range(count):
            left = jnp.concatenate([lefts[2 * n], lefts[2 * n + 1]], axis=1)
            part = dot(left, rights[n], 0, 0)
            total = part if total is None else total + part
        return total

    firsts, seconds, ones = take(2 * count), take(2 * count), take(2 * count)
    grads, mixed, first_sums, second_sums = take(count), take(count), take(2 * count), take(2 * count)
    width = mixed[0].shape[2] // 2
    x_first, x_second = ([ref[0] for ref in group] for group in (firsts, seconds))
    kept_ref, *sent_refs = refs
    for group in range(2):
        start = 3 * group * width
        pairs = [ref[:, start : start + 2 * width] for ref in grads]
        heads = summed(x_first, pairs)
        values = summed(x_second, [ref[:, start + 2 * width : start + 3 * width] for ref in grads])
        outputs = summed(
            [ref[...] for ref in ones], [ref[0, :, group * width : (group + 1) * width] for ref in mixed]
        )
        for step in range(2):
            rows = slice(step * BLOCK, (step + 1) * BLOCK)
            out = sent_refs[step] if group else kept_ref.at[step]
            out[0:BLOCK, :] = heads[rows, 0:width]
            out[BLOCK : 2 * BLOCK, :] = heads[rows, width:]
            out[2 * BLOCK : 3 * BLOCK, :] = values[rows, :]
            out[3 * BLOCK : 4 * BLOCK, :] = outputs[rows, :]
            out[4 * BLOCK :, :] = jnp.zeros((8, width), F32)
            for row, sums in ((0, first_sums), (2, second_sums)):
                gains = sums[step][0:2, :]
                for n in range(1, count):
                    gains = gains + sums[2 * n + step][0:2, :]
                last = 4 * BLOCK + row
                out[last : last + 2, 0:BLOCK] = gains


def head_products(pair, where, x, ones, grads, mixed, firsts, seconds, after):
    _, length, depth = x.shape
    count = len(ones)
    width = mixed[0].shape[2] // 2

    def tile(way, step, dims, lead=()):
        return pl.BlockSpec(
            (*dims, BLOCK),
            lambda j, w: (*[f(w) for f in lead], 0, w[4 + 2 * (2 * pair + step) + way]),
        )

    def inputs_of(way):
        return [
            tile(way, step, (1, length), (lambda w, i=i: 2 * w[1] + i,))
            for i in range(count) for step in range(2)
        ]

    out = shape((4 * BLOCK + 8, width), F32)
    outs = [shape((2, *out.shape), F32), out, out]
    twice = lambda arrays: [a for a in arrays for _ in range(2)]
    return launch(
        functools.partial(head_products_kernel, count=count), "head_products", where,
        (
            *[x] * (4 * count), *twice(ones), *grads, *mixed, *twice(firsts), *twice(seconds)
        ),
        inputs_of(0) + inputs_of(1) + [tile(1, step, (length,)) for _ in ones for step in range(2)]
        + [RESIDENT] * (2 * count)
        + [tile(1, step, (8,)) for _ in range(2 * count) for step in range(2)],
        outs, [whole_block(o) for o in outs], (1,), 12, after, streamed=range(6 * count),
    )


def ring_kernel(where_ref, *refs, arrivals, sizes):
    outs = refs[-2:]
    sources = refs[arrivals : -2]
    for way in range(2):
        mine, start = [], 0
        count = sizes[way]
        kept = sources[way * sizes[0] : way * sizes[0] + count]
        base = sizes[0] + sizes[1]
        near = sources[base + way * sizes[0] : base + way * sizes[0] + count]
        for left, right in zip(kept, near):
            value = left[...].reshape(left.shape[-2:]) + right[...].reshape(right.shape[-2:])
            rows = slice(start, start + value.shape[0])
            if arrivals:
                value = refs[way][rows, :] + value
            outs[way][rows, :] = value
            start += value.shape[0]


def ring_step(where, arrived, kept, near, after):
    entries = [*kept[0], *kept[1], *near[0], *near[1]]
    specs = [whole_block(a) for a in arrived]
    specs += [pl.BlockSpec(dims, lambda i, w, at=at: at) for _, dims, at in entries]
    outs = [
        shape((sum(e[1][-2] for e in way), way[0][1][-1]), F32) for way in kept
    ]
    return launch(
        functools.partial(ring_kernel, arrivals=len(arrived), sizes=(len(kept[0]), len(kept[1]))),
        "ring_step", where, (*arrived, *[e[0] for e in entries]), specs, outs,
        [whole_block(o) for o in outs], (1,), 8, after,
    )


def last_kernel(where_ref, left_ref, right_ref, *refs):
    kept, near, outs = refs[0:3], refs[3:6], refs[6:]
    top, middle, low = (
        k[...].reshape(k.shape[-2:]) + n[...].reshape(n.shape[-2:]) for k, n in zip(kept, near)
    )
    left = left_ref[...] + top
    right = right_ref[0 : 2 * BLOCK, :] + middle
    low = right_ref[2 * BLOCK :, :] + low
    outs[0][...] = left[0:BLOCK, :]
    outs[1][...] = left[BLOCK:, :]
    outs[2][...] = right[0:BLOCK, :]
    outs[3][...] = right[BLOCK:, :].T
    for row, out in enumerate(outs[4:]):
        out[...] = low[row : row + 1, 0:BLOCK]


def last_step(where, arrived, kept, near, after):
    entries = [*kept[0], *kept[1], *near[0], *near[1]]
    specs = [whole_block(a) for a in arrived]
    specs += [pl.BlockSpec(dims, lambda i, w, at=at: at) for _, dims, at in entries]
    width = arrived[0].shape[1]
    outs = [shape((BLOCK, width), F32)] * 3 + [shape((width, BLOCK), F32)]
    outs += [shape((1, BLOCK), F32)] * 4
    return launch(
        last_kernel, "last_step", where, (*arrived, *[e[0] for e in entries]), specs, outs,
        [whole_block(o) for o in outs], (1,), 8, after, stored=range(8),
    )


def turn_kernel(where_ref, value_ref, out_ref):
    out_ref[...] = value_ref[...].T


def turn(where, value, after):
    out = shape(value.shape[::-1], F32)
    return launch(
        turn_kernel, "turn", where, (value,), [whole_block(value)], [out], [whole_block(out)],
        (1,), 6, after, stored=(0,),
    )[0]


def hold_kernel(where_ref, *refs):
    *pairs, arrived = refs
    count = len(pairs) // 2
    copies = [
        pltpu.make_async_copy(pairs[n], pairs[count + n], arrived.at[n]) for n in range(count)
    ]
    for copy in copies:
        copy.start()
    for copy in copies:
        copy.wait()


def hold(where, *values, after):
    count = len(values)
    token = shape((8, 128), F32)

    def run(where_ref, *refs):
        refs[2 * count][...] = jnp.zeros((8, 128), F32)
        hold_kernel(where_ref, *refs[: 2 * count], refs[-1])

    return launch(
        run, "hold", where, values, [ANY] * count,
        [*[pltpu.VMEM(v.shape, v.dtype) for v in values], token],
        [*[RESIDENT] * count, whole_block(token)], (1,), 4, after, streamed=range(count),
        scratch=[pltpu.SemaphoreType.DMA((count,))],
    )[:count]


def clip_kernel(where_ref, query_ref, key_ref, factor_ref, query_out, key_out):
    query_out[...] = query_ref[...].astype(F32) * factor_ref[...]
    key_out[...] = key_ref[...].astype(F32) * factor_ref[...]


def clip(where, query, key, factor, after):
    specs = [rows_block(query.shape[0] // 4, query.shape[1])] * 2
    return launch(
        clip_kernel, "clip", where, (query, key, factor), [*specs, whole_block(factor)],
        [shape(query.shape, F32)] * 2, specs, (4,), 8, after, streamed=(0, 1), stored=(0, 1),
    )


def finish_kernel(where_ref, *refs):
    *halves, final_ref, out_ref, token_ref = refs
    del final_ref
    value = halves[0][...].reshape(out_ref.shape[1:])
    if len(halves) == 2:
        value = jnp.where(pl.program_id(0) == 0, value, halves[1][...])
    out_ref[0] = value.astype(BF16)
    token_ref[...] = jnp.zeros_like(token_ref)


def finish(i, where, values, final, after):
    half, depth = final.shape[1] // 2, final.shape[2]
    specs = [rows_block(half, depth)]
    if len(values) == 2:
        specs = [whole_block(v) for v in values]
    last = len(values)
    token = shape((8, 128), F32)
    return launch(
        finish_kernel, "finish", where, (*values, final), [*specs, ANY],
        [shape(final.shape, BF16), token],
        [
            pl.BlockSpec((1, half, depth), lambda g, w: (2 * (1 - w[1]) + i, g, 0)),
            whole_block(token),
        ],
        (2,), 10, after, aliases={last + 1: 0}, stored=(0,), streamed=(last,),
    )[0]


def solution(mesh):
    ranks = mesh.shape["dp"]
    group = mesh.shape["tensor"]
    assert group == 4 and ranks % 8 == 0
    near_pairs = [(t, t ^ 1) for t in range(group)]
    far_pairs = [(t, t ^ 2) for t in range(group)]
    turns = (
        [(RING[p], RING[(p + 1) % 8]) for p in range(8)],
        [(RING[p], RING[(p - 1) % 8]) for p in range(8)],
    )

    def near(value):
        return lax.ppermute(value, "tensor", near_pairs)

    def scatter(value):
        return lax.psum_scatter(value, "dp", scatter_dimension=0, tiled=True)

    def far(value):
        return lax.ppermute(value, "tensor", far_pairs)

    def body(
        block_input, segment_ids, query_weight, key_weight, value_weight, output_weight,
        first_gain, first_shift, up_weight, down_weight, second_gain, second_shift, out_grad,
    ):
        count, length, depth = block_input.shape
        width = query_weight.shape[1]
        part = depth // ranks
        mine = range(count // 2)
        me = lax.axis_index("tensor")
        rank = lax.axis_index("dp")
        natural = [n for n in range(8) for _ in range(2)]
        owners = jnp.asarray(OWNERS if ranks == 8 else [natural], jnp.int32)
        owners = lax.dynamic_index_in_dim(owners, rank if ranks == 8 else 0, 0, False)
        where = jnp.concatenate(
            [jnp.stack([me, me % 2, me // 2, rank]).astype(jnp.int32), owners]
        )
        seg = jnp.broadcast_to(segment_ids[:, None, :], (count, 8, length))
        gain_one, shift_one = first_gain[None], first_shift[None]
        gain_two, shift_two = second_gain[None], second_shift[None]
        order = Order()

        def then(call, *args, **kwargs):
            return call(*args, after=order, **kwargs)

        own_low, own_wide, wo_half = then(
            widen_heads, where, query_weight, key_weight, value_weight, output_weight
        )
        near_wide, wo_first = near(own_wide), far(wo_half)
        wide = convert(where, up_weight, down_weight, dtype=F32, after=Order())
        wide_near = [near(w) for w in wide]
        weights, wo_near = then(narrow_near, where, own_low, near_wide, output_weight)
        heads, mixed_far = [], []
        for i in mine:
            heads.append(then(attend, i, where, block_input, weights, seg))
            mixed_far.append(far(heads[i][3]))
            if i == 0:
                (wo_first,) = then(gate, where, wo_first)
                wo_second = lax.ppermute(wo_first, "dp", [(r, r ^ 1) for r in range(ranks)])
                wo_both = [near(wo_first)]
        mixed_low, qkv, tops, mixed = zip(*heads)
        up_near, down_near = then(convert, where, *wide_near, dtype=BF16)
        ups, downs = (up_weight, up_near), (down_weight, down_near)
        (wo_second,) = then(gate, where, wo_second)
        wo_both.append(near(wo_second))
        wo = then(assemble, where, output_weight, wo_near, (wo_first, wo_second), wo_both)

        forwards, part_far = [], []
        for i in mine:
            forwards.append(
                then(
                    forward, i, where, block_input, mixed[i], mixed_far[i], wo, gain_one,
                    shift_one, ups, downs,
                )
            )
            part_far.append(far(forwards[i][5]))

        heads_own = width // HEAD_DIM
        peak = functools.reduce(jnp.maximum, tops)
        peak = jnp.maximum(peak[:heads_own], near(peak)[heads_own:])
        step = 1
        while step < ranks:
            peak = jnp.maximum(peak, lax.ppermute(peak, "dp", [(i, i ^ step) for i in range(ranks)]))
            step *= 2
        factor = jnp.sqrt(CLIP / jnp.maximum(peak[:, 0], CLIP))
        factor = jnp.repeat(factor, HEAD_DIM)[None]
        query_clipped, key_clipped = then(clip, where, query_weight, key_weight, factor)

        written = {"layer_out": None, "input_grad": None}
        def finish_layer(i, values):
            written["layer_out"] = then(finish, i, where, values, written["layer_out"])

        backs, slope_parts, slope_far = [], [], []
        for i in mine:
            normed, scaled, low, active, pull, part_sum = forwards[i]
            weights_of = ups, downs
            if i > 0:
                normed, pull, *held = then(hold, where, normed, pull, *ups, *downs)
                weights_of = held[0:2], held[2:4]
            backs.append(
                then(
                    backward, i, where, normed, gain_one, shift_one, part_sum, part_far[i],
                    out_grad, gain_two, shift_two, pull, *weights_of, written["layer_out"],
                    resident=i > 0,
                )
            )
            written["layer_out"], *out, slope, slope_low, before, sums, part_sum = backs[i]
            backs[i] = (out, slope, slope_low, before, sums)
            slope_parts.append(part_sum)
            slope_far.append(far(part_sum))
            if i == 0:
                finish_layer(0, [near(v) for v in out])

        lows, actives = [f[2] for f in forwards], [f[3] for f in forwards]
        slope_lows, befores = [b[2] for b in backs], [b[3] for b in backs]
        def send(held):
            return [lax.ppermute(h, "dp", t) for h, t in zip(held, turns)]

        ff_blocks = {}

        def ff_part(*steps, apart=True):
            kept, *sent = then(products, steps, apart, where, lows, slope_lows, befores, actives)
            sent = [near(a) for a in sent]
            for index, n in enumerate(steps):
                mine = sent[:2] if index == 0 and apart else sent[index + int(apart)]
                ff_blocks[n] = (kept, index, mine)

        def ff_step(n, arrived):
            kept, index, sent = ff_blocks[n]
            dims = (1, 1, BLOCK, kept.shape[3])
            if isinstance(sent, list):
                near = [[(array, dims[2:], (0, 0))] for array in sent]
            else:
                near = [[(sent, dims[1:], (way, 0, 0))] for way in range(2)]
            return then(
                ring_step, where, arrived,
                [[(kept, dims, (index, way, 0, 0))] for way in range(2)], near,
            )

        def ff_ring():
            held = ff_step(0, ())
            for n in range(1, 8):
                arrived = send(held)
                yield None
                held = ff_step(n, arrived)
            yield held

        head_parts = []

        def head_part(pair):
            kept, *sent = then(
                head_products, pair, where, block_input, [f[1] for f in firsts],
                [o[1] for o in owns], mixed_low, [f[3] for f in firsts], [b[4] for b in backs],
            )
            head_parts.append((kept, [near(a) for a in sent]))

        def head_step(n, arrived):
            kept, sent = head_parts[n // 2]

            def entries(array, lead):
                block = lambda rows, at: (
                    array, (*[1 for _ in lead], rows, width), (*lead, at, 0)
                )
                return [[block(2 * BLOCK, 0)], [block(2 * BLOCK, 1), block(8, 4 * BLOCK // 8)]]

            call = last_step if n == 7 else ring_step
            return then(call, where, arrived, entries(kept, (n % 2,)), entries(sent[n % 2], ()))

        def head_ring():
            held = head_step(0, ())
            for n in range(1, 8):
                arrived = send(held)
                yield None
                held = head_step(n, arrived)
            yield held

        def total_input(i):
            one, own = (firsts[i][0], owns[i][0]) if i == 0 else summands
            written["input_grad"], result = then(
                total, i, count, where, one, own, input_far[i], written["input_grad"]
            )
            return result

        def finish_input(i, value):
            written["input_grad"] = then(finish, i, where, [value], written["input_grad"])

        def first_back(i):
            firsts.append(
                then(
                    first, where, slope_parts[i], slope_far[i], backs[i][1], *forwards[i][:2],
                    gain_one, wo,
                )
            )

        def own_back(i):
            owns.append(then(attend_back, i, where, qkv[i], firsts[i][2], mixed[i], seg, weights))

        firsts, owns, input_far = [], [], []
        ring = ff_ring() if ranks == 8 else iter(())
        ff_part(0)
        ff_part(1, 2)
        next(ring, None)
        next(ring, None)
        ff_part(3, 4)
        first_back(0)
        next(ring, None)
        own_back(0)
        next(ring, None)
        ff_part(5, 6, 7)
        next(ring, None)
        slope_far[1], own_part = then(gate, where, slope_far[1], owns[0][0])
        owns[0] = (own_part, owns[0][1])
        input_far.append(far(own_part))
        first_back(1)
        next(ring, None)
        own_back(1)
        next(ring, None)
        head_part(0)
        head_part(1)
        head_part(2)
        if ranks == 8:
            *_, (up_grad, down_grad) = ring
        (own_part,) = then(gate, where, owns[1][0])
        owns[1] = (own_part, owns[1][1])
        input_far.append(far(own_part))
        ring = head_ring() if ranks == 8 else iter(())
        next(ring, None)
        head_part(3)
        next(ring, None)
        next(ring, None)
        rows = total_input(0)
        next(ring, None)
        (rows,) = then(gate, where, rows)
        rows = near(rows)
        summands = then(hold, where, firsts[1][0], owns[1][0])
        next(ring, None)
        if ranks == 8:
            down_grad = then(turn, where, down_grad)
        next(ring, None)
        result = total_input(1)
        next(ring, None)
        result, layer = then(gate, where, result, *backs[1][0])
        result, layer = near(result), near(layer)
        finish_input(0, rows)
        finish_input(1, result)
        finish_layer(1, [layer])

        if ranks == 8:
            *_, (query_grad, key_grad, value_grad, output_grad, *gains) = ring
            gains = [g.reshape(BLOCK) for g in gains]
        else:
            def rows_of(value, start, rows=BLOCK):
                return scatter(value[:, start : start + rows].reshape(8 * rows, width))

            up, down = [
                jnp.concatenate(
                    [kept[at, way] + sent[way] for kept, at, sent in map(ff_blocks.get, range(8))],
                    axis=0,
                )
                for way in range(2)
            ]
            up_grad, down_grad = scatter(up), scatter(down).T
            value = jnp.concatenate([k + jnp.stack(s) for k, s in head_parts], axis=0)
            query_grad, key_grad, value_grad = (rows_of(value, n * BLOCK) for n in range(3))
            output_grad = rows_of(value, 3 * BLOCK).T
            gains = value[:, 4 * BLOCK : 4 * BLOCK + 4, :BLOCK].transpose(0, 2, 1)
            gains = scatter(gains.reshape(depth, 4)).T

        return (
            written["layer_out"], written["input_grad"], query_grad, key_grad, value_grad, output_grad,
            gains[0], gains[1], up_grad, down_grad, gains[2], gains[3],
            query_clipped, key_clipped,
        )

    batch = P("dp", None, None)
    in_specs = (
        batch, P("dp", None), P(None, "tensor"), P(None, "tensor"), P(None, "tensor"),
        P("tensor", None), P(), P(), P(None, "tensor"), P("tensor", None), P(), P(), batch,
    )
    out_specs = (
        batch, batch, P("dp", "tensor"), P("dp", "tensor"), P("dp", "tensor"), P("tensor", "dp"),
        P("dp"), P("dp"), P("dp", "tensor"), P("tensor", "dp"), P("dp"), P("dp"),
        P(None, "tensor"), P(None, "tensor"),
    )
    return jax.shard_map(body, mesh=mesh, in_specs=in_specs, out_specs=out_specs, check_vma=False)
```

```python
import functools

import jax
import jax.numpy as jnp
from jax import lax
from jax.experimental import pallas as pl
from jax.experimental.pallas import tpu as pltpu
from jax.sharding import PartitionSpec as P

F32 = jnp.float32
BF16 = jnp.bfloat16
HEAD_DIM = 64
FAR = -1e30
EPS = 1e-06
CLIP = 10.0
SCALE = HEAD_DIM**-0.5
ROOT_HALF = 0.5**0.5
BELL = 0.3989422804014327
GROUP = 4
BLOCK = 128
DOCS = 4
MIB = 1 << 20
RING = (0, 2, 4, 6, 7, 5, 3, 1)
OWNERS = tuple(
    tuple(RING[(RING.index(r) + way * (1 + n)) % 8] for n in range(8) for way in (-1, 1))
    for r in range(8)
)
ANY = pl.BlockSpec(memory_space=pl.ANY)
RESIDENT = pl.BlockSpec(memory_space=pltpu.VMEM)


def dot(left, right, left_dim=1, right_dim=0):
    return lax.dot_general(
        left, right, (((left_dim,), (right_dim,)), ((), ())), preferred_element_type=F32
    )


def normalize(total):
    average = jnp.mean(total, axis=-1, keepdims=True)
    centred = total - average
    variance = jnp.mean(centred * centred, axis=-1, keepdims=True)
    scaled = lax.rsqrt(variance + EPS)
    return centred * scaled, scaled


def norm_back(upstream, normed, scaled, gain):
    weighted = upstream * gain
    first = jnp.mean(weighted, axis=-1, keepdims=True)
    second = jnp.mean(weighted * normed, axis=-1, keepdims=True)
    return scaled * (weighted - first - normed * second)


def lanes(width):
    lane = lax.broadcasted_iota(jnp.int32, (1, width), 1)
    return lane // HEAD_DIM, lane % HEAD_DIM


def split(value):
    high = value.astype(BF16)
    rest = value - high.astype(F32)
    middle = rest.astype(BF16)
    return high, middle, (rest - middle.astype(F32)).astype(BF16)


def pick(head, owner, own, spare, zero):
    return jnp.where(owner == head, own, jnp.where(owner == (head + 1) % GROUP, spare, zero))


def spare_columns(seg_rows, sums, group, width):
    owner, lane = lanes(width)
    row8 = lax.broadcasted_iota(jnp.int32, (8, 1), 0)
    equal = jnp.where(seg_rows == row8, 1.0, 0.0)
    rows = [equal]
    wanted = [jnp.where(lane == row8, FAR, 0.0)]
    if sums is not None:
        head = row8 % GROUP
        here = (row8 // GROUP == group) & ((head + 1) % GROUP == owner)
        for n, value in enumerate(split(sums)):
            rows.append(value.astype(F32))
            wanted.append(jnp.where(here & (lane == DOCS + n), -1.0, 0.0))
    placed = jnp.concatenate(wanted, axis=0).astype(BF16)
    queries = dot(jnp.concatenate(rows, axis=0).astype(BF16), placed, 0, 0).astype(BF16)
    ones = jnp.where((lane >= DOCS) & (lane < DOCS + 3), 1.0, 0.0)
    placed = jnp.where((lane == row8) & (row8 < DOCS), 1.0, 0.0).astype(BF16)
    differ = jnp.where(seg_rows == row8, 0.0, 1.0).astype(BF16)
    keys = (dot(differ, placed, 0, 0) + ones).astype(BF16)
    return queries, keys


def shape(dims, dtype):
    return jax.ShapeDtypeStruct(tuple(dims), dtype)


def whole_block(array):
    zeros = (0,) * len(array.shape)
    return pl.BlockSpec(tuple(array.shape), lambda i, w: zeros)


def rows_block(rows, columns):
    return pl.BlockSpec((rows, columns), lambda i, w: (i, 0))


class Order:
    def __init__(self):
        self.token, self.stored = None, False

    def taken(self):
        if self.token is None:
            return []
        if self.stored:
            return [pltpu.with_memory_space_constraint(self.token, pltpu.HBM)]
        return [self.token]

    def give(self, results, stored):
        sizes = [r.size * jnp.dtype(r.dtype).itemsize for r in results]
        index = sizes.index(min(sizes))
        self.token, self.stored = results[index], index in stored


def launch(
    kernel, name, where, inputs, in_specs, outs, out_specs, grid, vmem, after,
    scratch=(), aliases=None, streamed=(), stored=(),
):
    count = len(inputs)
    tokens = after.taken()
    inputs = [
        pltpu.with_memory_space_constraint(value, pltpu.HBM) if i in streamed else value
        for i, value in enumerate(inputs)
    ]
    outs = [
        pltpu.HBM(value.shape, value.dtype) if i in stored else value
        for i, value in enumerate(outs)
    ]

    def run(where_ref, *refs):
        kernel(where_ref, *refs[:count], *refs[count + len(tokens) :])

    results = pl.pallas_call(
        run,
        grid_spec=pltpu.PrefetchScalarGridSpec(
            num_scalar_prefetch=1,
            grid=grid,
            in_specs=list(in_specs) + [ANY] * len(tokens),
            out_specs=list(out_specs),
            scratch_shapes=list(scratch),
        ),
        out_shape=outs,
        input_output_aliases=aliases or {},
        compiler_params=pltpu.CompilerParams(
            vmem_limit_bytes=vmem * MIB, dimension_semantics=("arbitrary",) * len(grid)
        ),
        cost_estimate=pl.CostEstimate(flops=1, bytes_accessed=1, transcendentals=0),
        name=name,
    )(where, *inputs, *tokens)
    after.give(results, stored)
    return results


def gate_kernel(*refs):
    del refs


def gate(where, *values, after):
    outs = [shape(v.shape, v.dtype) for v in values]
    return launch(
        gate_kernel, "gate", where, values, [ANY] * len(values), outs, [ANY] * len(values), (1,),
        2, after, aliases={i + 1: i for i in range(len(values))},
    )


def widen_heads_kernel(where_ref, wq_ref, wk_ref, wv_ref, wo_ref, own, wide, wo):
    width = wq_ref.shape[1]
    for index, ref in enumerate((wq_ref, wk_ref, wv_ref)):
        columns = slice(index * width, (index + 1) * width)
        value = ref[...]
        own[:, columns] = value
        wide[:, columns] = value.astype(F32)
    rows, depth = wo_ref.shape
    for index in range(depth // width):
        wide[index * rows : (index + 1) * rows, 3 * width :] = wo_ref[
            :, index * width : (index + 1) * width
        ].astype(F32)
    half = rows // 2
    wo[...] = wo_ref[pl.ds(pl.multiple_of((where_ref[3] % 2) * half, half), half), :].astype(F32)


def widen_heads(where, wq, wk, wv, wo, after):
    depth, width = wq.shape
    outs = [
        shape((depth, 3 * width), BF16),
        shape((depth, 4 * width), F32),
        shape((wo.shape[0] // 2, depth), F32),
    ]
    inputs = (wq, wk, wv, wo)
    return launch(
        widen_heads_kernel, "widen_heads", where, inputs, [whole_block(a) for a in inputs], outs,
        [whole_block(o) for o in outs], (1,), 12, after, streamed=range(4),
    )


def assemble_kernel(where_ref, own_ref, near_ref, *refs):
    *halves, out_ref = refs
    rows = own_ref.shape[0]
    half = rows // 2
    mine = where_ref[2] * 2 * rows
    other = (1 - where_ref[2]) * 2 * rows
    out_ref[pl.ds(pl.multiple_of(mine, rows), rows), :] = own_ref[...]
    out_ref[pl.ds(pl.multiple_of(mine + rows, rows), rows), :] = near_ref[...]
    parity = where_ref[3] % 2
    for start, first, second in ((other, *halves[0:2]), (other + rows, *halves[2:4])):
        for ref, place in ((first, parity), (second, 1 - parity)):
            begin = pl.multiple_of(start + place * half, half)
            out_ref[pl.ds(begin, half), :] = ref[...].astype(BF16)


def assemble(where, own, near, far, both, after):
    rows, columns = own.shape
    out = shape((4 * rows, columns), BF16)
    inputs = (own, near, *far, *both)
    return launch(
        assemble_kernel, "assemble", where, inputs, [whole_block(a) for a in inputs], [out],
        [whole_block(out)], (1,), 14, after,
    )[0]


def narrow_near_kernel(where_ref, own_ref, wide_ref, heads_ref, wo_ref):
    width = own_ref.shape[1] // 3
    heads_ref[0] = own_ref[...]
    heads_ref[1] = wide_ref[:, 0 : 3 * width].astype(BF16)
    rows, depth = wo_ref.shape
    for index in range(depth // width):
        wo_ref[:, index * width : (index + 1) * width] = wide_ref[
            index * rows : (index + 1) * rows, 3 * width :
        ].astype(BF16)


def narrow_near(where, own, wide, wo, after):
    outs = [shape((2, *own.shape), BF16), shape(wo.shape, BF16)]
    return launch(
        narrow_near_kernel, "narrow_near", where, (own, wide),
        [whole_block(own), whole_block(wide)], outs, [whole_block(o) for o in outs], (1,), 16,
        after,
    )


def convert_kernel(where_ref, *refs):
    half = len(refs) // 2
    for source, target in zip(refs[:half], refs[half:]):
        target[...] = source[...].astype(target.dtype)


def convert(where, *values, dtype, after):
    specs = [rows_block(v.shape[0] // 4, v.shape[1]) for v in values]
    held = range(len(values))
    wide = dtype == F32
    return launch(
        convert_kernel, "convert", where, values, specs, [shape(v.shape, dtype) for v in values],
        specs, (4,), 10, after, streamed=held if wide else (), stored=() if wide else held,
    )


def project_group(x, weights):
    width = weights.shape[1] // 3
    q = (dot(x, weights[:, 0:width]).astype(BF16) * SCALE).astype(BF16)
    k = dot(x, weights[:, width : 2 * width]).astype(BF16)
    v = dot(x, weights[:, 2 * width : 3 * width]).astype(BF16)
    return q, k, v


def attend_kernel(
    where_ref, x_ref, weights_ref, seg_ref, low_ref, qkv_ref, top_ref, o_ref, held_ref
):
    x = x_ref[0]
    width = weights_ref.shape[2] // 3
    owner, _ = lanes(width)
    spare_q, spare_k = spare_columns(seg_ref[0], None, 0, width)
    zero = jnp.zeros((), BF16)
    held_ref[...] = jnp.zeros_like(held_ref)
    groups = [project_group(x, weights_ref.at[group]) for group in range(2)]
    for group, values in enumerate(groups):
        for index, value in enumerate(values):
            start = (3 * group + index) * width
            qkv_ref[0, :, start : start + width] = value

    def scores_of(group, head):
        queries, keys, _ = groups[group]
        return dot(
            pick(head, owner, queries, spare_q, zero),
            jnp.where(owner == head, keys, spare_k), 1, 1,
        )

    for group in range(2):
        total = jnp.zeros(groups[group][0].shape, F32)
        for head in range(GROUP):
            row = group * GROUP + head
            scores = scores_of(group, head)
            top = jnp.max(scores, axis=-1, keepdims=True)
            raised = jnp.exp(scores - top)
            summed = jnp.sum(raised, axis=-1, keepdims=True)
            chances = raised * (1.0 / summed)
            total = total + dot(
                chances.astype(BF16), jnp.where(owner == head, groups[group][2], zero)
            )
            held_ref[:, row : row + 1] = top + jnp.log(summed)
            top_ref[row : row + 1, :] = jnp.broadcast_to(
                jnp.max(top, axis=0, keepdims=True), (1, top_ref.shape[1])
            )
        low = total.astype(BF16)
        low_ref[0, :, group * width : (group + 1) * width] = low
        o_ref[0 : x.shape[0], group * width : (group + 1) * width] = low.astype(F32)
    o_ref[x.shape[0] :, :] = held_ref[...].T[0:8, :]


def sequence(i, dims):
    return pl.BlockSpec((1, *dims), lambda g, w: (2 * w[1] + i, 0, 0))


def attend(i, where, x, weights, seg, after):
    _, length, depth = x.shape
    columns = weights.shape[2]
    width = columns // 3
    outs = [
        shape((1, length, 2 * width), BF16),
        shape((1, length, 2 * columns), BF16),
        shape((2 * GROUP, 128), F32),
        shape((length + 2 * GROUP, 2 * width), F32),
    ]
    out_specs = [whole_block(o) for o in outs]
    return launch(
        attend_kernel, "attend", where, (x, weights, seg),
        [sequence(i, (length, depth)), RESIDENT, sequence(i, (8, length))],
        outs, out_specs, (1,), 20, after, streamed=(0,), stored=(0, 1),
        scratch=[pltpu.VMEM((length, 128), F32)],
    )


def fetch(sources, held_ref, arrived):
    first = pl.program_id(0) == 0
    copies = [
        pltpu.make_async_copy(source, held_ref.at[n], arrived.at[n])
        for n, source in enumerate(sources)
    ]

    @pl.when(first)
    def _():
        for copy in copies:
            copy.start()

    def get(n):
        @pl.when(first)
        def _():
            copies[n].wait()

        return held_ref[n]

    return get


def forward_kernel(
    where_ref, x_ref, mixed_ref, mixed_far_ref, wo_ref, gain_ref,
    shift_ref, up_own, up_near, down_own, down_near,
    normed_ref, scaled_ref, low_ref, active_ref, pull_ref, part_ref, both_ref, held_ref, arrived,
):
    weight = fetch((up_own, down_own, up_near, down_near), held_ref, arrived)
    width = mixed_ref.shape[1]
    chip = where_ref[2]
    both_ref[:, pl.ds(pl.multiple_of(chip * width, width), width)] = mixed_ref[...].astype(BF16)
    both_ref[:, pl.ds(pl.multiple_of((1 - chip) * width, width), width)] = mixed_far_ref[
        ...
    ].astype(BF16)
    normed, scaled = normalize(x_ref[0].astype(F32) + dot(both_ref[...], wo_ref[...]))
    normed_ref[...] = normed
    scaled_ref[...] = jnp.broadcast_to(scaled, scaled_ref.shape)
    low = (normed * gain_ref[...] + shift_ref[...]).astype(BF16)
    low_ref[...] = low
    hidden = up_own.shape[1]
    parts = []
    for group in range(2):
        columns = slice(group * hidden, (group + 1) * hidden)
        before = dot(low, weight(2 * group))
        chance = 0.5 * (1.0 + lax.erf(before * ROOT_HALF))
        active = (before * chance).astype(BF16)
        active_ref[:, columns] = active
        pull_ref[:, columns] = chance + before * (jnp.exp(-0.5 * before * before) * BELL)
        parts.append(dot(active, weight(2 * group + 1)))
    part_ref[...] = parts[0] + parts[1]


def fetched(array):
    return [pltpu.VMEM((4, *array.shape), array.dtype), pltpu.SemaphoreType.DMA((4,))]


def forward(i, where, x, mixed, mixed_far, wo, gain, shift, ups, downs, after):
    _, length, depth = x.shape
    width = mixed.shape[1]
    hidden = 2 * ups[0].shape[1]
    half = length // 2
    pieces = rows_block(half, width)
    outs = [
        shape((length, depth), F32),
        shape((length, 128), F32),
        shape((length, depth), BF16),
        shape((length, hidden), BF16),
        shape((length, hidden), F32),
    ]
    out_specs = [rows_block(half, o.shape[1]) for o in outs]
    outs.append(shape((length, depth), F32))
    out_specs.append(rows_block(half, depth))
    return launch(
        forward_kernel, "forward", where, (x, mixed, mixed_far, wo, gain, shift, *ups, *downs),
        [
            pl.BlockSpec((1, half, depth), lambda g, w: (2 * w[1] + i, g, 0)),
            pieces,
            pieces,
            RESIDENT,
            whole_block(gain),
            whole_block(shift),
            *[ANY] * 4,
        ],
        outs, out_specs, (2,), 30, after,
        streamed=(0, 6, 7, 8, 9), stored=(0, 1, 2, 3, 4),
        scratch=[pltpu.VMEM((half, 2 * width), BF16), *fetched(ups[0])],
    )


def backward_kernel(
    where_ref, normed_ref, gain_ref, shift_ref, grad_ref, second_gain_ref, second_shift_ref,
    pull_ref, up_own, up_near, down_own, down_near, part_ref, part_far_ref, *rest, carried, resident,
):
    (
        final_ref, *out_refs, slope_ref, slope_low_ref, before_ref, sums_ref, part_out_ref
    ) = rest[carried : len(rest) - (0 if resident else 2)]
    scratch = rest[-2:]
    weights = (down_own, up_own, down_near, up_near)
    if resident:
        weight = lambda n: weights[n][...]
    else:
        weight = fetch(weights, *scratch)
    step = pl.program_id(0)
    hidden = normed_ref[...] * gain_ref[...] + shift_ref[...]
    normed, scaled = normalize(hidden + (part_ref[...] + part_far_ref[...]))
    out = (normed * second_gain_ref[...] + second_shift_ref[...]).astype(BF16)
    final_ref[0] = out
    if len(out_refs) == 1:
        out_refs[0][...] = out.astype(F32)
    for index, ref in enumerate(out_refs if len(out_refs) == 2 else ()):

        @pl.when(step == index)
        def _(ref=ref):
            ref[...] = out.astype(F32)

    upstream = grad_ref[0].astype(F32)

    @pl.when(step == 0)
    def _():
        sums_ref[...] = jnp.zeros_like(sums_ref)

    sums_ref[0:1, :] += jnp.sum(upstream * normed, axis=0, keepdims=True)
    sums_ref[1:2, :] += jnp.sum(upstream, axis=0, keepdims=True)
    slope = norm_back(upstream, normed, scaled, second_gain_ref[...])
    slope_ref[...] = slope
    low = slope.astype(BF16)
    slope_low_ref[...] = low
    units = up_own.shape[1]
    parts = []
    for group in range(2):
        columns = slice(group * units, (group + 1) * units)
        before = (dot(low, weight(2 * group), 1, 1) * pull_ref[:, columns]).astype(BF16)
        before_ref[:, columns] = before
        parts.append(dot(before, weight(2 * group + 1), 1, 1))
    part_out_ref[...] = parts[0] + parts[1]


def backward(
    i, where, normed, gain, shift, part, part_far, out_grad, second_gain, second_shift, pull,
    ups, downs, final, after, resident,
):
    count, length, depth = out_grad.shape
    hidden = 2 * ups[0].shape[1]
    half = length // 2
    outs = [
        shape((length, depth), F32),
        shape((length, depth), BF16),
        shape((length, hidden), BF16),
        shape((8, depth), F32),
        shape((length, depth), F32),
    ]
    out_specs = [rows_block(half, o.shape[1]) for o in outs]
    out_specs[3] = whole_block(outs[3])
    halves = 2 if final is None else 1
    value = shape((length // halves, depth), F32)
    outs = [value] * halves + outs
    out_specs = [whole_block(value) if halves == 2 else rows_block(half, depth)] * halves + out_specs
    block = pl.BlockSpec((1, half, depth), lambda g, w: (2 * w[1] + i, g, 0))
    vector = whole_block(gain)
    rows = rows_block(half, depth)
    carried = [] if final is None else [final]
    last = 13
    return launch(
        functools.partial(backward_kernel, carried=len(carried), resident=resident), "backward",
        where,
        (
            normed, gain, shift, out_grad, second_gain, second_shift, pull, *ups, *downs, part,
            part_far, *carried,
        ),
        [
            rows,
            vector,
            vector,
            block,
            vector,
            vector,
            rows_block(half, hidden),
            *[RESIDENT if resident else ANY] * 4,
            rows,
            rows,
            *[ANY] * len(carried),
        ],
        [shape((count, length, depth), BF16), *outs], [block, *out_specs], (2,), 34, after,
        streamed=(3, *(() if resident else (0, *range(6, 11))), *[last] * len(carried)),
        stored=(0, 1 + halves, 2 + halves, *(() if resident else (3 + halves,))),
        scratch=() if resident else fetched(ups[0]), aliases={last + 1: 0} if carried else {},
    )


def products_kernel(where_ref, *refs, count, steps, apart):
    def take(number):
        nonlocal refs
        taken, refs = refs[:number], refs[number:]
        return taken

    lows, slopes = take(steps * count), take(steps * count)
    befores, actives = take(count), take(count)
    kept_ref, *sent_refs = refs
    width = kept_ref.shape[3]
    for place, (lefts, rights) in enumerate(((lows, befores), (slopes, actives))):
        for group in range(2):
            columns = slice(group * width, (group + 1) * width)
            total = None
            for n in range(count):
                left = [ref[...] for ref in lefts[steps * n : steps * (n + 1)]]
                left = jnp.concatenate(left, axis=1) if steps > 1 else left[0]
                part = dot(left, rights[n][:, columns], 0, 0)
                total = part if total is None else total + part
            for step in range(steps):
                value = total[step * BLOCK : (step + 1) * BLOCK, :]
                if group == 0:
                    kept_ref[step, place] = value
                elif step == 0 and apart:
                    sent_refs[place][...] = value
                else:
                    sent_refs[step + int(apart)][place] = value


def products(steps, apart, where, lows, slopes, befores, actives, after):
    length, depth = lows[0].shape
    width = befores[0].shape[1] // 2
    count = len(lows)
    tiles, values = [], []
    for way, arrays in enumerate((lows, slopes)):
        for array in arrays:
            for step in steps:
                place = 4 + 2 * step + way
                values.append(array)
                tiles.append(
                    pl.BlockSpec((length, BLOCK), lambda i, w, place=place: (0, w[place]))
                )
    outs = [shape((len(steps), 2, BLOCK, width), F32)]
    outs += [shape((BLOCK, width), F32)] * (2 * int(apart))
    outs += [shape((2, BLOCK, width), F32)] * (len(steps) - int(apart))
    return launch(
        functools.partial(products_kernel, count=count, steps=len(steps), apart=apart), "products",
        where, (*values, *befores, *actives), tiles + [RESIDENT] * (2 * count), outs,
        [whole_block(o) for o in outs], (1,), 24, after, streamed=range(2 * len(steps) * count),
    )


def first_kernel(
    where_ref, part_ref, part_far_ref, slope_ref, normed_ref, scaled_ref, gain_ref,
    wo_ref, one_ref, low_ref, mixed_ref, sums_ref,
):
    step = pl.program_id(0)
    upstream = slope_ref[...] + (part_ref[...] + part_far_ref[...])
    normed = normed_ref[...]

    @pl.when(step == 0)
    def _():
        sums_ref[...] = jnp.zeros_like(sums_ref)

    sums_ref[0:1, :] += jnp.sum(upstream * normed, axis=0, keepdims=True)
    sums_ref[1:2, :] += jnp.sum(upstream, axis=0, keepdims=True)
    slope = norm_back(upstream, normed, scaled_ref[:, 0:1], gain_ref[...])
    one_ref[...] = slope
    low = slope.astype(BF16)
    low_ref[...] = low
    width = mixed_ref.shape[1]
    weights = wo_ref[pl.ds(pl.multiple_of(where_ref[2] * width, width), width), :]
    mixed_ref[...] = dot(low, weights, 1, 1).astype(BF16)


def first(where, part, part_far, slope, normed, scaled, gain, wo, after):
    length, depth = slope.shape
    both = wo.shape[0] // 2
    half = length // 2
    outs = [
        shape((length, depth), F32),
        shape((length, depth), BF16),
        shape((length, both), BF16),
        shape((8, depth), F32),
    ]
    out_specs = [rows_block(half, o.shape[1]) for o in outs]
    out_specs[3] = whole_block(outs[3])
    rows = rows_block(half, depth)
    return launch(
        first_kernel, "first", where, (part, part_far, slope, normed, scaled, gain, wo),
        [rows, rows, rows, rows, rows_block(half, 128), whole_block(gain), RESIDENT],
        outs, out_specs, (2,), 18, after, streamed=(2, 3, 4), stored=(0, 1),
    )


def attend_back_kernel(
    where_ref, qkv_ref, go_ref, sums_ref, seg_ref, weights_ref, out_ref, grads_ref,
    key_slope, value_slope,
):
    width = weights_ref.shape[2] // 3
    owner, _ = lanes(width)
    zero = jnp.zeros((), BF16)
    spares = [spare_columns(seg_ref[0], sums_ref[...], group, width) for group in range(2)]

    def part_of(group, n):
        start = (3 * group + n) * width
        return qkv_ref[0, :, start : start + width]

    def products_of(group, head):
        spare_q, spare_k = spares[group]
        mine = owner == head
        score = dot(
            pick(head, owner, part_of(group, 0), spare_q, zero),
            jnp.where(mine, part_of(group, 1), spare_k), 1, 1,
        )
        upstream = go_ref[:, group * width : (group + 1) * width]
        return score, dot(jnp.where(mine, upstream, zero), part_of(group, 2), 1, 1)

    ahead = products_of(0, 0)
    for group in range(2):
        keys = part_of(group, 1)
        queries_t = part_of(group, 0).T
        upstream_t = go_ref[:, group * width : (group + 1) * width].T
        query_slope = jnp.zeros(keys.shape, F32)
        for head in range(GROUP):
            row = group * GROUP + head
            score, drift = ahead
            if row + 1 < 2 * GROUP:
                ahead = products_of((row + 1) // GROUP, (row + 1) % GROUP)
            place = slice(head * HEAD_DIM, (head + 1) * HEAD_DIM)
            chances = jnp.exp(score)
            slopes = chances * (drift - jnp.sum(drift * chances, axis=-1, keepdims=True))
            slopes = slopes.astype(BF16)
            query_slope = query_slope + dot(slopes, jnp.where(owner == head, keys, zero))
            key_slope[place, :] = dot(queries_t[place, :], slopes)
            value_slope[place, :] = dot(upstream_t[place, :], chances.astype(BF16))
        start = 3 * group * width
        grads_ref[:, start : start + width] = (query_slope * SCALE).astype(BF16)
        grads_ref[:, start + width : start + 2 * width] = key_slope[...].T.astype(BF16)
        grads_ref[:, start + 2 * width : start + 3 * width] = value_slope[...].T.astype(BF16)
        part = dot(grads_ref[:, start : start + 3 * width], weights_ref[group], 1, 1)
        if group == 0:
            out_ref[...] = part
        else:
            out_ref[...] += part


def attend_back(i, where, qkv, go, mixed, seg, weights, after):
    _, length, columns = qkv.shape
    _, depth, width = weights.shape
    outs = [shape((length, depth), F32), shape((length, columns), BF16)]
    return launch(
        attend_back_kernel, "attend_back", where, (qkv, go, mixed, seg, weights),
        [
            whole_block(qkv),
            whole_block(go),
            pl.BlockSpec((8, columns // 3), lambda g, w: (length // 8, 0)),
            sequence(i, (8, length)),
            RESIDENT,
        ],
        outs, [whole_block(o) for o in outs], (1,), 22, after,
        scratch=[pltpu.VMEM((width // 3, length), F32)] * 2, streamed=(0,), stored=(1,),
    )


def total_kernel(where_ref, one_ref, part_ref, far_ref, *rest):
    final_ref, out_ref = rest[-2:]
    final = (one_ref[...] + (part_ref[...] + far_ref[...])).astype(BF16)
    final_ref[0] = final
    out_ref[...] = final.astype(F32)


def total(i, count, where, one, part, far, final, after):
    length, depth = one.shape
    quarter = length // 4
    rows = rows_block(quarter, depth)
    carried = [] if final is None else [final]
    return launch(
        total_kernel, "total", where, (one, part, far, *carried),
        [rows] * 3 + [ANY] * len(carried),
        [shape((count, length, depth), BF16), shape((length, depth), F32)],
        [pl.BlockSpec((1, quarter, depth), lambda g, w: (2 * w[1] + i, g, 0)), rows],
        (4,), 10, after, streamed=(3,) if carried else (0,), stored=(0,),
        aliases={4: 0} if carried else {},
    )


def head_products_kernel(where_ref, *refs, count):
    def take(number):
        nonlocal refs
        taken, refs = refs[:number], refs[number:]
        return taken

    def summed(lefts, rights):
        total = None
        for n in range(count):
            left = jnp.concatenate([lefts[2 * n], lefts[2 * n + 1]], axis=1)
            part = dot(left, rights[n], 0, 0)
            total = part if total is None else total + part
        return total

    firsts, seconds, ones = take(2 * count), take(2 * count), take(2 * count)
    grads, mixed, first_sums, second_sums = take(count), take(count), take(2 * count), take(2 * count)
    width = mixed[0].shape[2] // 2
    x_first, x_second = ([ref[0] for ref in group] for group in (firsts, seconds))
    kept_ref, *sent_refs = refs
    for group in range(2):
        start = 3 * group * width
        pairs = [ref[:, start : start + 2 * width] for ref in grads]
        heads = summed(x_first, pairs)
        values = summed(x_second, [ref[:, start + 2 * width : start + 3 * width] for ref in grads])
        outputs = summed(
            [ref[...] for ref in ones], [ref[0, :, group * width : (group + 1) * width] for ref in mixed]
        )
        for step in range(2):
            rows = slice(step * BLOCK, (step + 1) * BLOCK)
            out = sent_refs[step] if group else kept_ref.at[step]
            out[0:BLOCK, :] = heads[rows, 0:width]
            out[BLOCK : 2 * BLOCK, :] = heads[rows, width:]
            out[2 * BLOCK : 3 * BLOCK, :] = values[rows, :]
            out[3 * BLOCK : 4 * BLOCK, :] = outputs[rows, :]
            out[4 * BLOCK :, :] = jnp.zeros((8, width), F32)
            for row, sums in ((0, first_sums), (2, second_sums)):
                gains = sums[step][0:2, :]
                for n in range(1, count):
                    gains = gains + sums[2 * n + step][0:2, :]
                last = 4 * BLOCK + row
                out[last : last + 2, 0:BLOCK] = gains


def head_products(pair, where, x, ones, grads, mixed, firsts, seconds, after):
    _, length, depth = x.shape
    count = len(ones)
    width = mixed[0].shape[2] // 2

    def tile(way, step, dims, lead=()):
        return pl.BlockSpec(
            (*dims, BLOCK),
            lambda j, w: (*[f(w) for f in lead], 0, w[4 + 2 * (2 * pair + step) + way]),
        )

    def inputs_of(way):
        return [
            tile(way, step, (1, length), (lambda w, i=i: 2 * w[1] + i,))
            for i in range(count) for step in range(2)
        ]

    out = shape((4 * BLOCK + 8, width), F32)
    outs = [shape((2, *out.shape), F32), out, out]
    twice = lambda arrays: [a for a in arrays for _ in range(2)]
    return launch(
        functools.partial(head_products_kernel, count=count), "head_products", where,
        (
            *[x] * (4 * count), *twice(ones), *grads, *mixed, *twice(firsts), *twice(seconds)
        ),
        inputs_of(0) + inputs_of(1) + [tile(1, step, (length,)) for _ in ones for step in range(2)]
        + [RESIDENT] * (2 * count)
        + [tile(1, step, (8,)) for _ in range(2 * count) for step in range(2)],
        outs, [whole_block(o) for o in outs], (1,), 12, after, streamed=range(6 * count),
    )


def ring_kernel(where_ref, *refs, arrivals, sizes):
    outs = refs[-2:]
    sources = refs[arrivals : -2]
    for way in range(2):
        mine, start = [], 0
        count = sizes[way]
        kept = sources[way * sizes[0] : way * sizes[0] + count]
        base = sizes[0] + sizes[1]
        near = sources[base + way * sizes[0] : base + way * sizes[0] + count]
        for left, right in zip(kept, near):
            value = left[...].reshape(left.shape[-2:]) + right[...].reshape(right.shape[-2:])
            rows = slice(start, start + value.shape[0])
            if arrivals:
                value = refs[way][rows, :] + value
            outs[way][rows, :] = value
            start += value.shape[0]


def ring_step(where, arrived, kept, near, after, stored=()):
    entries = [*kept[0], *kept[1], *near[0], *near[1]]
    specs = [whole_block(a) for a in arrived]
    specs += [pl.BlockSpec(dims, lambda i, w, at=at: at) for _, dims, at in entries]
    outs = [
        shape((sum(e[1][-2] for e in way), way[0][1][-1]), F32) for way in kept
    ]
    return launch(
        functools.partial(ring_kernel, arrivals=len(arrived), sizes=(len(kept[0]), len(kept[1]))),
        "ring_step", where, (*arrived, *[e[0] for e in entries]), specs, outs,
        [whole_block(o) for o in outs], (1,), 8, after, stored=stored,
    )


def last_kernel(where_ref, left_ref, right_ref, *refs):
    kept, near, outs = refs[0:3], refs[3:6], refs[6:]
    top, middle, low = (
        k[...].reshape(k.shape[-2:]) + n[...].reshape(n.shape[-2:]) for k, n in zip(kept, near)
    )
    left = left_ref[...] + top
    right = right_ref[0 : 2 * BLOCK, :] + middle
    low = right_ref[2 * BLOCK :, :] + low
    outs[0][...] = left[0:BLOCK, :]
    outs[1][...] = left[BLOCK:, :]
    outs[2][...] = right[0:BLOCK, :]
    outs[3][...] = right[BLOCK:, :].T
    for row, out in enumerate(outs[4:]):
        out[...] = low[row : row + 1, 0:BLOCK]


def last_step(where, arrived, kept, near, after):
    entries = [*kept[0], *kept[1], *near[0], *near[1]]
    specs = [whole_block(a) for a in arrived]
    specs += [pl.BlockSpec(dims, lambda i, w, at=at: at) for _, dims, at in entries]
    width = arrived[0].shape[1]
    outs = [shape((BLOCK, width), F32)] * 3 + [shape((width, BLOCK), F32)]
    outs += [shape((1, BLOCK), F32)] * 4
    return launch(
        last_kernel, "last_step", where, (*arrived, *[e[0] for e in entries]), specs, outs,
        [whole_block(o) for o in outs], (1,), 8, after, stored=range(8),
    )


def turn_kernel(where_ref, value_ref, out_ref):
    out_ref[...] = value_ref[...].T


def turn(where, value, after):
    out = shape(value.shape[::-1], F32)
    return launch(
        turn_kernel, "turn", where, (value,), [whole_block(value)], [out], [whole_block(out)],
        (1,), 6, after, stored=(0,),
    )[0]


def hold_kernel(where_ref, *refs):
    *pairs, arrived = refs
    count = len(pairs) // 2
    copies = [
        pltpu.make_async_copy(pairs[n], pairs[count + n], arrived.at[n]) for n in range(count)
    ]
    for copy in copies:
        copy.start()
    for copy in copies:
        copy.wait()


def hold(where, *values, after):
    count = len(values)
    token = shape((8, 128), F32)

    def run(where_ref, *refs):
        refs[2 * count][...] = jnp.zeros((8, 128), F32)
        hold_kernel(where_ref, *refs[: 2 * count], refs[-1])

    return launch(
        run, "hold", where, values, [ANY] * count,
        [*[pltpu.VMEM(v.shape, v.dtype) for v in values], token],
        [*[RESIDENT] * count, whole_block(token)], (1,), 4, after, streamed=range(count),
        scratch=[pltpu.SemaphoreType.DMA((count,))],
    )[:count]


def clip_kernel(where_ref, query_ref, key_ref, factor_ref, query_out, key_out):
    query_out[...] = query_ref[...].astype(F32) * factor_ref[...]
    key_out[...] = key_ref[...].astype(F32) * factor_ref[...]


def clip(where, query, key, factor, after):
    specs = [rows_block(query.shape[0] // 4, query.shape[1])] * 2
    return launch(
        clip_kernel, "clip", where, (query, key, factor), [*specs, whole_block(factor)],
        [shape(query.shape, F32)] * 2, specs, (4,), 8, after, streamed=(0, 1), stored=(0, 1),
    )


def finish_kernel(where_ref, *refs):
    *halves, final_ref, out_ref, token_ref = refs
    del final_ref
    value = halves[0][...].reshape(out_ref.shape[1:])
    if len(halves) == 2:
        value = jnp.where(pl.program_id(0) == 0, value, halves[1][...])
    out_ref[0] = value.astype(BF16)
    token_ref[...] = jnp.zeros_like(token_ref)


def finish(i, where, values, final, after):
    half, depth = final.shape[1] // 2, final.shape[2]
    specs = [rows_block(half, depth)]
    if len(values) == 2:
        specs = [whole_block(v) for v in values]
    last = len(values)
    token = shape((8, 128), F32)
    return launch(
        finish_kernel, "finish", where, (*values, final), [*specs, ANY],
        [shape(final.shape, BF16), token],
        [
            pl.BlockSpec((1, half, depth), lambda g, w: (2 * (1 - w[1]) + i, g, 0)),
            whole_block(token),
        ],
        (2,), 10, after, aliases={last + 1: 0}, stored=(0,), streamed=(last,),
    )[0]


def solution(mesh):
    ranks = mesh.shape["dp"]
    group = mesh.shape["tensor"]
    assert group == 4 and ranks % 8 == 0
    near_pairs = [(t, t ^ 1) for t in range(group)]
    far_pairs = [(t, t ^ 2) for t in range(group)]
    turns = (
        [(RING[p], RING[(p + 1) % 8]) for p in range(8)],
        [(RING[p], RING[(p - 1) % 8]) for p in range(8)],
    )

    def near(value):
        return lax.ppermute(value, "tensor", near_pairs)

    def scatter(value):
        return lax.psum_scatter(value, "dp", scatter_dimension=0, tiled=True)

    def far(value):
        return lax.ppermute(value, "tensor", far_pairs)

    def body(
        block_input, segment_ids, query_weight, key_weight, value_weight, output_weight,
        first_gain, first_shift, up_weight, down_weight, second_gain, second_shift, out_grad,
    ):
        count, length, depth = block_input.shape
        width = query_weight.shape[1]
        part = depth // ranks
        mine = range(count // 2)
        me = lax.axis_index("tensor")
        rank = lax.axis_index("dp")
        natural = [n for n in range(8) for _ in range(2)]
        owners = jnp.asarray(OWNERS if ranks == 8 else [natural], jnp.int32)
        owners = lax.dynamic_index_in_dim(owners, rank if ranks == 8 else 0, 0, False)
        where = jnp.concatenate(
            [jnp.stack([me, me % 2, me // 2, rank]).astype(jnp.int32), owners]
        )
        seg = jnp.broadcast_to(segment_ids[:, None, :], (count, 8, length))
        gain_one, shift_one = first_gain[None], first_shift[None]
        gain_two, shift_two = second_gain[None], second_shift[None]
        order = Order()

        def then(call, *args, **kwargs):
            return call(*args, after=order, **kwargs)

        own_low, own_wide, wo_half = then(
            widen_heads, where, query_weight, key_weight, value_weight, output_weight
        )
        near_wide, wo_first = near(own_wide), far(wo_half)
        wide = convert(where, up_weight, down_weight, dtype=F32, after=Order())
        wide_near = [near(w) for w in wide]
        weights, wo_near = then(narrow_near, where, own_low, near_wide, output_weight)
        heads, mixed_far = [], []
        for i in mine:
            heads.append(then(attend, i, where, block_input, weights, seg))
            mixed_far.append(far(heads[i][3]))
            if i == 0:
                (wo_first,) = then(gate, where, wo_first)
                wo_second = lax.ppermute(wo_first, "dp", [(r, r ^ 1) for r in range(ranks)])
                wo_both = [near(wo_first)]
        mixed_low, qkv, tops, mixed = zip(*heads)
        up_near, down_near = then(convert, where, *wide_near, dtype=BF16)
        ups, downs = (up_weight, up_near), (down_weight, down_near)
        (wo_second,) = then(gate, where, wo_second)
        wo_both.append(near(wo_second))
        wo = then(assemble, where, output_weight, wo_near, (wo_first, wo_second), wo_both)

        forwards, part_far = [], []
        for i in mine:
            forwards.append(
                then(
                    forward, i, where, block_input, mixed[i], mixed_far[i], wo, gain_one,
                    shift_one, ups, downs,
                )
            )
            part_far.append(far(forwards[i][5]))

        heads_own = width // HEAD_DIM
        peak = functools.reduce(jnp.maximum, tops)
        peak = jnp.maximum(peak[:heads_own], near(peak)[heads_own:])
        step = 1
        while step < ranks:
            peak = jnp.maximum(peak, lax.ppermute(peak, "dp", [(i, i ^ step) for i in range(ranks)]))
            step *= 2
        factor = jnp.sqrt(CLIP / jnp.maximum(peak[:, 0], CLIP))
        factor = jnp.repeat(factor, HEAD_DIM)[None]
        query_clipped, key_clipped = then(clip, where, query_weight, key_weight, factor)

        written = {"layer_out": None, "input_grad": None}
        def finish_layer(i, values):
            written["layer_out"] = then(finish, i, where, values, written["layer_out"])

        backs, slope_parts, slope_far = [], [], []
        for i in mine:
            normed, scaled, low, active, pull, part_sum = forwards[i]
            weights_of = ups, downs
            if i > 0:
                normed, pull, *held = then(hold, where, normed, pull, *ups, *downs)
                weights_of = held[0:2], held[2:4]
            backs.append(
                then(
                    backward, i, where, normed, gain_one, shift_one, part_sum, part_far[i],
                    out_grad, gain_two, shift_two, pull, *weights_of, written["layer_out"],
                    resident=i > 0,
                )
            )
            written["layer_out"], *out, slope, slope_low, before, sums, part_sum = backs[i]
            backs[i] = (out, slope, slope_low, before, sums)
            slope_parts.append(part_sum)
            slope_far.append(far(part_sum))
            if i == 0:
                finish_layer(0, [near(v) for v in out])

        lows, actives = [f[2] for f in forwards], [f[3] for f in forwards]
        slope_lows, befores = [b[2] for b in backs], [b[3] for b in backs]
        def send(held):
            return [lax.ppermute(h, "dp", t) for h, t in zip(held, turns)]

        ff_blocks = {}

        def ff_part(*steps, apart=True):
            kept, *sent = then(products, steps, apart, where, lows, slope_lows, befores, actives)
            sent = [near(a) for a in sent]
            for index, n in enumerate(steps):
                mine = sent[:2] if index == 0 and apart else sent[index + int(apart)]
                ff_blocks[n] = (kept, index, mine)

        def ff_step(n, arrived):
            kept, index, sent = ff_blocks[n]
            dims = (1, 1, BLOCK, kept.shape[3])
            if isinstance(sent, list):
                near = [[(array, dims[2:], (0, 0))] for array in sent]
            else:
                near = [[(sent, dims[1:], (way, 0, 0))] for way in range(2)]
            return then(
                ring_step, where, arrived,
                [[(kept, dims, (index, way, 0, 0))] for way in range(2)], near,
                stored=range(2) if n == 7 else (),
            )

        def ff_ring():
            held = ff_step(0, ())
            for n in range(1, 8):
                arrived = send(held)
                yield None
                held = ff_step(n, arrived)
            yield held

        head_parts = []

        def head_part(pair):
            kept, *sent = then(
                head_products, pair, where, block_input, [f[1] for f in firsts],
                [o[1] for o in owns], mixed_low, [f[3] for f in firsts], [b[4] for b in backs],
            )
            head_parts.append((kept, [near(a) for a in sent]))

        def head_step(n, arrived):
            kept, sent = head_parts[n // 2]

            def entries(array, lead):
                block = lambda rows, at: (
                    array, (*[1 for _ in lead], rows, width), (*lead, at, 0)
                )
                return [[block(2 * BLOCK, 0)], [block(2 * BLOCK, 1), block(8, 4 * BLOCK // 8)]]

            call = last_step if n == 7 else ring_step
            return then(call, where, arrived, entries(kept, (n % 2,)), entries(sent[n % 2], ()))

        def head_ring():
            held = head_step(0, ())
            for n in range(1, 8):
                arrived = send(held)
                yield None
                held = head_step(n, arrived)
            yield held

        def total_input(i):
            one, own = (firsts[i][0], owns[i][0]) if i == 0 else summands
            written["input_grad"], result = then(
                total, i, count, where, one, own, input_far[i], written["input_grad"]
            )
            return result

        def finish_input(i, value):
            written["input_grad"] = then(finish, i, where, [value], written["input_grad"])

        def first_back(i):
            firsts.append(
                then(
                    first, where, slope_parts[i], slope_far[i], backs[i][1], *forwards[i][:2],
                    gain_one, wo,
                )
            )

        def own_back(i):
            owns.append(then(attend_back, i, where, qkv[i], firsts[i][2], mixed[i], seg, weights))

        firsts, owns, input_far = [], [], []
        ring = ff_ring() if ranks == 8 else iter(())
        ff_part(0)
        ff_part(1, 2)
        next(ring, None)
        next(ring, None)
        ff_part(3, 4)
        first_back(0)
        next(ring, None)
        own_back(0)
        next(ring, None)
        ff_part(5, 6, 7)
        next(ring, None)
        slope_far[1], own_part = then(gate, where, slope_far[1], owns[0][0])
        owns[0] = (own_part, owns[0][1])
        input_far.append(far(own_part))
        first_back(1)
        next(ring, None)
        own_back(1)
        next(ring, None)
        head_part(0)
        head_part(1)
        head_part(2)
        if ranks == 8:
            *_, (up_grad, down_grad) = ring
        (own_part,) = then(gate, where, owns[1][0])
        owns[1] = (own_part, owns[1][1])
        input_far.append(far(own_part))
        ring = head_ring() if ranks == 8 else iter(())
        next(ring, None)
        head_part(3)
        next(ring, None)
        next(ring, None)
        rows = total_input(0)
        next(ring, None)
        (rows,) = then(gate, where, rows)
        rows = near(rows)
        summands = then(hold, where, firsts[1][0], owns[1][0])
        next(ring, None)
        if ranks == 8:
            down_grad = then(turn, where, down_grad)
        next(ring, None)
        result = total_input(1)
        next(ring, None)
        result, layer = then(gate, where, result, *backs[1][0])
        result, layer = near(result), near(layer)
        finish_input(0, rows)
        finish_input(1, result)
        finish_layer(1, [layer])

        if ranks == 8:
            *_, (query_grad, key_grad, value_grad, output_grad, *gains) = ring
            gains = [g.reshape(BLOCK) for g in gains]
        else:
            def rows_of(value, start, rows=BLOCK):
                return scatter(value[:, start : start + rows].reshape(8 * rows, width))

            up, down = [
                jnp.concatenate(
                    [kept[at, way] + sent[way] for kept, at, sent in map(ff_blocks.get, range(8))],
                    axis=0,
                )
                for way in range(2)
            ]
            up_grad, down_grad = scatter(up), scatter(down).T
            value = jnp.concatenate([k + jnp.stack(s) for k, s in head_parts], axis=0)
            query_grad, key_grad, value_grad = (rows_of(value, n * BLOCK) for n in range(3))
            output_grad = rows_of(value, 3 * BLOCK).T
            gains = value[:, 4 * BLOCK : 4 * BLOCK + 4, :BLOCK].transpose(0, 2, 1)
            gains = scatter(gains.reshape(depth, 4)).T

        return (
            written["layer_out"], written["input_grad"], query_grad, key_grad, value_grad, output_grad,
            gains[0], gains[1], up_grad, down_grad, gains[2], gains[3],
            query_clipped, key_clipped,
        )

    batch = P("dp", None, None)
    in_specs = (
        batch, P("dp", None), P(None, "tensor"), P(None, "tensor"), P(None, "tensor"),
        P("tensor", None), P(), P(), P(None, "tensor"), P("tensor", None), P(), P(), batch,
    )
    out_specs = (
        batch, batch, P("dp", "tensor"), P("dp", "tensor"), P("dp", "tensor"), P("tensor", "dp"),
        P("dp"), P("dp"), P("dp", "tensor"), P("tensor", "dp"), P("dp"), P("dp"),
        P(None, "tensor"), P(None, "tensor"),
    )
    return jax.shard_map(body, mesh=mesh, in_specs=in_specs, out_specs=out_specs, check_vma=False)
```

```python
import functools

import jax
import jax.numpy as jnp
from jax import lax
from jax.experimental import pallas as pl
from jax.experimental.pallas import tpu as pltpu
from jax.sharding import PartitionSpec as P

F32 = jnp.float32
BF16 = jnp.bfloat16
HEAD_DIM = 64
FAR = -1e30
EPS = 1e-06
CLIP = 10.0
SCALE = HEAD_DIM**-0.5
ROOT_HALF = 0.5**0.5
BELL = 0.3989422804014327
GROUP = 4
BLOCK = 128
DOCS = 4
MIB = 1 << 20
RING = (0, 2, 4, 6, 7, 5, 3, 1)
OWNERS = tuple(
    tuple(RING[(RING.index(r) + way * (1 + n)) % 8] for n in range(8) for way in (-1, 1))
    for r in range(8)
)
ANY = pl.BlockSpec(memory_space=pl.ANY)
RESIDENT = pl.BlockSpec(memory_space=pltpu.VMEM)


def dot(left, right, left_dim=1, right_dim=0):
    return lax.dot_general(
        left, right, (((left_dim,), (right_dim,)), ((), ())), preferred_element_type=F32
    )


def normalize(total):
    average = jnp.mean(total, axis=-1, keepdims=True)
    centred = total - average
    variance = jnp.mean(centred * centred, axis=-1, keepdims=True)
    scaled = lax.rsqrt(variance + EPS)
    return centred * scaled, scaled


def norm_back(upstream, normed, scaled, gain):
    weighted = upstream * gain
    first = jnp.mean(weighted, axis=-1, keepdims=True)
    second = jnp.mean(weighted * normed, axis=-1, keepdims=True)
    return scaled * (weighted - first - normed * second)


def lanes(width):
    lane = lax.broadcasted_iota(jnp.int32, (1, width), 1)
    return lane // HEAD_DIM, lane % HEAD_DIM


def split(value):
    high = value.astype(BF16)
    rest = value - high.astype(F32)
    middle = rest.astype(BF16)
    return high, middle, (rest - middle.astype(F32)).astype(BF16)


def pick(head, owner, own, spare, zero):
    return jnp.where(owner == head, own, jnp.where(owner == (head + 1) % GROUP, spare, zero))


def spare_columns(seg_rows, sums, group, width):
    owner, lane = lanes(width)
    row8 = lax.broadcasted_iota(jnp.int32, (8, 1), 0)
    equal = jnp.where(seg_rows == row8, 1.0, 0.0)
    rows = [equal]
    wanted = [jnp.where(lane == row8, FAR, 0.0)]
    if sums is not None:
        head = row8 % GROUP
        here = (row8 // GROUP == group) & ((head + 1) % GROUP == owner)
        for n, value in enumerate(split(sums)):
            rows.append(value.astype(F32))
            wanted.append(jnp.where(here & (lane == DOCS + n), -1.0, 0.0))
    placed = jnp.concatenate(wanted, axis=0).astype(BF16)
    queries = dot(jnp.concatenate(rows, axis=0).astype(BF16), placed, 0, 0).astype(BF16)
    ones = jnp.where((lane >= DOCS) & (lane < DOCS + 3), 1.0, 0.0)
    placed = jnp.where((lane == row8) & (row8 < DOCS), 1.0, 0.0).astype(BF16)
    differ = jnp.where(seg_rows == row8, 0.0, 1.0).astype(BF16)
    keys = (dot(differ, placed, 0, 0) + ones).astype(BF16)
    return queries, keys


def shape(dims, dtype):
    return jax.ShapeDtypeStruct(tuple(dims), dtype)


def whole_block(array):
    zeros = (0,) * len(array.shape)
    return pl.BlockSpec(tuple(array.shape), lambda i, w: zeros)


def rows_block(rows, columns):
    return pl.BlockSpec((rows, columns), lambda i, w: (i, 0))


class Order:
    def __init__(self):
        self.token, self.stored = None, False

    def taken(self):
        if self.token is None:
            return []
        if self.stored:
            return [pltpu.with_memory_space_constraint(self.token, pltpu.HBM)]
        return [self.token]

    def give(self, results, stored):
        sizes = [r.size * jnp.dtype(r.dtype).itemsize for r in results]
        index = sizes.index(min(sizes))
        self.token, self.stored = results[index], index in stored


def launch(
    kernel, name, where, inputs, in_specs, outs, out_specs, grid, vmem, after,
    scratch=(), aliases=None, streamed=(), stored=(),
):
    count = len(inputs)
    tokens = after.taken()
    inputs = [
        pltpu.with_memory_space_constraint(value, pltpu.HBM) if i in streamed else value
        for i, value in enumerate(inputs)
    ]
    outs = [
        pltpu.HBM(value.shape, value.dtype) if i in stored else value
        for i, value in enumerate(outs)
    ]

    def run(where_ref, *refs):
        kernel(where_ref, *refs[:count], *refs[count + len(tokens) :])

    results = pl.pallas_call(
        run,
        grid_spec=pltpu.PrefetchScalarGridSpec(
            num_scalar_prefetch=1,
            grid=grid,
            in_specs=list(in_specs) + [ANY] * len(tokens),
            out_specs=list(out_specs),
            scratch_shapes=list(scratch),
        ),
        out_shape=outs,
        input_output_aliases=aliases or {},
        compiler_params=pltpu.CompilerParams(
            vmem_limit_bytes=vmem * MIB, dimension_semantics=("arbitrary",) * len(grid)
        ),
        cost_estimate=pl.CostEstimate(flops=1, bytes_accessed=1, transcendentals=0),
        name=name,
    )(where, *inputs, *tokens)
    after.give(results, stored)
    return results


def gate_kernel(*refs):
    del refs


def gate(where, *values, after):
    outs = [shape(v.shape, v.dtype) for v in values]
    return launch(
        gate_kernel, "gate", where, values, [ANY] * len(values), outs, [ANY] * len(values), (1,),
        2, after, aliases={i + 1: i for i in range(len(values))},
    )


def widen_heads_kernel(where_ref, wq_ref, wk_ref, wv_ref, wo_ref, own, wide, wo):
    width = wq_ref.shape[1]
    for index, ref in enumerate((wq_ref, wk_ref, wv_ref)):
        columns = slice(index * width, (index + 1) * width)
        value = ref[...]
        own[:, columns] = value
        wide[:, columns] = value.astype(F32)
    rows, depth = wo_ref.shape
    for index in range(depth // width):
        wide[index * rows : (index + 1) * rows, 3 * width :] = wo_ref[
            :, index * width : (index + 1) * width
        ].astype(F32)
    half = rows // 2
    wo[...] = wo_ref[pl.ds(pl.multiple_of((where_ref[3] % 2) * half, half), half), :].astype(F32)


def widen_heads(where, wq, wk, wv, wo, after):
    depth, width = wq.shape
    outs = [
        shape((depth, 3 * width), BF16),
        shape((depth, 4 * width), F32),
        shape((wo.shape[0] // 2, depth), F32),
    ]
    inputs = (wq, wk, wv, wo)
    return launch(
        widen_heads_kernel, "widen_heads", where, inputs, [whole_block(a) for a in inputs], outs,
        [whole_block(o) for o in outs], (1,), 12, after, streamed=range(4),
    )


def assemble_kernel(where_ref, own_ref, near_ref, *refs):
    *halves, out_ref = refs
    rows = own_ref.shape[0]
    half = rows // 2
    mine = where_ref[2] * 2 * rows
    other = (1 - where_ref[2]) * 2 * rows
    out_ref[pl.ds(pl.multiple_of(mine, rows), rows), :] = own_ref[...]
    out_ref[pl.ds(pl.multiple_of(mine + rows, rows), rows), :] = near_ref[...]
    parity = where_ref[3] % 2
    for start, first, second in ((other, *halves[0:2]), (other + rows, *halves[2:4])):
        for ref, place in ((first, parity), (second, 1 - parity)):
            begin = pl.multiple_of(start + place * half, half)
            out_ref[pl.ds(begin, half), :] = ref[...].astype(BF16)


def assemble(where, own, near, far, both, after):
    rows, columns = own.shape
    out = shape((4 * rows, columns), BF16)
    inputs = (own, near, *far, *both)
    return launch(
        assemble_kernel, "assemble", where, inputs, [whole_block(a) for a in inputs], [out],
        [whole_block(out)], (1,), 14, after,
    )[0]


def narrow_near_kernel(where_ref, own_ref, wide_ref, heads_ref, wo_ref):
    width = own_ref.shape[1] // 3
    heads_ref[0] = own_ref[...]
    heads_ref[1] = wide_ref[:, 0 : 3 * width].astype(BF16)
    rows, depth = wo_ref.shape
    for index in range(depth // width):
        wo_ref[:, index * width : (index + 1) * width] = wide_ref[
            index * rows : (index + 1) * rows, 3 * width :
        ].astype(BF16)


def narrow_near(where, own, wide, wo, after):
    outs = [shape((2, *own.shape), BF16), shape(wo.shape, BF16)]
    return launch(
        narrow_near_kernel, "narrow_near", where, (own, wide),
        [whole_block(own), whole_block(wide)], outs, [whole_block(o) for o in outs], (1,), 16,
        after,
    )


def convert_kernel(where_ref, *refs):
    half = len(refs) // 2
    for source, target in zip(refs[:half], refs[half:]):
        target[...] = source[...].astype(target.dtype)


def convert(where, *values, dtype, after):
    specs = [rows_block(v.shape[0] // 4, v.shape[1]) for v in values]
    held = range(len(values))
    wide = dtype == F32
    return launch(
        convert_kernel, "convert", where, values, specs, [shape(v.shape, dtype) for v in values],
        specs, (4,), 10, after, streamed=held if wide else (), stored=() if wide else held,
    )


def project_group(x, weights):
    width = weights.shape[1] // 3
    q = (dot(x, weights[:, 0:width]).astype(BF16) * SCALE).astype(BF16)
    k = dot(x, weights[:, width : 2 * width]).astype(BF16)
    v = dot(x, weights[:, 2 * width : 3 * width]).astype(BF16)
    return q, k, v


def attend_kernel(
    where_ref, x_ref, weights_ref, seg_ref, low_ref, qkv_ref, top_ref, o_ref, held_ref
):
    x = x_ref[0]
    width = weights_ref.shape[2] // 3
    owner, _ = lanes(width)
    spare_q, spare_k = spare_columns(seg_ref[0], None, 0, width)
    zero = jnp.zeros((), BF16)
    held_ref[...] = jnp.zeros_like(held_ref)
    groups = [project_group(x, weights_ref.at[group]) for group in range(2)]
    for group, values in enumerate(groups):
        for index, value in enumerate(values):
            start = (3 * group + index) * width
            qkv_ref[0, :, start : start + width] = value

    def scores_of(group, head):
        queries, keys, _ = groups[group]
        return dot(
            pick(head, owner, queries, spare_q, zero),
            jnp.where(owner == head, keys, spare_k), 1, 1,
        )

    for group in range(2):
        total = jnp.zeros(groups[group][0].shape, F32)
        for head in range(GROUP):
            row = group * GROUP + head
            scores = scores_of(group, head)
            top = jnp.max(scores, axis=-1, keepdims=True)
            raised = jnp.exp(scores - top)
            summed = jnp.sum(raised, axis=-1, keepdims=True)
            chances = raised * (1.0 / summed)
            total = total + dot(
                chances.astype(BF16), jnp.where(owner == head, groups[group][2], zero)
            )
            held_ref[:, row : row + 1] = top + jnp.log(summed)
            top_ref[row : row + 1, :] = jnp.broadcast_to(
                jnp.max(top, axis=0, keepdims=True), (1, top_ref.shape[1])
            )
        low = total.astype(BF16)
        low_ref[0, :, group * width : (group + 1) * width] = low
        o_ref[0 : x.shape[0], group * width : (group + 1) * width] = low.astype(F32)
    o_ref[x.shape[0] :, :] = held_ref[...].T[0:8, :]


def sequence(i, dims):
    return pl.BlockSpec((1, *dims), lambda g, w: (2 * w[1] + i, 0, 0))


def attend(i, where, x, weights, seg, after):
    _, length, depth = x.shape
    columns = weights.shape[2]
    width = columns // 3
    outs = [
        shape((1, length, 2 * width), BF16),
        shape((1, length, 2 * columns), BF16),
        shape((2 * GROUP, 128), F32),
        shape((length + 2 * GROUP, 2 * width), F32),
    ]
    out_specs = [whole_block(o) for o in outs]
    return launch(
        attend_kernel, "attend", where, (x, weights, seg),
        [sequence(i, (length, depth)), RESIDENT, sequence(i, (8, length))],
        outs, out_specs, (1,), 20, after, streamed=(0,), stored=(0, 1),
        scratch=[pltpu.VMEM((length, 128), F32)],
    )


def fetch(sources, held_ref, arrived):
    first = pl.program_id(0) == 0
    copies = [
        pltpu.make_async_copy(source, held_ref.at[n], arrived.at[n])
        for n, source in enumerate(sources)
    ]

    @pl.when(first)
    def _():
        for copy in copies:
            copy.start()

    def get(n):
        @pl.when(first)
        def _():
            copies[n].wait()

        return held_ref[n]

    return get


def forward_kernel(
    where_ref, x_ref, mixed_ref, mixed_far_ref, wo_ref, gain_ref,
    shift_ref, up_own, up_near, down_own, down_near,
    normed_ref, scaled_ref, low_ref, active_ref, pull_ref, part_ref, both_ref, held_ref, arrived,
):
    weight = fetch((up_own, down_own, up_near, down_near), held_ref, arrived)
    width = mixed_ref.shape[1]
    chip = where_ref[2]
    both_ref[:, pl.ds(pl.multiple_of(chip * width, width), width)] = mixed_ref[...].astype(BF16)
    both_ref[:, pl.ds(pl.multiple_of((1 - chip) * width, width), width)] = mixed_far_ref[
        ...
    ].astype(BF16)
    normed, scaled = normalize(x_ref[0].astype(F32) + dot(both_ref[...], wo_ref[...]))
    normed_ref[...] = normed
    scaled_ref[...] = jnp.broadcast_to(scaled, scaled_ref.shape)
    low = (normed * gain_ref[...] + shift_ref[...]).astype(BF16)
    low_ref[...] = low
    hidden = up_own.shape[1]
    parts = []
    for group in range(2):
        columns = slice(group * hidden, (group + 1) * hidden)
        before = dot(low, weight(2 * group))
        chance = 0.5 * (1.0 + lax.erf(before * ROOT_HALF))
        active = (before * chance).astype(BF16)
        active_ref[:, columns] = active
        pull_ref[:, columns] = chance + before * (jnp.exp(-0.5 * before * before) * BELL)
        parts.append(dot(active, weight(2 * group + 1)))
    part_ref[...] = parts[0] + parts[1]


def fetched(array):
    return [pltpu.VMEM((4, *array.shape), array.dtype), pltpu.SemaphoreType.DMA((4,))]


def forward(i, where, x, mixed, mixed_far, wo, gain, shift, ups, downs, after):
    _, length, depth = x.shape
    width = mixed.shape[1]
    hidden = 2 * ups[0].shape[1]
    half = length // 2
    pieces = rows_block(half, width)
    outs = [
        shape((length, depth), F32),
        shape((length, 128), F32),
        shape((length, depth), BF16),
        shape((length, hidden), BF16),
        shape((length, hidden), F32),
    ]
    out_specs = [rows_block(half, o.shape[1]) for o in outs]
    outs.append(shape((length, depth), F32))
    out_specs.append(rows_block(half, depth))
    return launch(
        forward_kernel, "forward", where, (x, mixed, mixed_far, wo, gain, shift, *ups, *downs),
        [
            pl.BlockSpec((1, half, depth), lambda g, w: (2 * w[1] + i, g, 0)),
            pieces,
            pieces,
            RESIDENT,
            whole_block(gain),
            whole_block(shift),
            *[ANY] * 4,
        ],
        outs, out_specs, (2,), 30, after,
        streamed=(0, 6, 7, 8, 9), stored=(0, 1, 2, 3, 4),
        scratch=[pltpu.VMEM((half, 2 * width), BF16), *fetched(ups[0])],
    )


def backward_kernel(
    where_ref, normed_ref, gain_ref, shift_ref, grad_ref, second_gain_ref, second_shift_ref,
    pull_ref, up_own, up_near, down_own, down_near, part_ref, part_far_ref, *rest, carried, resident,
):
    (
        final_ref, *out_refs, slope_ref, slope_low_ref, before_ref, sums_ref, part_out_ref
    ) = rest[carried : len(rest) - (0 if resident else 2)]
    scratch = rest[-2:]
    weights = (down_own, up_own, down_near, up_near)
    if resident:
        weight = lambda n: weights[n][...]
    else:
        weight = fetch(weights, *scratch)
    step = pl.program_id(0)
    hidden = normed_ref[...] * gain_ref[...] + shift_ref[...]
    normed, scaled = normalize(hidden + (part_ref[...] + part_far_ref[...]))
    out = (normed * second_gain_ref[...] + second_shift_ref[...]).astype(BF16)
    final_ref[0] = out
    if len(out_refs) == 1:
        out_refs[0][...] = out.astype(F32)
    for index, ref in enumerate(out_refs if len(out_refs) == 2 else ()):

        @pl.when(step == index)
        def _(ref=ref):
            ref[...] = out.astype(F32)

    upstream = grad_ref[0].astype(F32)

    @pl.when(step == 0)
    def _():
        sums_ref[...] = jnp.zeros_like(sums_ref)

    sums_ref[0:1, :] += jnp.sum(upstream * normed, axis=0, keepdims=True)
    sums_ref[1:2, :] += jnp.sum(upstream, axis=0, keepdims=True)
    slope = norm_back(upstream, normed, scaled, second_gain_ref[...])
    slope_ref[...] = slope
    low = slope.astype(BF16)
    slope_low_ref[...] = low
    units = up_own.shape[1]
    parts = []
    for group in range(2):
        columns = slice(group * units, (group + 1) * units)
        before = (dot(low, weight(2 * group), 1, 1) * pull_ref[:, columns]).astype(BF16)
        before_ref[:, columns] = before
        parts.append(dot(before, weight(2 * group + 1), 1, 1))
    part_out_ref[...] = parts[0] + parts[1]


def backward(
    i, where, normed, gain, shift, part, part_far, out_grad, second_gain, second_shift, pull,
    ups, downs, final, after, resident,
):
    count, length, depth = out_grad.shape
    hidden = 2 * ups[0].shape[1]
    half = length // 2
    outs = [
        shape((length, depth), F32),
        shape((length, depth), BF16),
        shape((length, hidden), BF16),
        shape((8, depth), F32),
        shape((length, depth), F32),
    ]
    out_specs = [rows_block(half, o.shape[1]) for o in outs]
    out_specs[3] = whole_block(outs[3])
    halves = 2 if final is None else 1
    value = shape((length // halves, depth), F32)
    outs = [value] * halves + outs
    out_specs = [whole_block(value) if halves == 2 else rows_block(half, depth)] * halves + out_specs
    block = pl.BlockSpec((1, half, depth), lambda g, w: (2 * w[1] + i, g, 0))
    vector = whole_block(gain)
    rows = rows_block(half, depth)
    carried = [] if final is None else [final]
    last = 13
    return launch(
        functools.partial(backward_kernel, carried=len(carried), resident=resident), "backward",
        where,
        (
            normed, gain, shift, out_grad, second_gain, second_shift, pull, *ups, *downs, part,
            part_far, *carried,
        ),
        [
            rows,
            vector,
            vector,
            block,
            vector,
            vector,
            rows_block(half, hidden),
            *[RESIDENT if resident else ANY] * 4,
            rows,
            rows,
            *[ANY] * len(carried),
        ],
        [shape((count, length, depth), BF16), *outs], [block, *out_specs], (2,), 34, after,
        streamed=(3, *(() if resident else (0, *range(6, 11))), *[last] * len(carried)),
        stored=(0, 1 + halves, 2 + halves, *(() if resident else (3 + halves,))),
        scratch=() if resident else fetched(ups[0]), aliases={last + 1: 0} if carried else {},
    )


def products_kernel(where_ref, *refs, count, steps, apart):
    def take(number):
        nonlocal refs
        taken, refs = refs[:number], refs[number:]
        return taken

    lows, slopes = take(steps * count), take(steps * count)
    befores, actives = take(count), take(count)
    kept_ref, *sent_refs = refs
    width = kept_ref.shape[3]
    for place, (lefts, rights) in enumerate(((lows, befores), (slopes, actives))):
        for group in range(2):
            columns = slice(group * width, (group + 1) * width)
            total = None
            for n in range(count):
                left = [ref[...] for ref in lefts[steps * n : steps * (n + 1)]]
                left = jnp.concatenate(left, axis=1) if steps > 1 else left[0]
                part = dot(left, rights[n][:, columns], 0, 0)
                total = part if total is None else total + part
            for step in range(steps):
                value = total[step * BLOCK : (step + 1) * BLOCK, :]
                if group == 0:
                    kept_ref[step, place] = value
                elif step == 0 and apart:
                    sent_refs[place][...] = value
                else:
                    sent_refs[step + int(apart)][place] = value


def products(steps, apart, where, lows, slopes, befores, actives, after):
    length, depth = lows[0].shape
    width = befores[0].shape[1] // 2
    count = len(lows)
    tiles, values = [], []
    for way, arrays in enumerate((lows, slopes)):
        for array in arrays:
            for step in steps:
                place = 4 + 2 * step + way
                values.append(array)
                tiles.append(
                    pl.BlockSpec((length, BLOCK), lambda i, w, place=place: (0, w[place]))
                )
    outs = [shape((len(steps), 2, BLOCK, width), F32)]
    outs += [shape((BLOCK, width), F32)] * (2 * int(apart))
    outs += [shape((2, BLOCK, width), F32)] * (len(steps) - int(apart))
    return launch(
        functools.partial(products_kernel, count=count, steps=len(steps), apart=apart), "products",
        where, (*values, *befores, *actives), tiles + [RESIDENT] * (2 * count), outs,
        [whole_block(o) for o in outs], (1,), 24, after, streamed=range(2 * len(steps) * count),
    )


def first_kernel(
    where_ref, part_ref, part_far_ref, slope_ref, normed_ref, scaled_ref, gain_ref,
    wo_ref, one_ref, low_ref, mixed_ref, sums_ref,
):
    step = pl.program_id(0)
    upstream = slope_ref[...] + (part_ref[...] + part_far_ref[...])
    normed = normed_ref[...]

    @pl.when(step == 0)
    def _():
        sums_ref[...] = jnp.zeros_like(sums_ref)

    sums_ref[0:1, :] += jnp.sum(upstream * normed, axis=0, keepdims=True)
    sums_ref[1:2, :] += jnp.sum(upstream, axis=0, keepdims=True)
    slope = norm_back(upstream, normed, scaled_ref[:, 0:1], gain_ref[...])
    one_ref[...] = slope
    low = slope.astype(BF16)
    low_ref[...] = low
    width = mixed_ref.shape[1]
    weights = wo_ref[pl.ds(pl.multiple_of(where_ref[2] * width, width), width), :]
    mixed_ref[...] = dot(low, weights, 1, 1).astype(BF16)


def first(where, part, part_far, slope, normed, scaled, gain, wo, after):
    length, depth = slope.shape
    both = wo.shape[0] // 2
    half = length // 2
    outs = [
        shape((length, depth), F32),
        shape((length, depth), BF16),
        shape((length, both), BF16),
        shape((8, depth), F32),
    ]
    out_specs = [rows_block(half, o.shape[1]) for o in outs]
    out_specs[3] = whole_block(outs[3])
    rows = rows_block(half, depth)
    return launch(
        first_kernel, "first", where, (part, part_far, slope, normed, scaled, gain, wo),
        [rows, rows, rows, rows, rows_block(half, 128), whole_block(gain), RESIDENT],
        outs, out_specs, (2,), 18, after, streamed=(2, 3, 4), stored=(0, 1),
    )


def attend_back_kernel(
    where_ref, qkv_ref, go_ref, sums_ref, seg_ref, weights_ref, out_ref, grads_ref,
    key_slope, value_slope,
):
    width = weights_ref.shape[2] // 3
    owner, _ = lanes(width)
    zero = jnp.zeros((), BF16)
    spares = [spare_columns(seg_ref[0], sums_ref[...], group, width) for group in range(2)]

    def part_of(group, n):
        start = (3 * group + n) * width
        return qkv_ref[0, :, start : start + width]

    def products_of(group, head):
        spare_q, spare_k = spares[group]
        mine = owner == head
        score = dot(
            pick(head, owner, part_of(group, 0), spare_q, zero),
            jnp.where(mine, part_of(group, 1), spare_k), 1, 1,
        )
        upstream = go_ref[:, group * width : (group + 1) * width]
        return score, dot(jnp.where(mine, upstream, zero), part_of(group, 2), 1, 1)

    ahead = products_of(0, 0)
    for group in range(2):
        keys = part_of(group, 1)
        queries_t = part_of(group, 0).T
        upstream_t = go_ref[:, group * width : (group + 1) * width].T
        query_slope = jnp.zeros(keys.shape, F32)
        for head in range(GROUP):
            row = group * GROUP + head
            score, drift = ahead
            if row + 1 < 2 * GROUP:
                ahead = products_of((row + 1) // GROUP, (row + 1) % GROUP)
            place = slice(head * HEAD_DIM, (head + 1) * HEAD_DIM)
            chances = jnp.exp(score)
            slopes = chances * (drift - jnp.sum(drift * chances, axis=-1, keepdims=True))
            slopes = slopes.astype(BF16)
            query_slope = query_slope + dot(slopes, jnp.where(owner == head, keys, zero))
            key_slope[place, :] = dot(queries_t[place, :], slopes)
            value_slope[place, :] = dot(upstream_t[place, :], chances.astype(BF16))
        start = 3 * group * width
        grads_ref[:, start : start + width] = (query_slope * SCALE).astype(BF16)
        grads_ref[:, start + width : start + 2 * width] = key_slope[...].T.astype(BF16)
        grads_ref[:, start + 2 * width : start + 3 * width] = value_slope[...].T.astype(BF16)
        part = dot(grads_ref[:, start : start + 3 * width], weights_ref[group], 1, 1)
        if group == 0:
            out_ref[...] = part
        else:
            out_ref[...] += part


def attend_back(i, where, qkv, go, mixed, seg, weights, after):
    _, length, columns = qkv.shape
    _, depth, width = weights.shape
    outs = [shape((length, depth), F32), shape((length, columns), BF16)]
    return launch(
        attend_back_kernel, "attend_back", where, (qkv, go, mixed, seg, weights),
        [
            whole_block(qkv),
            whole_block(go),
            pl.BlockSpec((8, columns // 3), lambda g, w: (length // 8, 0)),
            sequence(i, (8, length)),
            RESIDENT,
        ],
        outs, [whole_block(o) for o in outs], (1,), 22, after,
        scratch=[pltpu.VMEM((width // 3, length), F32)] * 2, streamed=(0,), stored=(1,),
    )


def total_kernel(where_ref, one_ref, part_ref, far_ref, *rest):
    final_ref, out_ref = rest[-2:]
    size = out_ref.shape[0]
    start = pl.multiple_of(pl.program_id(0) * size, size)

    def block(ref):
        return ref[...] if ref.shape == out_ref.shape else ref[pl.ds(start, size), :]

    final = (block(one_ref) + (block(part_ref) + block(far_ref))).astype(BF16)
    final_ref[0] = final
    out_ref[...] = final.astype(F32)


def total(i, count, where, one, part, far, final, after):
    length, depth = one.shape
    carried = [] if final is None else [final]
    steps = 2 if carried else 4
    size = length // steps
    rows = rows_block(size, depth)
    return launch(
        total_kernel, "total", where, (one, part, far, *carried),
        [RESIDENT if carried else rows] * 3 + [ANY] * len(carried),
        [shape((count, length, depth), BF16), shape((length, depth), F32)],
        [pl.BlockSpec((1, size, depth), lambda g, w: (2 * w[1] + i, g, 0)), rows],
        (steps,), 12, after, streamed=(3,) if carried else (0,), stored=(0,),
        aliases={4: 0} if carried else {},
    )


def head_products_kernel(where_ref, *refs, count):
    def take(number):
        nonlocal refs
        taken, refs = refs[:number], refs[number:]
        return taken

    def summed(lefts, rights):
        total = None
        for n in range(count):
            left = jnp.concatenate([lefts[2 * n], lefts[2 * n + 1]], axis=1)
            part = dot(left, rights[n], 0, 0)
            total = part if total is None else total + part
        return total

    firsts, seconds, ones = take(2 * count), take(2 * count), take(2 * count)
    grads, mixed, first_sums, second_sums = take(count), take(count), take(2 * count), take(2 * count)
    width = mixed[0].shape[2] // 2
    x_first, x_second = ([ref[0] for ref in group] for group in (firsts, seconds))
    kept_ref, *sent_refs = refs
    for group in range(2):
        start = 3 * group * width
        pairs = [ref[:, start : start + 2 * width] for ref in grads]
        heads = summed(x_first, pairs)
        values = summed(x_second, [ref[:, start + 2 * width : start + 3 * width] for ref in grads])
        outputs = summed(
            [ref[...] for ref in ones], [ref[0, :, group * width : (group + 1) * width] for ref in mixed]
        )
        for step in range(2):
            rows = slice(step * BLOCK, (step + 1) * BLOCK)
            out = sent_refs[step] if group else kept_ref.at[step]
            out[0:BLOCK, :] = heads[rows, 0:width]
            out[BLOCK : 2 * BLOCK, :] = heads[rows, width:]
            out[2 * BLOCK : 3 * BLOCK, :] = values[rows, :]
            out[3 * BLOCK : 4 * BLOCK, :] = outputs[rows, :]
            out[4 * BLOCK :, :] = jnp.zeros((8, width), F32)
            for row, sums in ((0, first_sums), (2, second_sums)):
                gains = sums[step][0:2, :]
                for n in range(1, count):
                    gains = gains + sums[2 * n + step][0:2, :]
                last = 4 * BLOCK + row
                out[last : last + 2, 0:BLOCK] = gains


def head_products(pair, where, x, ones, grads, mixed, firsts, seconds, after):
    _, length, depth = x.shape
    count = len(ones)
    width = mixed[0].shape[2] // 2

    def tile(way, step, dims, lead=()):
        return pl.BlockSpec(
            (*dims, BLOCK),
            lambda j, w: (*[f(w) for f in lead], 0, w[4 + 2 * (2 * pair + step) + way]),
        )

    def inputs_of(way):
        return [
            tile(way, step, (1, length), (lambda w, i=i: 2 * w[1] + i,))
            for i in range(count) for step in range(2)
        ]

    out = shape((4 * BLOCK + 8, width), F32)
    outs = [shape((2, *out.shape), F32), out, out]
    twice = lambda arrays: [a for a in arrays for _ in range(2)]
    return launch(
        functools.partial(head_products_kernel, count=count), "head_products", where,
        (
            *[x] * (4 * count), *twice(ones), *grads, *mixed, *twice(firsts), *twice(seconds)
        ),
        inputs_of(0) + inputs_of(1) + [tile(1, step, (length,)) for _ in ones for step in range(2)]
        + [RESIDENT] * (2 * count)
        + [tile(1, step, (8,)) for _ in range(2 * count) for step in range(2)],
        outs, [whole_block(o) for o in outs], (1,), 12, after, streamed=range(6 * count),
    )


def ring_kernel(where_ref, *refs, arrivals, sizes):
    outs = refs[-2:]
    sources = refs[arrivals : -2]
    for way in range(2):
        mine, start = [], 0
        count = sizes[way]
        kept = sources[way * sizes[0] : way * sizes[0] + count]
        base = sizes[0] + sizes[1]
        near = sources[base + way * sizes[0] : base + way * sizes[0] + count]
        for left, right in zip(kept, near):
            value = left[...].reshape(left.shape[-2:]) + right[...].reshape(right.shape[-2:])
            rows = slice(start, start + value.shape[0])
            if arrivals:
                value = refs[way][rows, :] + value
            outs[way][rows, :] = value
            start += value.shape[0]


def ring_step(where, arrived, kept, near, after, stored=()):
    entries = [*kept[0], *kept[1], *near[0], *near[1]]
    specs = [whole_block(a) for a in arrived]
    specs += [pl.BlockSpec(dims, lambda i, w, at=at: at) for _, dims, at in entries]
    outs = [
        shape((sum(e[1][-2] for e in way), way[0][1][-1]), F32) for way in kept
    ]
    return launch(
        functools.partial(ring_kernel, arrivals=len(arrived), sizes=(len(kept[0]), len(kept[1]))),
        "ring_step", where, (*arrived, *[e[0] for e in entries]), specs, outs,
        [whole_block(o) for o in outs], (1,), 8, after, stored=stored,
    )


def last_kernel(where_ref, left_ref, right_ref, *refs):
    kept, near, outs = refs[0:3], refs[3:6], refs[6:]
    top, middle, low = (
        k[...].reshape(k.shape[-2:]) + n[...].reshape(n.shape[-2:]) for k, n in zip(kept, near)
    )
    left = left_ref[...] + top
    right = right_ref[0 : 2 * BLOCK, :] + middle
    low = right_ref[2 * BLOCK :, :] + low
    outs[0][...] = left[0:BLOCK, :]
    outs[1][...] = left[BLOCK:, :]
    outs[2][...] = right[0:BLOCK, :]
    outs[3][...] = right[BLOCK:, :].T
    for row, out in enumerate(outs[4:]):
        out[...] = low[row : row + 1, 0:BLOCK]


def last_step(where, arrived, kept, near, after):
    entries = [*kept[0], *kept[1], *near[0], *near[1]]
    specs = [whole_block(a) for a in arrived]
    specs += [pl.BlockSpec(dims, lambda i, w, at=at: at) for _, dims, at in entries]
    width = arrived[0].shape[1]
    outs = [shape((BLOCK, width), F32)] * 3 + [shape((width, BLOCK), F32)]
    outs += [shape((1, BLOCK), F32)] * 4
    return launch(
        last_kernel, "last_step", where, (*arrived, *[e[0] for e in entries]), specs, outs,
        [whole_block(o) for o in outs], (1,), 8, after, stored=range(8),
    )


def turn_kernel(where_ref, value_ref, out_ref):
    out_ref[...] = value_ref[...].T


def turn(where, value, after):
    out = shape(value.shape[::-1], F32)
    return launch(
        turn_kernel, "turn", where, (value,), [whole_block(value)], [out], [whole_block(out)],
        (1,), 6, after, stored=(0,),
    )[0]


def hold_kernel(where_ref, *refs):
    *pairs, arrived = refs
    count = len(pairs) // 2
    copies = [
        pltpu.make_async_copy(pairs[n], pairs[count + n], arrived.at[n]) for n in range(count)
    ]
    for copy in copies:
        copy.start()
    for copy in copies:
        copy.wait()


def hold(where, *values, after):
    count = len(values)
    token = shape((8, 128), F32)

    def run(where_ref, *refs):
        refs[2 * count][...] = jnp.zeros((8, 128), F32)
        hold_kernel(where_ref, *refs[: 2 * count], refs[-1])

    return launch(
        run, "hold", where, values, [ANY] * count,
        [*[pltpu.VMEM(v.shape, v.dtype) for v in values], token],
        [*[RESIDENT] * count, whole_block(token)], (1,), 4, after, streamed=range(count),
        scratch=[pltpu.SemaphoreType.DMA((count,))],
    )[:count]


def clip_kernel(where_ref, query_ref, key_ref, factor_ref, query_out, key_out):
    query_out[...] = query_ref[...].astype(F32) * factor_ref[...]
    key_out[...] = key_ref[...].astype(F32) * factor_ref[...]


def clip(where, query, key, factor, after):
    specs = [rows_block(query.shape[0] // 4, query.shape[1])] * 2
    return launch(
        clip_kernel, "clip", where, (query, key, factor), [*specs, whole_block(factor)],
        [shape(query.shape, F32)] * 2, specs, (4,), 8, after, streamed=(0, 1), stored=(0, 1),
    )


def finish_kernel(where_ref, *refs):
    *halves, final_ref, out_ref, token_ref = refs
    del final_ref
    value = halves[0][...].reshape(out_ref.shape[1:])
    if len(halves) == 2:
        value = jnp.where(pl.program_id(0) == 0, value, halves[1][...])
    out_ref[0] = value.astype(BF16)
    token_ref[...] = jnp.zeros_like(token_ref)


def finish(i, where, values, final, after):
    half, depth = final.shape[1] // 2, final.shape[2]
    specs = [rows_block(half, depth)]
    if len(values) == 2:
        specs = [whole_block(v) for v in values]
    last = len(values)
    token = shape((8, 128), F32)
    return launch(
        finish_kernel, "finish", where, (*values, final), [*specs, ANY],
        [shape(final.shape, BF16), token],
        [
            pl.BlockSpec((1, half, depth), lambda g, w: (2 * (1 - w[1]) + i, g, 0)),
            whole_block(token),
        ],
        (2,), 10, after, aliases={last + 1: 0}, stored=(0,), streamed=(last,),
    )[0]


def solution(mesh):
    ranks = mesh.shape["dp"]
    group = mesh.shape["tensor"]
    assert group == 4 and ranks % 8 == 0
    near_pairs = [(t, t ^ 1) for t in range(group)]
    far_pairs = [(t, t ^ 2) for t in range(group)]
    turns = (
        [(RING[p], RING[(p + 1) % 8]) for p in range(8)],
        [(RING[p], RING[(p - 1) % 8]) for p in range(8)],
    )

    def near(value):
        return lax.ppermute(value, "tensor", near_pairs)

    def scatter(value):
        return lax.psum_scatter(value, "dp", scatter_dimension=0, tiled=True)

    def far(value):
        return lax.ppermute(value, "tensor", far_pairs)

    def body(
        block_input, segment_ids, query_weight, key_weight, value_weight, output_weight,
        first_gain, first_shift, up_weight, down_weight, second_gain, second_shift, out_grad,
    ):
        count, length, depth = block_input.shape
        width = query_weight.shape[1]
        part = depth // ranks
        mine = range(count // 2)
        me = lax.axis_index("tensor")
        rank = lax.axis_index("dp")
        natural = [n for n in range(8) for _ in range(2)]
        owners = jnp.asarray(OWNERS if ranks == 8 else [natural], jnp.int32)
        owners = lax.dynamic_index_in_dim(owners, rank if ranks == 8 else 0, 0, False)
        where = jnp.concatenate(
            [jnp.stack([me, me % 2, me // 2, rank]).astype(jnp.int32), owners]
        )
        seg = jnp.broadcast_to(segment_ids[:, None, :], (count, 8, length))
        gain_one, shift_one = first_gain[None], first_shift[None]
        gain_two, shift_two = second_gain[None], second_shift[None]
        order = Order()

        def then(call, *args, **kwargs):
            return call(*args, after=order, **kwargs)

        own_low, own_wide, wo_half = then(
            widen_heads, where, query_weight, key_weight, value_weight, output_weight
        )
        near_wide, wo_first = near(own_wide), far(wo_half)
        wide = convert(where, up_weight, down_weight, dtype=F32, after=Order())
        wide_near = [near(w) for w in wide]
        weights, wo_near = then(narrow_near, where, own_low, near_wide, output_weight)
        heads, mixed_far = [], []
        for i in mine:
            heads.append(then(attend, i, where, block_input, weights, seg))
            mixed_far.append(far(heads[i][3]))
            if i == 0:
                (wo_first,) = then(gate, where, wo_first)
                wo_second = lax.ppermute(wo_first, "dp", [(r, r ^ 1) for r in range(ranks)])
                wo_both = [near(wo_first)]
        mixed_low, qkv, tops, mixed = zip(*heads)
        up_near, down_near = then(convert, where, *wide_near, dtype=BF16)
        ups, downs = (up_weight, up_near), (down_weight, down_near)
        (wo_second,) = then(gate, where, wo_second)
        wo_both.append(near(wo_second))
        wo = then(assemble, where, output_weight, wo_near, (wo_first, wo_second), wo_both)

        forwards, part_far = [], []
        for i in mine:
            forwards.append(
                then(
                    forward, i, where, block_input, mixed[i], mixed_far[i], wo, gain_one,
                    shift_one, ups, downs,
                )
            )
            part_far.append(far(forwards[i][5]))

        heads_own = width // HEAD_DIM
        peak = functools.reduce(jnp.maximum, tops)
        peak = jnp.maximum(peak[:heads_own], near(peak)[heads_own:])
        step = 1
        while step < ranks:
            peak = jnp.maximum(peak, lax.ppermute(peak, "dp", [(i, i ^ step) for i in range(ranks)]))
            step *= 2
        factor = jnp.sqrt(CLIP / jnp.maximum(peak[:, 0], CLIP))
        factor = jnp.repeat(factor, HEAD_DIM)[None]
        query_clipped, key_clipped = then(clip, where, query_weight, key_weight, factor)

        written = {"layer_out": None, "input_grad": None}
        def finish_layer(i, values):
            written["layer_out"] = then(finish, i, where, values, written["layer_out"])

        backs, slope_parts, slope_far = [], [], []
        for i in mine:
            normed, scaled, low, active, pull, part_sum = forwards[i]
            weights_of = ups, downs
            if i > 0:
                normed, pull, *held = then(hold, where, normed, pull, *ups, *downs)
                weights_of = held[0:2], held[2:4]
            backs.append(
                then(
                    backward, i, where, normed, gain_one, shift_one, part_sum, part_far[i],
                    out_grad, gain_two, shift_two, pull, *weights_of, written["layer_out"],
                    resident=i > 0,
                )
            )
            written["layer_out"], *out, slope, slope_low, before, sums, part_sum = backs[i]
            backs[i] = (out, slope, slope_low, before, sums)
            slope_parts.append(part_sum)
            slope_far.append(far(part_sum))
            if i == 0:
                finish_layer(0, [near(v) for v in out])

        lows, actives = [f[2] for f in forwards], [f[3] for f in forwards]
        slope_lows, befores = [b[2] for b in backs], [b[3] for b in backs]
        def send(held):
            return [lax.ppermute(h, "dp", t) for h, t in zip(held, turns)]

        ff_blocks = {}

        def ff_part(*steps, apart=True):
            kept, *sent = then(products, steps, apart, where, lows, slope_lows, befores, actives)
            sent = [near(a) for a in sent]
            for index, n in enumerate(steps):
                mine = sent[:2] if index == 0 and apart else sent[index + int(apart)]
                ff_blocks[n] = (kept, index, mine)

        def ff_step(n, arrived):
            kept, index, sent = ff_blocks[n]
            dims = (1, 1, BLOCK, kept.shape[3])
            if isinstance(sent, list):
                near = [[(array, dims[2:], (0, 0))] for array in sent]
            else:
                near = [[(sent, dims[1:], (way, 0, 0))] for way in range(2)]
            return then(
                ring_step, where, arrived,
                [[(kept, dims, (index, way, 0, 0))] for way in range(2)], near,
                stored=range(2) if n == 7 else (),
            )

        def ff_ring():
            held = ff_step(0, ())
            for n in range(1, 8):
                arrived = send(held)
                yield None
                held = ff_step(n, arrived)
            yield held

        head_parts = []

        def head_part(pair):
            kept, *sent = then(
                head_products, pair, where, block_input, [f[1] for f in firsts],
                [o[1] for o in owns], mixed_low, [f[3] for f in firsts], [b[4] for b in backs],
            )
            head_parts.append((kept, [near(a) for a in sent]))

        def head_step(n, arrived):
            kept, sent = head_parts[n // 2]

            def entries(array, lead):
                block = lambda rows, at: (
                    array, (*[1 for _ in lead], rows, width), (*lead, at, 0)
                )
                return [[block(2 * BLOCK, 0)], [block(2 * BLOCK, 1), block(8, 4 * BLOCK // 8)]]

            call = last_step if n == 7 else ring_step
            return then(call, where, arrived, entries(kept, (n % 2,)), entries(sent[n % 2], ()))

        def head_ring():
            held = head_step(0, ())
            for n in range(1, 8):
                arrived = send(held)
                yield None
                held = head_step(n, arrived)
            yield held

        def total_input(i):
            one, own = (firsts[i][0], owns[i][0]) if i == 0 else summands
            written["input_grad"], result = then(
                total, i, count, where, one, own, input_far[i], written["input_grad"]
            )
            return result

        def finish_input(i, value):
            written["input_grad"] = then(finish, i, where, [value], written["input_grad"])

        def first_back(i):
            firsts.append(
                then(
                    first, where, slope_parts[i], slope_far[i], backs[i][1], *forwards[i][:2],
                    gain_one, wo,
                )
            )

        def own_back(i):
            owns.append(then(attend_back, i, where, qkv[i], firsts[i][2], mixed[i], seg, weights))

        firsts, owns, input_far = [], [], []
        ring = ff_ring() if ranks == 8 else iter(())
        ff_part(0)
        ff_part(1, 2)
        next(ring, None)
        next(ring, None)
        ff_part(3, 4)
        first_back(0)
        next(ring, None)
        own_back(0)
        next(ring, None)
        ff_part(5, 6, 7)
        next(ring, None)
        slope_far[1], own_part = then(gate, where, slope_far[1], owns[0][0])
        owns[0] = (own_part, owns[0][1])
        input_far.append(far(own_part))
        first_back(1)
        next(ring, None)
        own_back(1)
        next(ring, None)
        head_part(0)
        head_part(1)
        head_part(2)
        if ranks == 8:
            *_, (up_grad, down_grad) = ring
        (own_part,) = then(gate, where, owns[1][0])
        owns[1] = (own_part, owns[1][1])
        input_far.append(far(own_part))
        ring = head_ring() if ranks == 8 else iter(())
        next(ring, None)
        head_part(3)
        next(ring, None)
        next(ring, None)
        rows = total_input(0)
        next(ring, None)
        (rows,) = then(gate, where, rows)
        rows = near(rows)
        summands = then(hold, where, firsts[1][0], owns[1][0])
        next(ring, None)
        if ranks == 8:
            down_grad = then(turn, where, down_grad)
        next(ring, None)
        result = total_input(1)
        next(ring, None)
        result, layer = then(gate, where, result, *backs[1][0])
        result, layer = near(result), near(layer)
        finish_input(0, rows)
        finish_input(1, result)
        finish_layer(1, [layer])

        if ranks == 8:
            *_, (query_grad, key_grad, value_grad, output_grad, *gains) = ring
            gains = [g.reshape(BLOCK) for g in gains]
        else:
            def rows_of(value, start, rows=BLOCK):
                return scatter(value[:, start : start + rows].reshape(8 * rows, width))

            up, down = [
                jnp.concatenate(
                    [kept[at, way] + sent[way] for kept, at, sent in map(ff_blocks.get, range(8))],
                    axis=0,
                )
                for way in range(2)
            ]
            up_grad, down_grad = scatter(up), scatter(down).T
            value = jnp.concatenate([k + jnp.stack(s) for k, s in head_parts], axis=0)
            query_grad, key_grad, value_grad = (rows_of(value, n * BLOCK) for n in range(3))
            output_grad = rows_of(value, 3 * BLOCK).T
            gains = value[:, 4 * BLOCK : 4 * BLOCK + 4, :BLOCK].transpose(0, 2, 1)
            gains = scatter(gains.reshape(depth, 4)).T

        return (
            written["layer_out"], written["input_grad"], query_grad, key_grad, value_grad, output_grad,
            gains[0], gains[1], up_grad, down_grad, gains[2], gains[3],
            query_clipped, key_clipped,
        )

    batch = P("dp", None, None)
    in_specs = (
        batch, P("dp", None), P(None, "tensor"), P(None, "tensor"), P(None, "tensor"),
        P("tensor", None), P(), P(), P(None, "tensor"), P("tensor", None), P(), P(), batch,
    )
    out_specs = (
        batch, batch, P("dp", "tensor"), P("dp", "tensor"), P("dp", "tensor"), P("tensor", "dp"),
        P("dp"), P("dp"), P("dp", "tensor"), P("tensor", "dp"), P("dp"), P("dp"),
        P(None, "tensor"), P(None, "tensor"),
    )
    return jax.shard_map(body, mesh=mesh, in_specs=in_specs, out_specs=out_specs, check_vma=False)
```
